32 devices in a mesh: dp: 8 (over z, y), rep: 4 (over x, core).
Axes of the slice: x: 2, y: 2, z: 4, core: 2. Of those that a mesh axis runs over, the one named last changes fastest.
Arguments:
- clip_input: bfloat16 [32, 4, 20, 20, 832], P(('dp', 'rep')), may hold values from -6 to 6
- cotangent: bfloat16 [32, 2, 10, 10, 832], P(('dp', 'rep')), may hold values from -6 to 6
- clip_group: int32 [32], P(('dp', 'rep')), may hold values from 0 to 2
- crop_sides: int32 [3], replicated, may hold values from 14 to 20, as said below
- w_single: bfloat16 [2, 832, 256], replicated, may hold values from -0.21875 to 0.21875
- w_reduce: bfloat16 [2, 832, 160], replicated, may hold values from -0.21875 to 0.21875
- w_spatial: bfloat16 [2, 3, 3, 3, 160, 320], replicated, may hold values from -0.09375 to 0.09375
- w_squeeze: bfloat16 [2, 832, 32], replicated, may hold values from -0.21875 to 0.21875
- w_narrow: bfloat16 [2, 3, 3, 3, 32, 128], replicated, may hold values from -0.21875 to 0.21875
- w_project: bfloat16 [2, 832, 128], replicated, may hold values from -0.21875 to 0.21875
- bn_scale: float32 [2, 1024], replicated, may hold values from 0.1 to 1.9
- bn_shift: float32 [2, 1024], replicated, may hold values from -3 to 3
Outputs:
- activations: bfloat16 [32, 2, 10, 10, 832], P(('dp', 'rep'))
- input_grad: bfloat16 [32, 4, 20, 20, 832], P(('dp', 'rep'))
- grad_single: float32 [2, 832, 256], replicated
- grad_reduce: float32 [2, 832, 160], replicated
- grad_spatial: float32 [2, 3, 3, 3, 160, 320], replicated
- grad_squeeze: float32 [2, 832, 32], replicated
- grad_narrow: float32 [2, 3, 3, 3, 32, 128], replicated
- grad_project: float32 [2, 832, 128], replicated
- grad_scale: float32 [2, 1024], replicated
- grad_shift: float32 [2, 1024], replicated
The draws below stay inside these ranges and needn't reach their ends.
Inputs may be any that keep to these rules, and one draw needn't show every extreme that they name: `crop_sides`: the three entries are 20, 16 and 14, in an order drawn from the seed.
All inputs are finite; a program needn't handle non-finite values.
Results may differ from the reference program's by a relative error of at most 0.015.
Values sent between devices are 32-bit elements; how exact they have to be, the bound alone decides.
No kernel may reach another device: no remote copies, remote signals or barrier semaphores. Data moves between devices by JAX's collectives and lax.ppermute only.
A program may use at most 320 MiB of HBM per device.

```python
import jax
import jax.numpy as jnp
from jax import lax

B1 = 256
B2R = 160
B2 = 320
B3R = 32
B3 = 128
B4 = 128
IN = 832
NORM = 1024
FRAMES = 4
SIDE = 20
LAYERS = 2
GROUPS = 3
CLIPS = 32


def draw_crop_sides(key, part):
    key = jax.random.fold_in(key, 7)
    table = jnp.array([SIDE, SIDE - 4, SIDE - 6], dtype=jnp.int32)
    return jax.random.permutation(key, table)


def plant(values, own_key, low, high):
    spot = [jax.random.randint(jax.random.fold_in(own_key, axis), (), 0, length) for axis, length in enumerate(values.shape)]
    widest = values.shape.index(max(values.shape))
    neighbour = spot[:widest] + [(spot[widest] + 1) % values.shape[widest]] + spot[widest + 1:]
    return values.at[tuple(spot)].set(low).at[tuple(neighbour)].set(high)


def shard_levels(key, dims, split, least, largest):
    def one(axis_at, shards_of):
        steps = jax.random.uniform(jax.random.fold_in(jax.random.fold_in(key, 6), axis_at), (shards_of,), jnp.float32, least / len(split), largest / len(split))
        return jnp.repeat(jnp.exp(steps), dims[axis_at] // shards_of).reshape((-1,) + (1,) * (len(dims) - axis_at - 1))

    factor_of = one(*split[0])
    for cut in split[1:]:
        factor_of = factor_of * one(*cut)
    return factor_of


def bell_draw(key, dims, scale, limit, pieces=(), kind=jnp.bfloat16):
    factor_of = shard_levels(key, dims, pieces, -0.22, 0.18) if pieces else 1.0
    values = jax.random.normal(key, dims, jnp.float32) * scale * factor_of
    return jnp.minimum(jnp.maximum(values, -limit), limit).astype(kind)


def setup_inputs(seed: int = 0) -> dict:
    key_list = jax.random.split(jax.random.key(seed), 13)
    clip_input = bell_draw(key_list[0], (CLIPS, FRAMES, SIDE, SIDE, IN), 1.0, 6.0, ((0, 32),))
    cotangent = bell_draw(key_list[1], (CLIPS, FRAMES // 2, SIDE // 2, SIDE // 2, IN), 1.0, 6.0, ((0, 32),))
    clip_group = plant(jax.random.randint(key_list[2], (CLIPS,), 0, GROUPS), jax.random.fold_in(key_list[2], 1), 0, GROUPS - 1).astype(jnp.int32)
    crop_sides = draw_crop_sides(jax.random.fold_in(key_list[12], 71), 0)
    w_single = bell_draw(key_list[4], (LAYERS, IN, B1), IN ** -0.5, 0.21875)
    w_reduce = bell_draw(key_list[5], (LAYERS, IN, B2R), IN ** -0.5, 0.21875)
    w_spatial = bell_draw(key_list[6], (LAYERS, 3, 3, 3, B2R, B2), (27 * B2R) ** -0.5, 0.09375)
    w_squeeze = bell_draw(key_list[7], (LAYERS, IN, B3R), IN ** -0.5, 0.21875)
    w_narrow = bell_draw(key_list[8], (LAYERS, 3, 3, 3, B3R, B3), (27 * B3R) ** -0.5, 0.21875)
    w_project = bell_draw(key_list[9], (LAYERS, IN, B4), IN ** -0.5, 0.21875)
    bn_scale = jnp.clip(1.0 + 0.18 * jax.random.normal(key_list[10], (LAYERS, NORM), jnp.float32), 0.1, 1.9)
    bn_shift = bell_draw(key_list[11], (LAYERS, NORM), 0.5, 3.0, (), jnp.float32)
    return {"clip_input": clip_input, "cotangent": cotangent, "clip_group": clip_group, "crop_sides": crop_sides, "w_single": w_single, "w_reduce": w_reduce, "w_spatial": w_spatial, "w_squeeze": w_squeeze, "w_narrow": w_narrow, "w_project": w_project, "bn_scale": bn_scale, "bn_shift": bn_shift}


@jax.custom_vjp
def low(v):
    return lax.optimization_barrier(v.astype(jnp.bfloat16)).astype(jnp.float32)

@jax.custom_vjp
def low_back(v):
    return v

def low_keep(v):
    return (low(v), None)

def low_pass(kept, grad):
    return (grad,)

def back_keep(v):
    return (v, None)

def back_low(kept, grad):
    return (low(grad),)
low.defvjp(low_keep, low_pass)
low_back.defvjp(back_keep, back_low)

def mask_for(sides, frames, side):
    place = jnp.arange(side, dtype=jnp.int32)
    inside = (place[None, :, None] < sides[:, None, None]) & (place[None, None, :] < sides[:, None, None])
    return jnp.broadcast_to(inside[:, None, :, :, None], (sides.shape[0], frames, side, side, 1)).astype(jnp.float32)

def crop_masks(clip_group, crop_sides, frames, side):
    choose = (clip_group[:, None] == jnp.arange(3, dtype=jnp.int32)[None, :]).astype(jnp.int32)
    sides = lax.optimization_barrier(jnp.sum(choose * crop_sides[None, :].astype(jnp.int32), axis=1)).astype(jnp.int32)
    return (mask_for(sides, frames, side), mask_for(sides // 2, frames // 2, side // 2))

def neighbour_mean(value):
    for axis in (1, 2, 3):
        pads = [(0, 0)] * 5
        pads[axis] = (1, 1)
        padded = jnp.pad(value, pads)
        length = value.shape[axis]
        value = lax.slice_in_dim(padded, 0, length, axis=axis) + lax.slice_in_dim(padded, 1, length + 1, axis=axis) + lax.slice_in_dim(padded, 2, length + 2, axis=axis)
    return value / 27.0

def pool_pairs(value):
    n, t, h, w, c = value.shape
    return lax.optimization_barrier(jnp.mean(value.reshape(n, t // 2, 2, h // 2, 2, w // 2, 2, c), axis=(2, 4, 6)))

def convolve(value, kernel):
    if kernel.ndim == 2:
        return jnp.einsum('nthwc,cd->nthwd', value, kernel, precision=lax.Precision.HIGHEST)
    return lax.conv_general_dilated(value, kernel, (1, 1, 1), [(1, 1), (1, 1), (1, 1)], dimension_numbers=('NDHWC', 'DHWIO', 'NDHWC'), precision=lax.Precision.HIGHEST)

def unit(value, kernel, gamma, beta, mask, count):
    pre = low_back(convolve(value, kernel))
    mean = lax.optimization_barrier(jnp.sum(pre * mask, axis=(0, 1, 2, 3))) / count
    square = lax.optimization_barrier(jnp.sum(pre * pre * mask, axis=(0, 1, 2, 3))) / count
    inverse = lax.rsqrt(square - mean * mean + 1e-05)
    shifted = gamma * ((pre - mean) * inverse) + beta
    return jax.nn.silu(shifted) * mask

def block(value, kernels, gains, offsets, mask, count):
    w_single, w_reduce, w_spatial, w_squeeze, w_narrow, w_project = kernels
    widths = [w_single.shape[1], w_reduce.shape[1], w_spatial.shape[-1], w_squeeze.shape[1], w_narrow.shape[-1], w_project.shape[1]]
    starts = [sum(widths[:index]) for index in range(6)]
    gamma = [gains[start:start + width] for start, width in zip(starts, widths)]
    beta = [offsets[start:start + width] for start, width in zip(starts, widths)]
    single = unit(value, w_single, gamma[0], beta[0], mask, count)
    reduce_out = low(unit(value, w_reduce, gamma[1], beta[1], mask, count))
    spatial = unit(reduce_out, w_spatial, gamma[2], beta[2], mask, count)
    squeeze_out = low(unit(value, w_squeeze, gamma[3], beta[3], mask, count))
    narrow = unit(squeeze_out, w_narrow, gamma[4], beta[4], mask, count)
    pooled = low(neighbour_mean(value))
    project = unit(pooled, w_project, gamma[5], beta[5], mask, count)
    return jnp.concatenate([single, spatial, narrow, project], axis=-1)

def reference(clip_input, cotangent, clip_group, crop_sides, w_single, w_reduce, w_spatial, w_squeeze, w_narrow, w_project, bn_scale, bn_shift):
    mask, small_mask = crop_masks(clip_group, crop_sides, clip_input.shape[1], clip_input.shape[2])
    count = jnp.sum(mask)
    small_count = jnp.sum(small_mask)

    def forward(source, k_single, k_reduce, k_spatial, k_squeeze, k_narrow, k_project, gains, offsets):
        first = block(source * mask, (k_single[0], k_reduce[0], k_spatial[0], k_squeeze[0], k_narrow[0], k_project[0]), gains[0], offsets[0], mask, count)
        middle = low(pool_pairs(first))
        return block(middle, (k_single[1], k_reduce[1], k_spatial[1], k_squeeze[1], k_narrow[1], k_project[1]), gains[1], offsets[1], small_mask, small_count)
    floats = [item.astype(jnp.float32) for item in (clip_input, w_single, w_reduce, w_spatial, w_squeeze, w_narrow, w_project, bn_scale, bn_shift)]
    result, pull = jax.vjp(forward, *floats)
    grads = pull(cotangent.astype(jnp.float32))
    return (result.astype(jnp.bfloat16), grads[0].astype(jnp.bfloat16), grads[1], grads[2], grads[3], grads[4], grads[5], grads[6], grads[7], grads[8])
```

```python
import jax
import jax.numpy as jnp
from jax import lax
from jax.sharding import PartitionSpec as P


def mask_for(sides, frames, side):
    place = jnp.arange(side, dtype=jnp.int32)
    inside = (place[None, :, None] < sides[:, None, None]) & (
        place[None, None, :] < sides[:, None, None]
    )
    return jnp.broadcast_to(
        inside[:, None, :, :, None], (sides.shape[0], frames, side, side, 1)
    ).astype(jnp.float32)


def crop_masks(clip_group, crop_sides, frames, side):
    choose = (clip_group[:, None] == jnp.arange(3, dtype=jnp.int32)[None, :]).astype(jnp.int32)
    sides = jnp.sum(choose * crop_sides[None, :], axis=1)
    return (mask_for(sides, frames, side), mask_for(sides // 2, frames // 2, side // 2))


def neighbour_mean(value):
    for axis in (1, 2, 3):
        pads = [(0, 0)] * 5
        pads[axis] = (1, 1)
        padded = jnp.pad(value, pads)
        length = value.shape[axis]
        value = (
            lax.slice_in_dim(padded, 0, length, axis=axis)
            + lax.slice_in_dim(padded, 1, length + 1, axis=axis)
            + lax.slice_in_dim(padded, 2, length + 2, axis=axis)
        )
    return value / 27.0


def pool_pairs(value):
    n, t, h, w, c = value.shape
    return jnp.mean(value.reshape(n, t // 2, 2, h // 2, 2, w // 2, 2, c), axis=(2, 4, 6))


def spread_pairs(grad):
    n, t, h, w, c = grad.shape
    wide = jnp.broadcast_to(grad[:, :, None, :, None, :, None, :], (n, t, 2, h, 2, w, 2, c))
    return wide.reshape(n, 2 * t, 2 * h, 2 * w, c) / 8.0


def point_forward(value, kernel):
    return jnp.einsum("nthwc,cd->nthwd", value, kernel, preferred_element_type=jnp.float32)


def point_backward(value, kernel, grad_low):
    kernel_grad = jnp.einsum("nthwc,nthwd->cd", value, grad_low, preferred_element_type=jnp.float32)
    value_grad = jnp.einsum("nthwd,cd->nthwc", grad_low, kernel, preferred_element_type=jnp.float32)
    return (kernel_grad, value_grad)


CONV_FORM = ("NDHWC", "DHWIO", "NDHWC")
CONV_PADS = [(1, 1), (1, 1), (1, 1)]


def spatial_forward(value, kernel):
    return lax.conv_general_dilated(
        value,
        kernel,
        (1, 1, 1),
        CONV_PADS,
        dimension_numbers=CONV_FORM,
        preferred_element_type=jnp.float32,
    )


def spatial_backward(value, kernel, grad_low):
    turned = jnp.swapaxes(jnp.flip(kernel, (0, 1, 2)), 3, 4)
    value_grad = spatial_forward(grad_low, turned)
    kernel_grad = lax.conv_general_dilated(
        value,
        grad_low,
        (1, 1, 1),
        CONV_PADS,
        dimension_numbers=("CDHWN", "IDHWO", "DHWNC"),
        preferred_element_type=jnp.float32,
    )
    return (kernel_grad, value_grad)


def local_stats(pre, mask):
    return jnp.stack(
        [jnp.sum(pre * mask, axis=(0, 1, 2, 3)), jnp.sum(pre * pre * mask, axis=(0, 1, 2, 3))]
    )


def sync_stats(parts):
    return [lax.psum(item, ("dp", "rep")) for item in parts]


def normalize(pre, sums, count, gamma, beta, mask):
    mean = sums[0] / count
    square = sums[1] / count
    inverse = lax.rsqrt(square - mean * mean + 1e-05)
    normed = (pre - mean) * inverse
    shifted = gamma * normed + beta
    return (jax.nn.silu(shifted) * mask, (normed, shifted, inverse))


def unit_terms(grad_out, kept, mask):
    normed, shifted, inverse = kept
    gate_value = jax.nn.sigmoid(shifted)
    grad_shift = grad_out * mask * (gate_value * (1.0 + shifted * (1.0 - gate_value)))
    sums = jnp.stack(
        [jnp.sum(grad_shift, axis=(0, 1, 2, 3)), jnp.sum(grad_shift * normed, axis=(0, 1, 2, 3))]
    )
    return (grad_shift, sums)


def unit_grad(grad_shift, kept, gamma, sums, count, mask):
    normed, shifted, inverse = kept
    full = gamma * inverse * (grad_shift - sums[0] / count - normed * (sums[1] / count)) * mask
    return full.astype(jnp.bfloat16)


def split_params(kernels, vector):
    w_single, w_reduce, w_spatial, w_squeeze, w_narrow, w_project = kernels
    widths = [
        w_single.shape[1],
        w_reduce.shape[1],
        w_spatial.shape[-1],
        w_squeeze.shape[1],
        w_narrow.shape[-1],
        w_project.shape[1],
    ]
    pieces = []
    start = 0
    for width in widths:
        pieces.append(vector[start : start + width])
        start = start + width
    return pieces


def block_forward(source, kernels, gains, offsets, mask, count):
    w_single, w_reduce, w_spatial, w_squeeze, w_narrow, w_project = kernels
    gamma = split_params(kernels, gains)
    beta = split_params(kernels, offsets)
    z_single = point_forward(source, w_single)
    z_reduce = point_forward(source, w_reduce)
    z_squeeze = point_forward(source, w_squeeze)
    pooled_low = neighbour_mean(source.astype(jnp.float32)).astype(jnp.bfloat16)
    z_project = point_forward(pooled_low, w_project)
    first = sync_stats(
        [local_stats(item, mask) for item in (z_single, z_reduce, z_squeeze, z_project)]
    )
    out_single, keep_single = normalize(z_single, first[0], count, gamma[0], beta[0], mask)
    out_reduce, keep_reduce = normalize(z_reduce, first[1], count, gamma[1], beta[1], mask)
    out_squeeze, keep_squeeze = normalize(z_squeeze, first[2], count, gamma[3], beta[3], mask)
    out_project, keep_project = normalize(z_project, first[3], count, gamma[5], beta[5], mask)
    reduce_low = out_reduce.astype(jnp.bfloat16)
    squeeze_low = out_squeeze.astype(jnp.bfloat16)
    z_spatial = spatial_forward(reduce_low, w_spatial)
    z_narrow = spatial_forward(squeeze_low, w_narrow)
    second = sync_stats([local_stats(z_spatial, mask), local_stats(z_narrow, mask)])
    out_spatial, keep_spatial = normalize(z_spatial, second[0], count, gamma[2], beta[2], mask)
    out_narrow, keep_narrow = normalize(z_narrow, second[1], count, gamma[4], beta[4], mask)
    result = jnp.concatenate([out_single, out_spatial, out_narrow, out_project], axis=-1)
    inputs = (source, reduce_low, squeeze_low, pooled_low)
    kept = (keep_single, keep_reduce, keep_spatial, keep_squeeze, keep_narrow, keep_project)
    return (result, (inputs, kept))


def block_backward(grad_out, saved, kernels, gains, mask, count):
    w_single, w_reduce, w_spatial, w_squeeze, w_narrow, w_project = kernels
    inputs, kept = saved
    source, reduce_low, squeeze_low, pooled_low = inputs
    keep_single, keep_reduce, keep_spatial, keep_squeeze, keep_narrow, keep_project = kept
    gamma = split_params(kernels, gains)
    edge_one = w_single.shape[1]
    edge_two = edge_one + w_spatial.shape[-1]
    edge_three = edge_two + w_narrow.shape[-1]
    grad_single = grad_out[..., :edge_one]
    grad_spatial = grad_out[..., edge_one:edge_two]
    grad_narrow = grad_out[..., edge_two:edge_three]
    grad_project = grad_out[..., edge_three:]
    shift_spatial, sums_spatial = unit_terms(grad_spatial, keep_spatial, mask)
    shift_narrow, sums_narrow = unit_terms(grad_narrow, keep_narrow, mask)
    second = sync_stats([sums_spatial, sums_narrow])
    dz_spatial = unit_grad(shift_spatial, keep_spatial, gamma[2], second[0], count, mask)
    dz_narrow = unit_grad(shift_narrow, keep_narrow, gamma[4], second[1], count, mask)
    kernel_spatial, grad_reduce = spatial_backward(reduce_low, w_spatial, dz_spatial)
    kernel_narrow, grad_squeeze = spatial_backward(squeeze_low, w_narrow, dz_narrow)
    shift_single, sums_single = unit_terms(grad_single, keep_single, mask)
    shift_reduce, sums_reduce = unit_terms(grad_reduce, keep_reduce, mask)
    shift_squeeze, sums_squeeze = unit_terms(grad_squeeze, keep_squeeze, mask)
    shift_project, sums_project = unit_terms(grad_project, keep_project, mask)
    first = sync_stats([sums_single, sums_reduce, sums_squeeze, sums_project])
    dz_single = unit_grad(shift_single, keep_single, gamma[0], first[0], count, mask)
    dz_reduce = unit_grad(shift_reduce, keep_reduce, gamma[1], first[1], count, mask)
    dz_squeeze = unit_grad(shift_squeeze, keep_squeeze, gamma[3], first[2], count, mask)
    dz_project = unit_grad(shift_project, keep_project, gamma[5], first[3], count, mask)
    kernel_single, from_single = point_backward(source, w_single, dz_single)
    kernel_reduce, from_reduce = point_backward(source, w_reduce, dz_reduce)
    kernel_squeeze, from_squeeze = point_backward(source, w_squeeze, dz_squeeze)
    kernel_project, from_pooled = point_backward(pooled_low, w_project, dz_project)
    source_grad = from_single + from_reduce + from_squeeze + neighbour_mean(from_pooled)
    order = [first[0], first[1], second[0], first[2], second[1], first[3]]
    scale_grad = jnp.concatenate([item[1] for item in order])
    shift_grad = jnp.concatenate([item[0] for item in order])
    kernel_grads = (
        kernel_single,
        kernel_reduce,
        kernel_spatial,
        kernel_squeeze,
        kernel_narrow,
        kernel_project,
    )
    return (source_grad, kernel_grads, scale_grad, shift_grad)


def shards(
    clip_input,
    cotangent,
    clip_group,
    crop_sides,
    w_single,
    w_reduce,
    w_spatial,
    w_squeeze,
    w_narrow,
    w_project,
    bn_scale,
    bn_shift,
):
    mask, small_mask = crop_masks(clip_group, crop_sides, clip_input.shape[1], clip_input.shape[2])
    count = lax.psum(jnp.sum(mask), ("dp", "rep"))
    small_count = count / 8.0
    lower = (w_single[0], w_reduce[0], w_spatial[0], w_squeeze[0], w_narrow[0], w_project[0])
    upper = (w_single[1], w_reduce[1], w_spatial[1], w_squeeze[1], w_narrow[1], w_project[1])
    source = clip_input * mask.astype(jnp.bfloat16)
    first_out, first_saved = block_forward(source, lower, bn_scale[0], bn_shift[0], mask, count)
    middle = pool_pairs(first_out).astype(jnp.bfloat16)
    second_out, second_saved = block_forward(
        middle, upper, bn_scale[1], bn_shift[1], small_mask, small_count
    )
    middle_grad, upper_grads, upper_scale, upper_shift = block_backward(
        cotangent.astype(jnp.float32), second_saved, upper, bn_scale[1], small_mask, small_count
    )
    source_grad, lower_grads, lower_scale, lower_shift = block_backward(
        spread_pairs(middle_grad), first_saved, lower, bn_scale[0], mask, count
    )
    joined = [
        jnp.stack([low_item, high_item]) for low_item, high_item in zip(lower_grads, upper_grads)
    ]
    stacked = lax.psum(
        (joined[0], joined[1], joined[2], joined[3], joined[4], joined[5]), ("dp", "rep")
    )
    input_grad = (source_grad * mask).astype(jnp.bfloat16)
    return (
        second_out.astype(jnp.bfloat16),
        input_grad,
        stacked[0],
        stacked[1],
        stacked[2],
        stacked[3],
        stacked[4],
        stacked[5],
        jnp.stack([lower_scale, upper_scale]),
        jnp.stack([lower_shift, upper_shift]),
    )


def solution(mesh):
    placed = (
        P(("dp", "rep"), None, None, None, None),
        P(("dp", "rep"), None, None, None, None),
        P(("dp", "rep")),
        P(),
        P(),
        P(),
        P(),
        P(),
        P(),
        P(),
        P(),
        P(),
    )
    return jax.shard_map(
        shards,
        mesh=mesh,
        in_specs=placed,
        out_specs=(
            P(("dp", "rep"), None, None, None, None),
            P(("dp", "rep"), None, None, None, None),
            P(),
            P(),
            P(),
            P(),
            P(),
            P(),
            P(),
            P(),
        ),
        check_vma=False,
    )
```

```python
import functools

import jax
import jax.numpy as jnp
from jax import lax
from jax.experimental import pallas as pl
from jax.experimental.pallas import tpu as pltpu
from jax.sharding import PartitionSpec as P

AXES = ("dp", "rep")
F32 = jnp.float32
LOW = jnp.bfloat16
EDGE = 32
TAPS = [(dh, dw) for dh in (-1, 0, 1) for dw in (-1, 0, 1)]
UNIT_TILES = [("b", 0), ("b", 1), ("c", 0), ("c", 1), ("c", 2), ("c", 3), ("b", 2)]
VMEM = pl.BlockSpec(memory_space=pltpu.VMEM)
SMEM = pl.BlockSpec(memory_space=pltpu.SMEM)
MIB = 1024 * 1024


def struct(shape, kind):
    return jax.ShapeDtypeStruct(shape, kind)


def call(body, ins, outs, scratch=(), scalars=2, limit=48, flops=0, name=None):
    return pl.pallas_call(
        body,
        out_shape=tuple(outs),
        in_specs=[SMEM] * scalars + [VMEM] * (len(ins) - scalars),
        out_specs=tuple([VMEM] * len(outs)),
        scratch_shapes=list(scratch),
        compiler_params=pltpu.CompilerParams(vmem_limit_bytes=limit * MIB),
        cost_estimate=pl.CostEstimate(
            flops=flops,
            bytes_accessed=sum(x.size * x.dtype.itemsize for x in ins),
            transcendentals=0,
        ),
        name=name,
    )(*ins)


def tile(index, width=1):
    return slice(index * 128, (index + width) * 128)


def lanes():
    return lax.broadcasted_iota(jnp.int32, (1, 128), 1)


def sigmoid(v):
    return 0.5 * jnp.tanh(0.5 * v) + 0.5


def places(frame, side):
    at = lax.broadcasted_iota(jnp.int32, (frame, 1), 0).astype(F32)
    row = jnp.floor((at + 0.5) * (1.0 / side))
    return row, at - row * side


def crop_mask(frame, side, crop):
    row, column = places(frame, side)
    return jnp.where((row < crop) & (column < crop), 1.0, 0.0).astype(F32)


def column_mask(frame, side, step):
    row, column = places(frame, side)
    inside = (column + step > -0.5) & (column + step < side - 0.5)
    return jnp.where(inside, 1.0, 0.0).astype(F32)


def crop_of(group_ref, sides_ref, halved):
    crop = sides_ref[group_ref[0]]
    if halved:
        crop = lax.shift_right_logical(crop, 1)
    return crop.astype(F32)


def moments(sums, count):
    mean = sums[0:1] / count
    square = sums[1:2] / count
    return mean, lax.rsqrt(square - mean * mean + 1e-05)


def back_terms(sums, count, gamma, inverse):
    scale = gamma * inverse
    return scale, scale * (sums[0:1] / count), scale * (sums[1:2] / count)


def add_sums(ref, at, first, second):
    ref[0:1, at] += jnp.sum(first, axis=0, keepdims=True)
    ref[1:2, at] += jnp.sum(second, axis=0, keepdims=True)


def neighbour_sum(values, around, frame, side, put):
    frames = len(values)
    left = column_mask(frame, side, -1)
    right = column_mask(frame, side, 1)
    for t in range(frames):
        total = values[t]
        if t > 0:
            total = total + values[t - 1]
        if t < frames - 1:
            total = total + values[t + 1]
        around[EDGE : EDGE + frame, tile(0)] = total
        total = (
            total
            + around[EDGE - side : EDGE - side + frame, tile(0)]
            + around[EDGE + side : EDGE + side + frame, tile(0)]
        )
        around[EDGE : EDGE + frame, tile(0)] = total
        total = (
            total
            + around[EDGE - 1 : EDGE - 1 + frame, tile(0)] * left
            + around[EDGE + 1 : EDGE + 1 + frame, tile(0)] * right
        )
        put(t, total * (1.0 / 27.0))


def clear_edges(around, frame):
    width = around.shape[1]
    around[0:EDGE, :] = jnp.zeros((EDGE, width), F32)
    around[EDGE + frame : 2 * EDGE + frame, :] = jnp.zeros((EDGE, width), F32)


def dot(a, b):
    return lax.dot_general(a, b, (((1,), (0,)), ((), ())), preferred_element_type=F32)


def dot_nt(a, b):
    return lax.dot_general(a, b, (((1,), (1,)), ((), ())), preferred_element_type=F32)


def dot_tn(a, b):
    return lax.dot_general(a, b, (((0,), (0,)), ((), ())), preferred_element_type=F32)


class Layer:
    def __init__(self, frames, side, halved):
        self.frames = frames
        self.side = side
        self.halved = halved
        self.frame = -(-side * side // 16) * 16
        self.rows = frames * self.frame

    def at(self, t):
        return slice(t * self.frame, (t + 1) * self.frame)


def point_a(layer, mask, x_ref, w_ref, za_ref, sums_ref):
    sums_ref[...] = jnp.zeros(sums_ref.shape, F32)
    for t in range(layer.frames):
        z = dot(x_ref[layer.at(t), :], w_ref[:, 384:768])
        za_ref[layer.at(t), :] = z
        for j in range(3):
            part = z[:, tile(j)] * mask
            add_sums(sums_ref, tile(j), part, part * z[:, tile(j)])
    cells = jnp.sum(mask, axis=0, keepdims=True) * layer.frames
    sums_ref[2:3, :] = jnp.broadcast_to(cells, (1, 384))


def point_b(layer, mask, x_ref, w_ref, zb_ref, sums_ref, around):
    sums_ref[...] = jnp.zeros(sums_ref.shape, F32)
    clear_edges(around, layer.frame)
    flat = []
    for t in range(layer.frames):
        z = dot(x_ref[layer.at(t), :], w_ref[:, 0:384])
        zb_ref[layer.at(t), 0:256] = z[:, 0:256]
        zb_ref[layer.at(t), tile(2)] = z[:, tile(2)] * mask
        for j in range(2):
            part = z[:, tile(j)] * mask
            add_sums(sums_ref, tile(j), part, part * z[:, tile(j)])
    flat = [zb_ref[layer.at(t), tile(2)] for t in range(layer.frames)]

    def put(t, value):
        zb_ref[layer.at(t), tile(2)] = value
        part = value * mask
        add_sums(sums_ref, tile(2), part, part * value)

    neighbour_sum(flat, around, layer.frame, layer.side, put)


def first_a(layer, group_ref, sides_ref, x_ref, w_ref, za_ref, sums_ref):
    mask = crop_mask(layer.frame, layer.side, crop_of(group_ref, sides_ref, layer.halved))
    point_a(layer, mask, x_ref, w_ref, za_ref, sums_ref)


def first_b(layer, group_ref, sides_ref, x_ref, w_ref, zb_ref, sums_ref, around):
    mask = crop_mask(layer.frame, layer.side, crop_of(group_ref, sides_ref, layer.halved))
    point_b(layer, mask, x_ref, w_ref, zb_ref, sums_ref, around)


def conv_forward(
    layer, group_ref, sides_ref, za_ref, suma_ref, para_ref, sumb_ref, w_ref, wn_ref,
    wide_ref, thin_ref, zc_ref, sums_ref, around, rem,
):
    frames, frame, side = layer.frames, layer.frame, layer.side
    mask = crop_mask(frame, side, crop_of(group_ref, sides_ref, layer.halved))
    count = suma_ref[2:3, :]
    mean, inverse = moments(suma_ref, count)
    gain = para_ref[0:1, :] * inverse
    offset = para_ref[1:2, :] - mean * gain
    column = [column_mask(frame, side, dw) for dw in (-1, 0, 1)]
    part_of = lanes() // 32
    clear_edges(around, frame)
    for t in range(frames):
        rows = layer.at(t)
        for j in range(3):
            u = za_ref[rows, tile(j)] * gain[:, tile(j)] + offset[:, tile(j)]
            around[EDGE : EDGE + frame, tile(j)] = u * sigmoid(u) * mask
        mixed = {1: [None] * 3, 2: [None] * 3}
        for k, (dh, dw) in enumerate(TAPS):
            start = EDGE + dh * side + dw
            shifted = around[start : start + frame, tile(0)]
            if dw:
                shifted = shifted * column[dw + 1]
            wide_ref[rows, tile(k)] = shifted.astype(LOW)
            for j in (1, 2):
                shifted = around[start : start + frame, tile(j)]
                if dw:
                    shifted = shifted * column[dw + 1]
                shifted = jnp.where(part_of == k % 4, shifted, 0.0)
                held = mixed[j][k // 4]
                mixed[j][k // 4] = shifted if held is None else held + shifted
        for g in range(3):
            wide_ref[rows, tile(9 + g)] = mixed[1][g].astype(LOW)
            thin_ref[rows, tile(g)] = mixed[2][g].astype(LOW)
    sums_ref[:, 0:384] = sumb_ref[...]
    sums_ref[:, 384:896] = jnp.zeros((2, 512), F32)
    zc_ref[...] = jnp.zeros(zc_ref.shape, F32)
    for t in range(frames):
        source = wide_ref[layer.at(t), :]
        thin = thin_ref[layer.at(t), :]
        for k in range(3):
            to = t + 1 - k
            if 0 <= to < frames:
                rows = layer.at(to)
                zc_ref[rows, 0:256] += dot(source, w_ref[:, k * 256 : (k + 1) * 256])
                zc_ref[rows, tile(3)] += dot(thin, wn_ref[:, tile(k)])
        rem[layer.at(t), :] = dot(source, w_ref[:, 768:1024])
    for t in range(frames):
        rows = layer.at(t)
        total = pltpu.roll(rem[rows, 0:128], 64, 1)
        if t > 0:
            total = total + rem[layer.at(t - 1), 0:128]
        if t < frames - 1:
            total = total + rem[layer.at(t + 1), 128:256]
        zc_ref[rows, tile(2)] = jnp.where(lanes() < 64, total, 0.0)
        for j in range(4):
            z = zc_ref[rows, tile(j)]
            part = z * mask
            add_sums(sums_ref, tile(3 + j), part, part * z)


class Norms:
    def __init__(self, sums_ref, par_ref, count):
        mean, inverse = moments(sums_ref, count)
        self.mean, self.inverse = mean, inverse
        self.gamma, self.beta = par_ref[0:1, :], par_ref[1:2, :]

    def lane(self, kind, j):
        return tile(j if kind == "b" else 3 + j)

    def normed(self, z, at):
        return (z - self.mean[:, at]) * self.inverse[:, at]

    def shifted(self, n, at):
        return self.gamma[:, at] * n + self.beta[:, at]


def finish_lower(
    lower, upper, group_ref, sides_ref, zb_ref, zc_ref, suma_ref, sums_ref, par_ref, w_ref,
    q_ref, za2_ref, zb2_ref, suma2_ref, sumb2_ref, around, y_ref,
):
    crop = crop_of(group_ref, sides_ref, False)
    mask = crop_mask(lower.frame, lower.side, crop)
    norms = Norms(sums_ref, par_ref, suma_ref[2:3, 0:1])
    pick = pair_matrix(upper, lower)
    for t in range(upper.frames):
        for index, (kind, j) in enumerate(UNIT_TILES):
            at = norms.lane(kind, j)
            z_ref = zb_ref if kind == "b" else zc_ref
            total = None
            for source in (2 * t, 2 * t + 1):
                u = norms.shifted(norms.normed(z_ref[lower.at(source), tile(j)], at), at)
                out = u * sigmoid(u) * mask
                total = out if total is None else total + out
            high = total.astype(LOW)
            y_ref[:, tile(index)] = high
            y_ref[:, tile(7 + index)] = (total - high.astype(F32)).astype(LOW)
        both = dot(pick, y_ref[...])
        q_ref[upper.at(t), :] = (both[:, 0:896] + both[:, 896:1792]).astype(LOW)
    small = crop_mask(upper.frame, upper.side, crop_of(group_ref, sides_ref, True))
    point_a(upper, small, q_ref, w_ref, za2_ref, suma2_ref)
    point_b(upper, small, q_ref, w_ref, zb2_ref, sumb2_ref, around)


def pair_matrix(upper, lower):
    at = lax.broadcasted_iota(jnp.int32, (upper.frame, lower.frame), 1).astype(F32)
    row = jnp.floor((at + 0.5) * (1.0 / lower.side))
    column = at - row * lower.side
    group = jnp.floor(row * 0.5 + 0.25) * upper.side + jnp.floor(column * 0.5 + 0.25)
    mine = lax.broadcasted_iota(jnp.int32, (upper.frame, lower.frame), 0).astype(F32)
    return jnp.where(jnp.abs(group - mine) < 0.5, 0.125, 0.0).astype(LOW)


def spread_matrix(upper, lower):
    at = lax.broadcasted_iota(jnp.int32, (lower.frame, upper.frame), 0).astype(F32)
    row = jnp.floor((at + 0.5) * (1.0 / lower.side))
    column = at - row * lower.side
    group = jnp.floor(row * 0.5 + 0.25) * upper.side + jnp.floor(column * 0.5 + 0.25)
    mine = lax.broadcasted_iota(jnp.int32, (lower.frame, upper.frame), 1).astype(F32)
    return jnp.where(jnp.abs(group - mine) < 0.5, 0.125, 0.0).astype(LOW)


def finish_upper(
    layer, group_ref, sides_ref, zb_ref, zc_ref, suma_ref, sums_ref, par_ref, cot_ref,
    out_ref, gu_ref, back_ref,
):
    mask = crop_mask(layer.frame, layer.side, crop_of(group_ref, sides_ref, layer.halved))
    norms = Norms(sums_ref, par_ref, suma_ref[2:3, 0:1])
    back_ref[...] = jnp.zeros(back_ref.shape, F32)
    for t in range(layer.frames):
        rows = layer.at(t)
        for index, (kind, j) in enumerate(UNIT_TILES):
            at = norms.lane(kind, j)
            z_ref = zb_ref if kind == "b" else zc_ref
            n = norms.normed(z_ref[rows, tile(j)], at)
            u = norms.shifted(n, at)
            s = sigmoid(u)
            out_ref[rows, tile(index)] = (u * s * mask).astype(LOW)
            gu = cot_ref[rows, tile(index)].astype(F32) * mask * (s * (1.0 + u * (1.0 - s)))
            gu_ref[rows, tile(index)] = gu
            add_sums(back_ref, at, gu, gu * n)


def unit_backward(
    layer, group_ref, sides_ref, gu_ref, zb_ref, zc_ref, suma_ref, sums_ref, back_ref, par_ref,
    dzb_ref, three_ref, thin3_ref, around, flat,
):
    frames, frame, side = layer.frames, layer.frame, layer.side
    mask = crop_mask(frame, side, crop_of(group_ref, sides_ref, layer.halved))
    count = suma_ref[2:3, 0:1]
    norms = Norms(sums_ref, par_ref, count)
    c0, c1, c2 = back_terms(back_ref, count, norms.gamma, norms.inverse)
    low_half = lanes() < 64

    def dz_of(t, index):
        kind, j = UNIT_TILES[index]
        at = norms.lane(kind, j)
        z_ref = zb_ref if kind == "b" else zc_ref
        rows = layer.at(t)
        n = norms.normed(z_ref[rows, tile(j)], at)
        return (gu_ref[rows, tile(index)] * c0[:, at] - c1[:, at] - n * c2[:, at]) * mask

    clear_edges(around, frame)
    for t in range(frames):
        for index in (0, 1):
            dzb_ref[layer.at(t), tile(index)] = dz_of(t, index).astype(LOW)
        flat[layer.at(t), :] = dz_of(t, 6)

    def put(t, value):
        dzb_ref[layer.at(t), tile(2)] = (value * mask).astype(LOW)

    neighbour_sum([flat[layer.at(t), :] for t in range(frames)], around, frame, side, put)
    for t in range(frames):
        flat[layer.at(t), :] = jnp.where(low_half, dz_of(t, 4), 0.0)
    empty = jnp.zeros((frame, 128), LOW)
    for t in range(frames):
        parts = [dz_of(t, index).astype(LOW) for index in (2, 3, 5)]
        for k in range(3):
            to = t - 1 + k
            if 0 <= to < frames:
                rows = layer.at(to)
                three_ref[rows, tile(2 * k)] = parts[0]
                three_ref[rows, tile(2 * k + 1)] = parts[1]
                thin3_ref[rows, tile(k)] = parts[2]
        rest = pltpu.roll(flat[layer.at(t), :], 64, 1)
        if t < frames - 1:
            rest = rest + flat[layer.at(t + 1), :]
        three_ref[layer.at(t), tile(6)] = rest.astype(LOW)
        three_ref[layer.at(t), tile(7)] = flat[layer.at(t - 1), :].astype(LOW) if t else empty
    for rows, k in ((layer.at(0), 2), (layer.at(frames - 1), 0)):
        three_ref[rows, tile(2 * k)] = empty
        three_ref[rows, tile(2 * k + 1)] = empty
        thin3_ref[rows, tile(k)] = empty


def conv_backward(
    layer, group_ref, sides_ref, three_ref, thin3_ref, za_ref, suma_ref, para_ref, wt_ref, wnt_ref,
    gua_ref, backa_ref, around, shifts, thins, rem, main,
):
    frames, frame, side = layer.frames, layer.frame, layer.side
    mask = crop_mask(frame, side, crop_of(group_ref, sides_ref, layer.halved))
    column = [column_mask(frame, side, dw) for dw in (-1, 0, 1)]
    low_half = lanes() < 64
    first_part = lanes() < 32
    clear_edges(around, frame)
    main[...] = jnp.zeros(main.shape, F32)
    rem[...] = jnp.zeros(rem.shape, F32)
    for t in range(frames):
        rows = layer.at(t)
        rest = jnp.where(low_half, 0.0, three_ref[rows, tile(6)].astype(F32))
        parts = [
            three_ref[rows, tile(2)].astype(F32),
            three_ref[rows, tile(3)].astype(F32),
            rest + pltpu.roll(rest, 64, 1),
            thin3_ref[rows, tile(1)].astype(F32),
        ]
        for j in range(4):
            around[EDGE : EDGE + frame, tile(j)] = parts[j]
        mixed = [None] * 5
        for k, (dh, dw) in enumerate(TAPS):
            start = EDGE - dh * side - dw
            for j in range(4):
                shifted = around[start : start + frame, tile(j)]
                if dw:
                    shifted = shifted * column[1 - dw]
                if j < 2:
                    shifts[:, tile(2 * k + j)] = shifted.astype(LOW)
                elif j == 3:
                    thins[:, tile(k)] = shifted.astype(LOW)
                else:
                    shifted = jnp.where(low_half if k % 2 == 0 else ~low_half, shifted, 0.0)
                    held = mixed[k // 2]
                    mixed[k // 2] = shifted if held is None else held + shifted
        for g in range(5):
            shifts[:, tile(18 + g)] = mixed[g].astype(LOW)
        product = dot_nt(shifts[...], wt_ref[...])
        thin = dot_nt(thins[...], wnt_ref[...])
        for k in range(3):
            to = t - 1 + k
            if 0 <= to < frames:
                rows = layer.at(to)
                main[rows, :] += product[:, tile(k)]
                turn = (128 - 32 * k) % 128
                last = product[:, tile(3)]
                rem[rows, 0:128] += last if turn == 0 else pltpu.roll(last, turn, 1)
                rem[rows, 128:256] += thin if turn == 0 else pltpu.roll(thin, turn, 1)
    mean, inverse = moments(suma_ref, suma_ref[2:3, :])
    backa_ref[...] = jnp.zeros(backa_ref.shape, F32)
    for t in range(frames):
        rows = layer.at(t)
        for j in range(3):
            grad = main[rows, :] if j == 0 else rem[rows, tile(j - 1)]
            n = (za_ref[rows, tile(j)] - mean[:, tile(j)]) * inverse[:, tile(j)]
            u = para_ref[0:1, tile(j)] * n + para_ref[1:2, tile(j)]
            s = sigmoid(u)
            gu = grad * mask * (s * (1.0 + u * (1.0 - s)))
            if j:
                gu = jnp.where(first_part, gu, 0.0)
            gua_ref[rows, tile(j)] = gu
            add_sums(backa_ref, tile(j), gu, gu * n)


def point_back(layer, mask, gua_ref, za_ref, suma_ref, backa_ref, para_ref, dza_ref):
    count = suma_ref[2:3, :]
    mean, inverse = moments(suma_ref, count)
    c0, c1, c2 = back_terms(backa_ref, count, para_ref[0:1, :], inverse)
    for t in range(layer.frames):
        rows = layer.at(t)
        for j in range(3):
            at = tile(j)
            n = (za_ref[rows, at] - mean[:, at]) * inverse[:, at]
            dz = (gua_ref[rows, at] * c0[:, at] - c1[:, at] - n * c2[:, at]) * mask
            if j:
                dz = jnp.where(lanes() < 32, dz, 0.0)
            dza_ref[rows, at] = dz.astype(LOW)


def join_blocks(
    upper, lower, group_ref, sides_ref, gua_ref, za_ref, suma_ref, backa_ref, para_ref, dzb_ref, w_ref,
    zb_ref, zc_ref, suma1_ref, sums1_ref, par1_ref, dza_ref, gu_ref, back_ref, wide,
):
    small = crop_mask(upper.frame, upper.side, crop_of(group_ref, sides_ref, True))
    point_back(upper, small, gua_ref, za_ref, suma_ref, backa_ref, para_ref, dza_ref)
    mask = crop_mask(lower.frame, lower.side, crop_of(group_ref, sides_ref, False))
    norms = Norms(sums1_ref, par1_ref, suma1_ref[2:3, 0:1])
    back_ref[...] = jnp.zeros(back_ref.shape, F32)
    pick = spread_matrix(upper, lower)
    for t in range(upper.frames):
        rows = upper.at(t)
        dq = dot_nt(dzb_ref[rows, :], w_ref[:, 0:384]) + dot_nt(dza_ref[rows, :], w_ref[:, 384:768])
        high = dq.astype(LOW)
        rest = (dq - high.astype(F32)).astype(LOW)
        wide[...] = dot(pick, high) + dot(pick, rest)
        for source in (2 * t, 2 * t + 1):
            at_rows = lower.at(source)
            for index, (kind, j) in enumerate(UNIT_TILES):
                at = norms.lane(kind, j)
                z_ref = zb_ref if kind == "b" else zc_ref
                n = norms.normed(z_ref[at_rows, tile(j)], at)
                u = norms.shifted(n, at)
                s = sigmoid(u)
                gu = wide[:, tile(index)] * mask * (s * (1.0 + u * (1.0 - s)))
                gu_ref[at_rows, tile(index)] = gu
                add_sums(back_ref, at, gu, gu * n)


def last_back(
    layer, group_ref, sides_ref, gua_ref, za_ref, suma_ref, backa_ref, para_ref, dzb_ref, w_ref, dza_ref, grad_ref,
):
    mask = crop_mask(layer.frame, layer.side, crop_of(group_ref, sides_ref, layer.halved))
    point_back(layer, mask, gua_ref, za_ref, suma_ref, backa_ref, para_ref, dza_ref)
    for t in range(layer.frames):
        rows = layer.at(t)
        total = dot_nt(dzb_ref[rows, :], w_ref[:, 0:384]) + dot_nt(dza_ref[rows, :], w_ref[:, 384:768])
        grad_ref[rows, :] = (total * mask).astype(LOW)


def place(me, pair, core):
    bits = lax.shift_right_logical(me, 1) ^ pair
    x, y = bits & 1, lax.shift_right_logical(bits, 1) & 1
    near, far = lax.shift_right_logical(bits, 2) & 1, lax.shift_right_logical(bits, 3) & 1
    first = x + core * (y - x)
    second = y + core * (x - y)
    return first * 8 + second * 4 + near * 2 + far


def put_pair(me, keep_ref, send_ref, pair, rows, even, odd):
    core = me & 1
    mine = core == 0
    keep_ref[place(me, pair, core), rows, :] = jnp.where(mine, even, odd)
    send_ref[place(me, pair, 1 - core), rows, :] = jnp.where(mine, odd, even)


def get_pair(me, own_ref, other_ref, pair, rows):
    core = me & 1
    mine = core == 0
    own = own_ref[place(me, pair, core), rows, :]
    other = other_ref[place(me, pair, 1 - core), rows, :]
    return jnp.where(mine, own, other), jnp.where(mine, other, own)


def segments(blocks):
    rows = -(-sum(length for _, length in blocks) // 256) * 8
    pieces, piece, room = [], [], rows
    for name, length in blocks:
        at = 0
        while at < length:
            take = min(room, length - at)
            piece.append((name, at, at + take, rows - room))
            at += take
            room -= take
            if not room:
                pieces.append(piece)
                piece, room = [], rows
    if piece:
        pieces.append(piece)
    return rows, pieces + [[]] * (32 - len(pieces))


PARTS = [
    [("wide", j, 1440) for j in range(4)],
    [("wide", j, 1440) for j in range(4, 8)] + [("point", j, 832) for j in range(3)] + [("thin", j, 288) for j in range(3)],
    [("last", j, 832) for j in range(2)],
]
PARTS = [segments([((kind, j), length) for kind, j, length in part]) for part in PARTS]


def piece_value(piece, rows, read):
    parts = [read(name, first, end) for name, first, end, _ in piece]
    filled = sum(end - first for _, first, end, _ in piece)
    if filled < rows:
        parts.append(jnp.zeros((rows - filled, 128), F32))
    return parts[0] if len(parts) == 1 else jnp.concatenate(parts, axis=0)


def put_pieces(me, keep_ref, send_ref, part, read):
    rows, pieces = part
    for pair in range(16):
        even, odd = (piece_value(pieces[2 * pair + i], rows, read) for i in (0, 1))
        put_pair(me, keep_ref, send_ref, pair, slice(0, rows), even, odd)


def without_gap(ref, grad):
    if grad.shape[0] == 896:
        ref[0:576, :] = grad[0:576]
        ref[576:832, :] = grad[640:896]
    else:
        ref[...] = grad


def first_weights(me_ref, wide_ref, three_ref, keep_ref, send_ref, wide_grad):
    for n in range(2):
        wide_grad[:, n * 256 : (n + 1) * 256] = dot_tn(wide_ref[:, 0:1440], three_ref[:, n * 256 : (n + 1) * 256])

    def read(name, first, end):
        return wide_grad[first:end, tile(name[1])]

    put_pieces(me_ref[0], keep_ref, send_ref, PARTS[0], read)


def other_weights(
    me_ref, wide_ref, three_ref, thin_ref, thin3_ref, x_ref, dzb_ref, keep_ref, send_ref, wide_grad, thin_grad, point_grad
):
    for n in range(2):
        wide_grad[:, n * 256 : (n + 1) * 256] = dot_tn(wide_ref[:, 0:1440], three_ref[:, (n + 2) * 256 : (n + 3) * 256])
    thin_grad[...] = dot_tn(thin_ref[...], thin3_ref[...])
    without_gap(point_grad, dot_tn(x_ref[...], dzb_ref[...]))

    def read(name, first, end):
        kind, j = name
        if kind == "wide":
            return wide_grad[first:end, tile(j - 4)]
        return (point_grad if kind == "point" else thin_grad)[first:end, tile(j)]

    put_pieces(me_ref[0], keep_ref, send_ref, PARTS[1], read)


def last_weights(me_ref, x_ref, dza_ref, keep_ref, send_ref, last_grad):
    grad = dot_tn(x_ref[...], dza_ref[...])
    mixed = jnp.where(lanes() < 32, grad[:, 128:256], pltpu.roll(grad[:, 256:384], 32, 1))
    without_gap(last_grad, jnp.concatenate([grad[:, 0:128], mixed], axis=1))

    def read(name, first, end):
        return last_grad[first:end, tile(name[1])]

    put_pieces(me_ref[0], keep_ref, send_ref, PARTS[2], read)


def assemble(index, aliased, me_ref, *refs):
    me = me_ref[0]
    arrived, refs = refs[0:6], refs[6 + (6 if aliased else 0) :]
    outs, stages, sems = refs[0:6], refs[6:12], refs[12]
    single, reduce, spatial, squeeze, narrow, project = stages

    def put_wide(k, lanes_at, first, value):
        done = 0
        while done < value.shape[0]:
            row = first + done
            if row < 1152:
                tap, channel = row // 128, row % 128
                take = min(128 - channel, value.shape[0] - done)
            else:
                tap, channel = (row - 1152) // 32, 128 + (row - 1152) % 32
                take = min(160 - channel, value.shape[0] - done)
            spatial[k * 9 + tap, channel : channel + take, lanes_at] = value[done : done + take]
            done += take

    def put(name, first, end, value):
        kind, j = name
        if kind == "wide":
            if j < 6:
                put_wide(j // 2, tile(j % 2), first, value)
            elif j == 6:
                put_wide(0, slice(256, 320), first, value[:, 0:64])
                put_wide(1, slice(256, 320), first, pltpu.roll(value, 64, 1)[:, 0:64])
            else:
                put_wide(2, slice(256, 320), first, value[:, 0:64])
        elif kind == "point":
            if j < 2:
                single[first:end, tile(j)] = value
            else:
                project[first:end, :] = value
        elif kind == "thin":
            done = 0
            while done < end - first:
                tap, channel = (first + done) // 32, (first + done) % 32
                take = min(32 - channel, end - first - done)
                narrow[j * 9 + tap, channel : channel + take, :] = value[done : done + take]
                done += take
        elif j == 0:
            reduce[first:end, 0:128] = value
        else:
            reduce[first:end, 128:160] = value[:, 0:32]
            squeeze[first:end, :] = pltpu.roll(value, 96, 1)[:, 0:32]

    for at, (rows, pieces) in enumerate(PARTS):
        for pair in range(16):
            both = get_pair(me, arrived[2 * at], arrived[2 * at + 1], pair, slice(0, rows))
            for i in (0, 1):
                for name, first, end, row in pieces[2 * pair + i]:
                    put(name, first, end, both[i][row : row + end - first])
    copies = [pltpu.make_async_copy(stages[i], outs[i].at[index], sems.at[i]) for i in range(6)]
    for copy in copies:
        copy.start()
    for copy in copies:
        copy.wait()


OUT_SHAPES = [(832, 256), (832, 160), (27, 160, 320), (832, 32), (27, 32, 128), (832, 128)]


def assemble_call(index, me, arrived, outs):
    anywhere = pl.BlockSpec(memory_space=pl.ANY)
    return pl.pallas_call(
        functools.partial(assemble, index, outs is not None),
        out_shape=tuple(struct((2,) + shape, F32) for shape in OUT_SHAPES),
        in_specs=[SMEM] + [VMEM] * 6 + [anywhere] * (0 if outs is None else 6),
        out_specs=tuple([anywhere] * 6),
        scratch_shapes=[pltpu.VMEM(shape, F32) for shape in OUT_SHAPES] + [pltpu.SemaphoreType.DMA((6,))],
        input_output_aliases={} if outs is None else {7 + i: i for i in range(6)},
        compiler_params=pltpu.CompilerParams(vmem_limit_bytes=48 * MIB),
        cost_estimate=pl.CostEstimate(flops=0, bytes_accessed=18_000_000, transcendentals=0),
        name="assemble",
    )(me, *arrived, *([] if outs is None else outs))


def unfit_vectors(sums_a, sums):
    return jnp.concatenate(
        [sums[:, 0:256], sums_a[:, 0:160], sums[:, 384:704], sums_a[:, 256:288], sums[:, 768:896], sums[:, 256:384]], axis=1
    )


def four_times(value):
    value = value.astype(F32)
    return jnp.concatenate([value] * 4, axis=1).astype(LOW)


def fit_points(single_ref, project_ref, reduce_ref, squeeze_ref, out_ref):
    if out_ref.shape[0] == 896:
        spans = [(slice(0, 576), slice(0, 576)), (slice(640, 896), slice(576, 832))]
        out_ref[576:640, :] = jnp.zeros((64, 768), LOW)
    else:
        spans = [(slice(0, 832), slice(0, 832))]
    for to, source in spans:
        out_ref[to, 0:256] = single_ref[0, source, :]
        out_ref[to, 256:384] = project_ref[0, source, :]
        out_ref[to, 384:512] = reduce_ref[0, source, 0:128]
        out_ref[to, 512:640] = four_times(reduce_ref[0, source, 128:160])
        out_ref[to, 640:768] = four_times(squeeze_ref[0, source, :])


def pair_lanes(left, right):
    parts = [jnp.zeros((max(p.shape[0] for p in (left, right) if p is not None), 64), F32) if p is None else p.astype(F32) for p in (left, right)]
    return jnp.concatenate(parts, axis=1).astype(LOW)


def fit_convs(
    index, scale_ref, shift_ref, spatial_ref, narrow_ref, w_ref, wn_ref, wt_ref, wnt_ref, para_ref, par_ref
):
    spans = [(0, 128, 128 * tap, tap) for tap in range(9)] + [(128, 160, 1152 + 32 * tap, tap) for tap in range(9)]
    w_ref[1440:1536, :] = jnp.zeros((96, 1024), LOW)
    for first, end, row, tap in spans:
        rows = slice(row, row + end - first)
        rest = [spatial_ref[0, 9 * k + tap, first:end, 256:320] for k in range(3)]
        for k in range(3):
            w_ref[rows, k * 256 : (k + 1) * 256] = spatial_ref[0, 9 * k + tap, first:end, 0:256]
        w_ref[rows, 768:896] = pair_lanes(rest[0], rest[1])
        w_ref[rows, 896:1024] = pair_lanes(rest[2], None)
    wt_ref[480:512, :] = jnp.zeros((32, 2944), LOW)
    for k in range(3):
        for first, end, row in ((0, 128, 128 * k), (128, 160, 384 + 32 * k)):
            rows = slice(row, row + end - first)
            for tap in range(9):
                wt_ref[rows, tap * 256 : (tap + 1) * 256] = spatial_ref[0, 9 * k + tap, first:end, 0:256]
            for g in range(5):
                left = spatial_ref[0, 9 * k + 2 * g, first:end, 256:320]
                right = spatial_ref[0, 9 * k + 2 * g + 1, first:end, 256:320] if g < 4 else None
                wt_ref[rows, tile(18 + g)] = pair_lanes(left, right)
    wn_ref[288:384, :] = jnp.zeros((96, 384), LOW)
    wnt_ref[96:128, :] = jnp.zeros((32, 1152), LOW)
    for k in range(3):
        for tap in range(9):
            part = narrow_ref[0, 9 * k + tap]
            wn_ref[32 * tap : 32 * tap + 32, tile(k)] = part
            wnt_ref[32 * k : 32 * k + 32, tile(tap)] = part
    for row, ref in ((0, scale_ref), (1, shift_ref)):
        vector = ref[index : index + 1, :]
        rest = vector[:, 384:416]
        squeeze = vector[:, 736:768]
        para_ref[row : row + 1, 0:128] = vector[:, 256:384]
        para_ref[row : row + 1, 128:256] = jnp.concatenate([rest] * 4, axis=1)
        para_ref[row : row + 1, 256:384] = jnp.concatenate([squeeze] * 4, axis=1)
        par_ref[row : row + 1, 0:256] = vector[:, 0:256]
        par_ref[row : row + 1, 256:384] = vector[:, 896:1024]
        par_ref[row : row + 1, 384:768] = jnp.concatenate([vector[:, 416:736], jnp.zeros((1, 64), F32)], axis=1)
        par_ref[row : row + 1, 768:896] = vector[:, 768:896]


def layer_call(body, index, split, whole, outs, limit=32, name=None):
    specs = [pl.BlockSpec((1,) + x.shape[1:], functools.partial(lambda n, i: (index,) + (0,) * n, x.ndim - 1)) for x in split]
    return pl.pallas_call(
        body,
        grid=(1,),
        out_shape=tuple(outs),
        in_specs=[pl.BlockSpec(x.shape, lambda i, n=x.ndim: (0,) * n) for x in whole] + specs,
        out_specs=tuple(pl.BlockSpec(x.shape, lambda i, n=len(x.shape): (0,) * n) for x in outs),
        compiler_params=pltpu.CompilerParams(vmem_limit_bytes=limit * MIB),
        cost_estimate=pl.CostEstimate(
            flops=0, bytes_accessed=2 * sum(x.size * x.dtype.itemsize for x in outs), transcendentals=0
        ),
        name=name,
    )(*whole, *split)


def exchange(value, sizes, bits):
    total = sizes[0] * sizes[1]

    def swap(mask):
        return lax.ppermute(value, AXES, [(i, i ^ mask) for i in range(total)])

    if len(bits) == 1:
        return value + swap(1 << bits[0])
    one, two = 1 << bits[0], 1 << bits[1]
    return (value + swap(one)) + (swap(two) + swap(one | two))


def sum_all(value, sizes):
    total = sizes[0] * sizes[1]
    if total & (total - 1) or sizes[1] < 2:
        return lax.psum(value, AXES)
    bits = list(range(total.bit_length() - 1))
    value = exchange(value, sizes, bits[:1])
    rest = bits[1:]
    for at in range(0, len(rest), 2):
        value = exchange(value, sizes, rest[at : at + 2])
    return value


class Sharing:
    def __init__(self, sizes):
        dp, rep = sizes
        self.sizes = sizes
        self.total = dp * rep
        self.able = not (self.total & (self.total - 1)) and dp >= 8 and rep >= 4
        low = rep.bit_length() - 1
        self.bits = [0, 1, low, low + 1, low + 2]
        self.other = [bit for bit in range(self.total.bit_length() - 1) if bit not in self.bits]

    def me(self):
        if not self.able:
            return jnp.zeros((1,), jnp.int32)
        flat = lax.axis_index("dp") * self.sizes[1] + lax.axis_index("rep")
        index = sum(((flat >> bit) & 1) << i for i, bit in enumerate(self.bits))
        return index.reshape(1).astype(jnp.int32)

    def swap(self, value, even, odd=None):
        masks = [sum(1 << self.bits[i] for i in bits) for bits in (even, even if odd is None else odd)]
        return lax.ppermute(value, AXES, [(i, i ^ masks[i & 1]) for i in range(self.total)])

    def chain(self, keep, send):
        return Chain(self, keep, send)


def after(value, *others):
    return lax.optimization_barrier((value, others))[0]


class Chain:
    def __init__(self, sharing, keep, send):
        self.sharing, self.keep, self.send, self.stage = sharing, keep, send, 0
        self.done = keep

    def run(self, stages, *others):
        for _ in range(stages):
            if self.sharing.able:
                self.step(*others)
            others = ()
        return self.done

    def step(self, *others):
        swap = self.sharing.swap
        if others:
            self.send = after(self.send, *others)
        send = self.send
        if self.stage < 3:
            got = swap(send, *(((0,),), ((1,), (2,)), ((2,), (1,)))[self.stage])
            half = 8 >> self.stage
            if self.stage < 2:
                self.keep, self.send = self.keep[0:half] + got[0:half], self.keep[half:] + got[half:]
                self.done = self.send
            else:
                parts = [self.keep[i] + got[i] for i in range(4)]
                self.keep, self.send = parts[0], parts[1:]
                self.done = self.send[2]
        elif self.stage == 3:
            got = [swap(send[0], (4,)), swap(send[1], (3,)), swap(send[2], (3, 4))]
            whole = (self.keep + got[0]) + (got[1] + got[2])
            for bit in self.sharing.other:
                whole = exchange(whole, self.sharing.sizes, [bit])
            self.done = self.send = whole
        elif self.stage == 4:
            self.done = self.send = jnp.stack([send, swap(send, (4,)), swap(send, (3,)), swap(send, (3, 4))])
        elif self.stage < 7:
            self.done = self.send = jnp.concatenate([send, swap(send, *(((2,), (1,)), ((1,), (2,)))[self.stage - 5])])
        else:
            self.keep, self.done = send, swap(send, (0,))
            self.send = self.done
        self.stage += 1

    def result(self):
        if not self.sharing.able:
            return [lax.psum(self.keep, AXES), lax.psum(self.send, AXES)]
        self.run(8 - self.stage)
        return [self.keep, self.send]


def shards(sizes, *arguments):
    clip_input, cotangent, clip_group, crop_sides = arguments[:4]
    kernels, bn_scale, bn_shift = arguments[4:10], arguments[10], arguments[11]
    w_single, w_reduce, w_spatial, w_squeeze, w_narrow, w_project = kernels
    _, frames, side, _, width = clip_input.shape
    lower, upper = Layer(frames, side, False), Layer(frames // 2, side // 2, True)
    where = [clip_group, crop_sides]
    merged = [w_spatial.reshape(2, 27, 160, 320), w_narrow.reshape(2, 27, 32, 128)]
    points = [
        layer_call(
            fit_points, i, [w_single, w_project, w_reduce, w_squeeze], [], [struct((832 + 64 * i, 768), LOW)], name="fit_points"
        )[0]
        for i in (0, 1)
    ]
    fitted = [
        layer_call(
            functools.partial(fit_convs, i),
            i,
            merged,
            [bn_scale, bn_shift],
            [struct((1536, 1024), LOW), struct((384, 384), LOW), struct((512, 2944), LOW), struct((128, 1152), LOW)]
            + [struct((2, 384), F32), struct((2, 896), F32)],
            name="fit_convs",
        )
        for i in (0, 1)
    ]
    pars = [item[4:6] for item in fitted]
    spatials = [(item[0], item[2]) for item in fitted]
    narrows = [(item[1], item[3]) for item in fitted]
    x = clip_input.reshape(lower.rows, width)
    cot = cotangent.reshape(upper.frames, upper.side * upper.side, width)
    cot = jnp.concatenate(
        [cot[..., 0:576], jnp.zeros(cot.shape[:2] + (64,), LOW), cot[..., 576:832]], axis=2
    )
    cot = jnp.pad(cot, ((0, 0), (0, upper.frame - upper.side * upper.side), (0, 0))).reshape(upper.rows, 896)

    def around(layer, tiles):
        return pltpu.VMEM((layer.frame + 2 * EDGE, 128 * tiles), F32)

    def forward(layer, za, suma, sumb, index):
        r = layer.rows
        return call(
            functools.partial(conv_forward, layer),
            where + [za, suma, pars[index][0], sumb, spatials[index][0], narrows[index][0]],
            [struct((r, 1536), LOW), struct((r, 384), LOW), struct((r, 512), F32), struct((2, 896), F32)],
            [around(layer, 3), pltpu.VMEM((r, 256), F32)],
            flops=2 * r * 27 * 160 * 320,
            name="conv_forward",
        )

    def unit_back(layer, gu, zb, zc, suma, sums, back, index):
        r = layer.rows
        return call(
            functools.partial(unit_backward, layer),
            where + [gu, zb, zc, suma, sums, back, pars[index][1]],
            [struct((r, 384), LOW), struct((r, 1024), LOW), struct((r, 384), LOW)],
            [around(layer, 1), pltpu.VMEM((r, 128), F32)],
            name="unit_backward",
        )

    def conv_back(layer, three, thin3, za, suma, index):
        r = layer.rows
        return call(
            functools.partial(conv_backward, layer),
            where + [three, thin3, za, suma, pars[index][0], spatials[index][1], narrows[index][1]],
            [struct((r, 384), F32), struct((2, 384), F32)],
            [
                around(layer, 4),
                pltpu.VMEM((layer.frame, 2944), LOW),
                pltpu.VMEM((layer.frame, 1152), LOW),
                pltpu.VMEM((r, 256), F32),
                pltpu.VMEM((r, 128), F32),
            ],
            flops=2 * r * 27 * 160 * 320,
            name="conv_backward",
        )

    sharing = Sharing(sizes)
    me = sharing.me()

    def pieces(part):
        return [struct((16, PARTS[part][0], 128), F32)] * 2

    def weights(part, layer, *operands):
        body, scratch = [
            (first_weights, [(1440, 512)]),
            (other_weights, [(1440, 512), (384, 384), (832, 384)]),
            (last_weights, [(832, 256)]),
        ][part]
        made = call(
            body,
            [me, *operands],
            pieces(part),
            [pltpu.VMEM(shape, F32) for shape in scratch],
            scalars=1,
            flops=2 * layer.rows * 16 * PARTS[part][0] * 256,
            name=body.__name__,
        )
        return sharing.chain(*made)

    r0, r1 = lower.rows, upper.rows
    za, suma = call(
        functools.partial(first_a, lower), where + [x, points[0]],
        [struct((r0, 384), F32), struct((3, 384), F32)], flops=2 * r0 * 832 * 384, name="first_a",
    )
    suma = sum_all(suma, sizes)
    zb, sumb = call(
        functools.partial(first_b, lower), where + [x, points[0]],
        [struct((r0, 384), F32), struct((2, 384), F32)], [around(lower, 1)], flops=2 * r0 * 832 * 384, name="first_b",
    )
    wide, thin, zc, sums = forward(lower, za, suma, sumb, 0)
    sums = sum_all(sums, sizes)
    q, za2, zb2, suma2, sumb2 = call(
        functools.partial(finish_lower, lower, upper),
        where + [zb, zc, suma, sums, pars[0][1], points[1]],
        [struct((r1, 896), LOW), struct((r1, 384), F32), struct((r1, 384), F32), struct((3, 384), F32), struct((2, 384), F32)],
        [around(upper, 1), pltpu.VMEM((lower.frame, 1792), LOW)],
        flops=2 * r1 * 832 * 768,
        name="finish_lower",
    )
    suma2 = sum_all(suma2, sizes)
    wide2, thin2, zc2, sums2 = forward(upper, za2, suma2, sumb2, 1)
    sums2 = sum_all(sums2, sizes)
    out, gu2, back2 = call(
        functools.partial(finish_upper, upper),
        where + [zb2, zc2, suma2, sums2, pars[1][1], cot],
        [struct((r1, 896), LOW), struct((r1, 896), F32), struct((2, 896), F32)],
        name="finish_upper",
    )
    back2 = sum_all(back2, sizes)
    dzb2, three2, thin32 = unit_back(upper, gu2, zb2, zc2, suma2, sums2, back2, 1)
    gua2, backa2 = conv_back(upper, three2, thin32, za2, suma2, 1)
    backa2 = sum_all(backa2, sizes)
    chains2 = [weights(0, upper, wide2, three2), weights(1, upper, wide2, three2, thin2, thin32, q, dzb2)]
    dza2, gu, back = call(
        functools.partial(join_blocks, upper, lower),
        where + [gua2, za2, suma2, backa2, pars[1][0], dzb2, points[1], zb, zc, suma, sums, pars[0][1]],
        [struct((r1, 384), LOW), struct((r0, 896), F32), struct((2, 896), F32)],
        [pltpu.VMEM((lower.frame, 896), F32)],
        flops=2 * r1 * 832 * 768,
        name="join_blocks",
    )
    back = sum_all(back, sizes)
    chains2.append(weights(2, upper, q, dza2))
    gu = after(gu, *[chain.run(2) for chain in chains2[0:2]])
    dzb, three, thin3 = unit_back(lower, gu, zb, zc, suma, sums, back, 0)
    chains = [weights(0, lower, wide, three), weights(1, lower, wide, three, thin, thin3, x, dzb)]
    late = after(three, *[chain.run(1) for chain in chains2[0:2]])
    gua, backa = conv_back(lower, late, thin3, za, suma, 0)
    backa = sum_all(backa, sizes)
    gua = after(gua, *[chain.run(2) for chain in chains2[0:2]])
    dza, da = call(
        functools.partial(last_back, lower),
        where + [gua, za, suma, backa, pars[0][0], dzb, points[0]],
        [struct((r0, 384), LOW), struct((r0, 832), LOW)],
        flops=2 * r0 * 832 * 768,
        name="last_back",
    )
    chains.append(weights(2, lower, x, dza))
    joined = assemble_call(1, me, sum((chain.result() for chain in chains2), []), None)
    joined = assemble_call(0, me, sum((chain.result() for chain in chains), []), joined)
    joined = [value.reshape(kernel.shape) for value, kernel in zip(joined, kernels)]
    both = jnp.stack([unfit_vectors(backa, back), unfit_vectors(backa2, back2)])
    out = jnp.concatenate([out[:, 0:576], out[:, 640:896]], axis=1)
    out = out.reshape(upper.frames, upper.frame, width)[:, 0 : upper.side * upper.side]
    return (
        out.reshape(cotangent.shape),
        da.reshape(clip_input.shape),
        *joined,
        both[:, 1],
        both[:, 0],
    )


def solution(mesh):
    split = P(AXES, None, None, None, None)
    sizes = tuple(mesh.shape[axis] for axis in AXES)
    return jax.shard_map(
        functools.partial(shards, sizes),
        mesh=mesh,
        in_specs=(split, split, P(AXES)) + (P(),) * 9,
        out_specs=(split, split) + (P(),) * 8,
        check_vma=False,
    )
```

```python
import functools

import jax
import jax.numpy as jnp
from jax import lax
from jax.experimental import pallas as pl
from jax.experimental.pallas import tpu as pltpu
from jax.sharding import PartitionSpec as P

AXES = ("dp", "rep")
F32 = jnp.float32
LOW = jnp.bfloat16
EDGE = 32
TAPS = [(dh, dw) for dh in (-1, 0, 1) for dw in (-1, 0, 1)]
UNIT_TILES = [("b", 0), ("b", 1), ("c", 0), ("c", 1), ("c", 2), ("c", 3), ("b", 2)]
VMEM = pl.BlockSpec(memory_space=pltpu.VMEM)
SMEM = pl.BlockSpec(memory_space=pltpu.SMEM)
MIB = 1024 * 1024


def struct(shape, kind):
    return jax.ShapeDtypeStruct(shape, kind)


def scoped(scratch, room):
    total = 0
    for item in scratch:
        if isinstance(item, jax.core.ShapedArray) or hasattr(item, "shape"):
            shape = item.shape
            if len(shape) >= 2:
                size = -(-shape[-1] // 128) * 128 * -(-shape[-2] // 8) * 8 * jnp.dtype(item.dtype).itemsize
                for n in shape[:-2]:
                    size *= n
                total += size
    return total + room * MIB


def call(body, ins, outs, scratch=(), scalars=2, room=8, flops=0, name=None):
    return pl.pallas_call(
        body,
        out_shape=tuple(outs),
        in_specs=[SMEM] * scalars + [VMEM] * (len(ins) - scalars),
        out_specs=tuple([VMEM] * len(outs)),
        scratch_shapes=list(scratch),
        compiler_params=pltpu.CompilerParams(vmem_limit_bytes=scoped(scratch, room)),
        cost_estimate=pl.CostEstimate(
            flops=flops,
            bytes_accessed=sum(x.size * x.dtype.itemsize for x in ins),
            transcendentals=0,
        ),
        name=name,
    )(*ins)


def tile(index, width=1):
    return slice(index * 128, (index + width) * 128)


def lanes():
    return lax.broadcasted_iota(jnp.int32, (1, 128), 1)


def sigmoid(v):
    return 0.5 * jnp.tanh(0.5 * v) + 0.5


def places(frame, side):
    at = lax.broadcasted_iota(jnp.int32, (frame, 1), 0).astype(F32)
    row = jnp.floor((at + 0.5) * (1.0 / side))
    return row, at - row * side


def crop_mask(frame, side, crop):
    row, column = places(frame, side)
    return jnp.where((row < crop) & (column < crop), 1.0, 0.0).astype(F32)


def column_mask(frame, side, step):
    row, column = places(frame, side)
    inside = (column + step > -0.5) & (column + step < side - 0.5)
    return jnp.where(inside, 1.0, 0.0).astype(F32)


def crop_of(group_ref, sides_ref, halved):
    crop = sides_ref[group_ref[0]]
    if halved:
        crop = lax.shift_right_logical(crop, 1)
    return crop.astype(F32)


def moments(sums, count):
    mean = sums[0:1] / count
    square = sums[1:2] / count
    return mean, lax.rsqrt(square - mean * mean + 1e-05)


def back_terms(sums, count, gamma, inverse):
    scale = gamma * inverse
    return scale, scale * (sums[0:1] / count), scale * (sums[1:2] / count)


def add_sums(ref, at, first, second):
    ref[0:1, at] += jnp.sum(first, axis=0, keepdims=True)
    ref[1:2, at] += jnp.sum(second, axis=0, keepdims=True)


def neighbour_sum(values, around, frame, side, put):
    frames = len(values)
    left = column_mask(frame, side, -1)
    right = column_mask(frame, side, 1)
    for t in range(frames):
        total = values[t]
        if t > 0:
            total = total + values[t - 1]
        if t < frames - 1:
            total = total + values[t + 1]
        around[EDGE : EDGE + frame, tile(0)] = total
        total = (
            total
            + around[EDGE - side : EDGE - side + frame, tile(0)]
            + around[EDGE + side : EDGE + side + frame, tile(0)]
        )
        around[EDGE : EDGE + frame, tile(0)] = total
        total = (
            total
            + around[EDGE - 1 : EDGE - 1 + frame, tile(0)] * left
            + around[EDGE + 1 : EDGE + 1 + frame, tile(0)] * right
        )
        put(t, total * (1.0 / 27.0))


def clear_edges(around, frame):
    width = around.shape[1]
    around[0:EDGE, :] = jnp.zeros((EDGE, width), F32)
    around[EDGE + frame : 2 * EDGE + frame, :] = jnp.zeros((EDGE, width), F32)


def dot(a, b):
    return lax.dot_general(a, b, (((1,), (0,)), ((), ())), preferred_element_type=F32)


def dot_nt(a, b):
    return lax.dot_general(a, b, (((1,), (1,)), ((), ())), preferred_element_type=F32)


def dot_tn(a, b):
    return lax.dot_general(a, b, (((0,), (0,)), ((), ())), preferred_element_type=F32)


class Layer:
    def __init__(self, frames, side, halved):
        self.frames = frames
        self.side = side
        self.halved = halved
        self.frame = -(-side * side // 16) * 16
        self.rows = frames * self.frame

    def at(self, t):
        return slice(t * self.frame, (t + 1) * self.frame)


def point_a(layer, mask, x_ref, w_ref, za_ref, sums_ref):
    sums_ref[...] = jnp.zeros(sums_ref.shape, F32)
    for t in range(layer.frames):
        z = dot_nt(x_ref[layer.at(t), :], w_ref[...])
        za_ref[layer.at(t), :] = z
        for j in range(3):
            part = z[:, tile(j)] * mask
            add_sums(sums_ref, tile(j), part, part * z[:, tile(j)])
    cells = jnp.sum(mask, axis=0, keepdims=True) * layer.frames
    sums_ref[2:3, :] = jnp.broadcast_to(cells, (1, 384))


def point_b(layer, mask, x_ref, w_ref, zb_ref, sums_ref, around):
    sums_ref[...] = jnp.zeros(sums_ref.shape, F32)
    clear_edges(around, layer.frame)
    flat = []
    for t in range(layer.frames):
        z = dot(x_ref[layer.at(t), :], w_ref[...])
        zb_ref[layer.at(t), 0:256] = z[:, 0:256]
        zb_ref[layer.at(t), tile(2)] = z[:, tile(2)] * mask
        for j in range(2):
            part = z[:, tile(j)] * mask
            add_sums(sums_ref, tile(j), part, part * z[:, tile(j)])
    flat = [zb_ref[layer.at(t), tile(2)] for t in range(layer.frames)]

    def put(t, value):
        zb_ref[layer.at(t), tile(2)] = value
        part = value * mask
        add_sums(sums_ref, tile(2), part, part * value)

    neighbour_sum(flat, around, layer.frame, layer.side, put)


def first_a(layer, group_ref, sides_ref, x_ref, w_ref, za_ref, sums_ref):
    mask = crop_mask(layer.frame, layer.side, crop_of(group_ref, sides_ref, layer.halved))
    point_a(layer, mask, x_ref, w_ref, za_ref, sums_ref)


def first_b(layer, group_ref, sides_ref, x_ref, w_ref, zb_ref, sums_ref, around):
    mask = crop_mask(layer.frame, layer.side, crop_of(group_ref, sides_ref, layer.halved))
    point_b(layer, mask, x_ref, w_ref, zb_ref, sums_ref, around)


def conv_forward(
    layer, group_ref, sides_ref, za_ref, suma_ref, para_ref, sumb_ref, w_ref, wn_ref,
    wide_ref, thin_ref, zc_ref, sums_ref, around, rem,
):
    frames, frame, side = layer.frames, layer.frame, layer.side
    mask = crop_mask(frame, side, crop_of(group_ref, sides_ref, layer.halved))
    count = suma_ref[2:3, :]
    mean, inverse = moments(suma_ref, count)
    gain = para_ref[0:1, :] * inverse
    offset = para_ref[1:2, :] - mean * gain
    column = [column_mask(frame, side, dw) for dw in (-1, 0, 1)]
    part_of = lanes() // 32
    clear_edges(around, frame)
    for t in range(frames):
        rows = layer.at(t)
        for j in range(3):
            u = za_ref[rows, tile(j)] * gain[:, tile(j)] + offset[:, tile(j)]
            around[EDGE : EDGE + frame, tile(j)] = u * sigmoid(u) * mask
        mixed = {1: [None] * 3, 2: [None] * 3}
        for k, (dh, dw) in enumerate(TAPS):
            start = EDGE + dh * side + dw
            shifted = around[start : start + frame, tile(0)]
            if dw:
                shifted = shifted * column[dw + 1]
            wide_ref[rows, tile(k)] = shifted.astype(LOW)
            for j in (1, 2):
                shifted = around[start : start + frame, tile(j)]
                if dw:
                    shifted = shifted * column[dw + 1]
                shifted = jnp.where(part_of == k % 4, shifted, 0.0)
                held = mixed[j][k // 4]
                mixed[j][k // 4] = shifted if held is None else held + shifted
        for g in range(3):
            wide_ref[rows, tile(9 + g)] = mixed[1][g].astype(LOW)
            thin_ref[rows, tile(g)] = mixed[2][g].astype(LOW)
    sums_ref[:, 0:384] = sumb_ref[...]
    sums_ref[:, 384:896] = jnp.zeros((2, 512), F32)
    zc_ref[...] = jnp.zeros(zc_ref.shape, F32)
    for t in range(frames):
        source = wide_ref[layer.at(t), :]
        thin = thin_ref[layer.at(t), :]
        for k in range(3):
            to = t + 1 - k
            if 0 <= to < frames:
                rows = layer.at(to)
                zc_ref[rows, 0:256] += dot(source, w_ref[:, k * 256 : (k + 1) * 256])
                zc_ref[rows, tile(3)] += dot(thin, wn_ref[:, tile(k)])
        rem[layer.at(t), :] = dot(source, w_ref[:, 768:1024])
    for t in range(frames):
        rows = layer.at(t)
        total = pltpu.roll(rem[rows, 0:128], 64, 1)
        if t > 0:
            total = total + rem[layer.at(t - 1), 0:128]
        if t < frames - 1:
            total = total + rem[layer.at(t + 1), 128:256]
        zc_ref[rows, tile(2)] = jnp.where(lanes() < 64, total, 0.0)
        for j in range(4):
            z = zc_ref[rows, tile(j)]
            part = z * mask
            add_sums(sums_ref, tile(3 + j), part, part * z)


class Norms:
    def __init__(self, sums_ref, par_ref, count):
        mean, inverse = moments(sums_ref, count)
        self.mean, self.inverse = mean, inverse
        self.gamma, self.beta = par_ref[0:1, :], par_ref[1:2, :]

    def lane(self, kind, j):
        return tile(j if kind == "b" else 3 + j)

    def normed(self, z, at):
        return (z - self.mean[:, at]) * self.inverse[:, at]

    def shifted(self, n, at):
        return self.gamma[:, at] * n + self.beta[:, at]


def finish_lower(
    lower, upper, group_ref, sides_ref, zb_ref, zc_ref, suma_ref, sums_ref, par_ref, wa_ref, wb_ref,
    q_ref, za2_ref, zb2_ref, suma2_ref, sumb2_ref, around, y_ref,
):
    crop = crop_of(group_ref, sides_ref, False)
    mask = crop_mask(lower.frame, lower.side, crop)
    norms = Norms(sums_ref, par_ref, suma_ref[2:3, 0:1])
    pick = pair_matrix(upper, lower)
    for t in range(upper.frames):
        for index, (kind, j) in enumerate(UNIT_TILES):
            at = norms.lane(kind, j)
            z_ref = zb_ref if kind == "b" else zc_ref
            total = None
            for source in (2 * t, 2 * t + 1):
                u = norms.shifted(norms.normed(z_ref[lower.at(source), tile(j)], at), at)
                out = u * sigmoid(u) * mask
                total = out if total is None else total + out
            high = total.astype(LOW)
            y_ref[:, tile(index)] = high
            y_ref[:, tile(7 + index)] = (total - high.astype(F32)).astype(LOW)
        both = dot(pick, y_ref[...])
        q_ref[upper.at(t), :] = (both[:, 0:896] + both[:, 896:1792]).astype(LOW)
    small = crop_mask(upper.frame, upper.side, crop_of(group_ref, sides_ref, True))
    point_a(upper, small, q_ref, wa_ref, za2_ref, suma2_ref)
    point_b(upper, small, q_ref, wb_ref, zb2_ref, sumb2_ref, around)


def pair_matrix(upper, lower):
    at = lax.broadcasted_iota(jnp.int32, (upper.frame, lower.frame), 1).astype(F32)
    row = jnp.floor((at + 0.5) * (1.0 / lower.side))
    column = at - row * lower.side
    group = jnp.floor(row * 0.5 + 0.25) * upper.side + jnp.floor(column * 0.5 + 0.25)
    mine = lax.broadcasted_iota(jnp.int32, (upper.frame, lower.frame), 0).astype(F32)
    return jnp.where(jnp.abs(group - mine) < 0.5, 0.125, 0.0).astype(LOW)


def spread_matrix(upper, lower):
    at = lax.broadcasted_iota(jnp.int32, (lower.frame, upper.frame), 0).astype(F32)
    row = jnp.floor((at + 0.5) * (1.0 / lower.side))
    column = at - row * lower.side
    group = jnp.floor(row * 0.5 + 0.25) * upper.side + jnp.floor(column * 0.5 + 0.25)
    mine = lax.broadcasted_iota(jnp.int32, (lower.frame, upper.frame), 1).astype(F32)
    return jnp.where(jnp.abs(group - mine) < 0.5, 0.125, 0.0).astype(LOW)


def finish_upper(
    layer, group_ref, sides_ref, zb_ref, zc_ref, suma_ref, sums_ref, par_ref, cot_ref,
    out_ref, gu_ref, back_ref,
):
    mask = crop_mask(layer.frame, layer.side, crop_of(group_ref, sides_ref, layer.halved))
    norms = Norms(sums_ref, par_ref, suma_ref[2:3, 0:1])
    back_ref[...] = jnp.zeros(back_ref.shape, F32)
    for t in range(layer.frames):
        rows = layer.at(t)
        for index, (kind, j) in enumerate(UNIT_TILES):
            at = norms.lane(kind, j)
            z_ref = zb_ref if kind == "b" else zc_ref
            n = norms.normed(z_ref[rows, tile(j)], at)
            u = norms.shifted(n, at)
            s = sigmoid(u)
            out_ref[rows, tile(index)] = (u * s * mask).astype(LOW)
            gu = cot_ref[rows, tile(index)].astype(F32) * mask * (s * (1.0 + u * (1.0 - s)))
            gu_ref[rows, tile(index)] = gu
            add_sums(back_ref, at, gu, gu * n)


def unit_backward(
    layer, group_ref, sides_ref, gu_ref, zb_ref, zc_ref, suma_ref, sums_ref, back_ref, par_ref,
    dzb_ref, three_ref, thin3_ref, around, flat,
):
    frames, frame, side = layer.frames, layer.frame, layer.side
    mask = crop_mask(frame, side, crop_of(group_ref, sides_ref, layer.halved))
    count = suma_ref[2:3, 0:1]
    norms = Norms(sums_ref, par_ref, count)
    c0, c1, c2 = back_terms(back_ref, count, norms.gamma, norms.inverse)
    low_half = lanes() < 64

    def dz_of(t, index):
        kind, j = UNIT_TILES[index]
        at = norms.lane(kind, j)
        z_ref = zb_ref if kind == "b" else zc_ref
        rows = layer.at(t)
        n = norms.normed(z_ref[rows, tile(j)], at)
        return (gu_ref[rows, tile(index)] * c0[:, at] - c1[:, at] - n * c2[:, at]) * mask

    clear_edges(around, frame)
    for t in range(frames):
        for index in (0, 1):
            dzb_ref[layer.at(t), tile(index)] = dz_of(t, index).astype(LOW)
        flat[layer.at(t), :] = dz_of(t, 6)

    def put(t, value):
        dzb_ref[layer.at(t), tile(2)] = (value * mask).astype(LOW)

    neighbour_sum([flat[layer.at(t), :] for t in range(frames)], around, frame, side, put)
    for t in range(frames):
        flat[layer.at(t), :] = jnp.where(low_half, dz_of(t, 4), 0.0)
    empty = jnp.zeros((frame, 128), LOW)
    for t in range(frames):
        parts = [dz_of(t, index).astype(LOW) for index in (2, 3, 5)]
        for k in range(3):
            to = t - 1 + k
            if 0 <= to < frames:
                rows = layer.at(to)
                three_ref[rows, tile(2 * k)] = parts[0]
                three_ref[rows, tile(2 * k + 1)] = parts[1]
                thin3_ref[rows, tile(k)] = parts[2]
        rest = pltpu.roll(flat[layer.at(t), :], 64, 1)
        if t < frames - 1:
            rest = rest + flat[layer.at(t + 1), :]
        three_ref[layer.at(t), tile(6)] = rest.astype(LOW)
        three_ref[layer.at(t), tile(7)] = flat[layer.at(t - 1), :].astype(LOW) if t else empty
    for rows, k in ((layer.at(0), 2), (layer.at(frames - 1), 0)):
        three_ref[rows, tile(2 * k)] = empty
        three_ref[rows, tile(2 * k + 1)] = empty
        thin3_ref[rows, tile(k)] = empty


def conv_backward(
    layer, group_ref, sides_ref, three_ref, thin3_ref, za_ref, suma_ref, para_ref, wt_ref, wnt_ref,
    gua_ref, backa_ref, around, shifts, thins, rem, main,
):
    frames, frame, side = layer.frames, layer.frame, layer.side
    mask = crop_mask(frame, side, crop_of(group_ref, sides_ref, layer.halved))
    column = [column_mask(frame, side, dw) for dw in (-1, 0, 1)]
    low_half = lanes() < 64
    first_part = lanes() < 32
    clear_edges(around, frame)
    main[...] = jnp.zeros(main.shape, F32)
    rem[...] = jnp.zeros(rem.shape, F32)
    for t in range(frames):
        rows = layer.at(t)
        rest = jnp.where(low_half, 0.0, three_ref[rows, tile(6)].astype(F32))
        parts = [
            three_ref[rows, tile(2)].astype(F32),
            three_ref[rows, tile(3)].astype(F32),
            rest + pltpu.roll(rest, 64, 1),
            thin3_ref[rows, tile(1)].astype(F32),
        ]
        for j in range(4):
            around[EDGE : EDGE + frame, tile(j)] = parts[j]
        mixed = [None] * 5
        for k, (dh, dw) in enumerate(TAPS):
            start = EDGE - dh * side - dw
            for j in range(4):
                shifted = around[start : start + frame, tile(j)]
                if dw:
                    shifted = shifted * column[1 - dw]
                if j < 2:
                    shifts[:, tile(2 * k + j)] = shifted.astype(LOW)
                elif j == 3:
                    thins[:, tile(k)] = shifted.astype(LOW)
                else:
                    shifted = jnp.where(low_half if k % 2 == 0 else ~low_half, shifted, 0.0)
                    held = mixed[k // 2]
                    mixed[k // 2] = shifted if held is None else held + shifted
        for g in range(5):
            shifts[:, tile(18 + g)] = mixed[g].astype(LOW)
        product = dot_nt(shifts[...], wt_ref[...])
        thin = dot_nt(thins[...], wnt_ref[...])
        for k in range(3):
            to = t - 1 + k
            if 0 <= to < frames:
                rows = layer.at(to)
                main[rows, :] += product[:, tile(k)]
                turn = (128 - 32 * k) % 128
                last = product[:, tile(3)]
                rem[rows, 0:128] += last if turn == 0 else pltpu.roll(last, turn, 1)
                rem[rows, 128:256] += thin if turn == 0 else pltpu.roll(thin, turn, 1)
    mean, inverse = moments(suma_ref, suma_ref[2:3, :])
    backa_ref[...] = jnp.zeros(backa_ref.shape, F32)
    for t in range(frames):
        rows = layer.at(t)
        for j in range(3):
            grad = main[rows, :] if j == 0 else rem[rows, tile(j - 1)]
            n = (za_ref[rows, tile(j)] - mean[:, tile(j)]) * inverse[:, tile(j)]
            u = para_ref[0:1, tile(j)] * n + para_ref[1:2, tile(j)]
            s = sigmoid(u)
            gu = grad * mask * (s * (1.0 + u * (1.0 - s)))
            if j:
                gu = jnp.where(first_part, gu, 0.0)
            gua_ref[rows, tile(j)] = gu
            add_sums(backa_ref, tile(j), gu, gu * n)


def point_back(layer, mask, gua_ref, za_ref, suma_ref, backa_ref, para_ref, dza_ref):
    count = suma_ref[2:3, :]
    mean, inverse = moments(suma_ref, count)
    c0, c1, c2 = back_terms(backa_ref, count, para_ref[0:1, :], inverse)
    for t in range(layer.frames):
        rows = layer.at(t)
        for j in range(3):
            at = tile(j)
            n = (za_ref[rows, at] - mean[:, at]) * inverse[:, at]
            dz = (gua_ref[rows, at] * c0[:, at] - c1[:, at] - n * c2[:, at]) * mask
            if j:
                dz = jnp.where(lanes() < 32, dz, 0.0)
            dza_ref[rows, at] = dz.astype(LOW)


def join_blocks(
    upper, lower, group_ref, sides_ref, gua_ref, za_ref, suma_ref, backa_ref, para_ref, dzb_ref, wa_ref, wb_ref,
    zb_ref, zc_ref, suma1_ref, sums1_ref, par1_ref, dza_ref, gu_ref, back_ref, wide,
):
    small = crop_mask(upper.frame, upper.side, crop_of(group_ref, sides_ref, True))
    point_back(upper, small, gua_ref, za_ref, suma_ref, backa_ref, para_ref, dza_ref)
    mask = crop_mask(lower.frame, lower.side, crop_of(group_ref, sides_ref, False))
    norms = Norms(sums1_ref, par1_ref, suma1_ref[2:3, 0:1])
    back_ref[...] = jnp.zeros(back_ref.shape, F32)
    pick = spread_matrix(upper, lower)
    for t in range(upper.frames):
        rows = upper.at(t)
        dq = dot_nt(dzb_ref[rows, :], wb_ref[...]) + dot(dza_ref[rows, :], wa_ref[...])
        high = dq.astype(LOW)
        rest = (dq - high.astype(F32)).astype(LOW)
        wide[...] = dot(pick, high) + dot(pick, rest)
        for source in (2 * t, 2 * t + 1):
            at_rows = lower.at(source)
            for index, (kind, j) in enumerate(UNIT_TILES):
                at = norms.lane(kind, j)
                z_ref = zb_ref if kind == "b" else zc_ref
                n = norms.normed(z_ref[at_rows, tile(j)], at)
                u = norms.shifted(n, at)
                s = sigmoid(u)
                gu = wide[:, tile(index)] * mask * (s * (1.0 + u * (1.0 - s)))
                gu_ref[at_rows, tile(index)] = gu
                add_sums(back_ref, at, gu, gu * n)


def last_back(
    layer, group_ref, sides_ref, gua_ref, za_ref, suma_ref, backa_ref, para_ref, dzb_ref, wa_ref, wb_ref, dza_ref, grad_ref,
):
    mask = crop_mask(layer.frame, layer.side, crop_of(group_ref, sides_ref, layer.halved))
    point_back(layer, mask, gua_ref, za_ref, suma_ref, backa_ref, para_ref, dza_ref)
    for t in range(layer.frames):
        rows = layer.at(t)
        total = dot_nt(dzb_ref[rows, :], wb_ref[...]) + dot(dza_ref[rows, :], wa_ref[...])
        grad_ref[rows, :] = (total * mask).astype(LOW)


def place(me, pair, core):
    bits = lax.shift_right_logical(me, 1) ^ pair
    x, y = bits & 1, lax.shift_right_logical(bits, 1) & 1
    near, far = lax.shift_right_logical(bits, 2) & 1, lax.shift_right_logical(bits, 3) & 1
    first = x + core * (y - x)
    second = y + core * (x - y)
    return first * 8 + second * 4 + near * 2 + far


def put_pair(me, keep_ref, send_ref, pair, rows, even, odd):
    core = me & 1
    mine = core == 0
    keep_ref[place(me, pair, core), rows, :] = jnp.where(mine, even, odd)
    send_ref[place(me, pair, 1 - core), rows, :] = jnp.where(mine, odd, even)


def get_pair(me, own_ref, other_ref, pair, rows):
    core = me & 1
    mine = core == 0
    own = own_ref[place(me, pair, core), rows, :]
    other = other_ref[place(me, pair, 1 - core), rows, :]
    return jnp.where(mine, own, other), jnp.where(mine, other, own)


def segments(blocks):
    rows = -(-sum(length for _, length in blocks) // 256) * 8
    pieces, piece, room = [], [], rows
    for name, length in blocks:
        at = 0
        while at < length:
            take = min(room, length - at)
            piece.append((name, at, at + take, rows - room))
            at += take
            room -= take
            if not room:
                pieces.append(piece)
                piece, room = [], rows
    if piece:
        pieces.append(piece)
    return rows, pieces + [[]] * (32 - len(pieces))


def wide(layer, *tiles):
    return [(("wide", j, layer), 1440) for j in tiles]


def point_and_thin(layer):
    return [(("point", j, layer), 832) for j in range(3)] + [(("thin", j, layer), 288) for j in range(3)]


def last(layer):
    return [(("last", j, layer), 192) for j in range(7)]


PARTS = [
    segments(wide(1, *range(8)) + point_and_thin(1)),
    segments(wide(0, 0, 1, 2, 3, 6) + last(1)),
    segments(wide(0, 4, 5, 7) + point_and_thin(0)),
    segments(last(0)),
]


def joined_part(first, second):
    rows = first[0]
    pieces = [a + [(name, low, end, row + rows) for name, low, end, row in b] for a, b in zip(first[1], second[1])]
    return rows + second[0], pieces


def piece_value(piece, rows, read):
    parts = [read(name, first, end) for name, first, end, _ in piece]
    filled = sum(end - first for _, first, end, _ in piece)
    if filled < rows:
        parts.append(jnp.zeros((rows - filled, 128), F32))
    return parts[0] if len(parts) == 1 else jnp.concatenate(parts, axis=0)


def put_pieces(me, keep_ref, send_ref, part, read):
    rows, pieces = part
    for pair in range(16):
        even, odd = (piece_value(pieces[2 * pair + i], rows, read) for i in (0, 1))
        put_pair(me, keep_ref, send_ref, pair, slice(0, rows), even, odd)


def without_gap(ref, grad):
    if grad.shape[0] == 896:
        ref[0:576, :] = grad[0:576]
        ref[576:832, :] = grad[640:896]
    else:
        ref[...] = grad


def weights(part, columns, kinds, me_ref, *refs):
    refs = list(refs)
    read_from = {}
    operands = [refs.pop(0) for _ in range({"w": 2, "o": 4, "l": 2}[kinds[0]] + (0 if len(kinds) == 1 else {"o": 4, "l": 2}[kinds[1]]))]
    keep_ref, send_ref = refs.pop(0), refs.pop(0)
    for kind in kinds:
        if kind == "w":
            wide_ref, three_ref = operands.pop(0), operands.pop(0)
            grad = refs.pop(0)
            at = 0
            for first, count in columns:
                grad[:, tile(at, count)] = dot_tn(wide_ref[:, 0:1440], three_ref[:, tile(first, count)])
                for j in range(count):
                    read_from["wide", first + j] = (grad, at + j)
                at += count
        elif kind == "o":
            thin_ref, thin3_ref, x_ref, dzb_ref = (operands.pop(0) for _ in range(4))
            thin_grad, point_grad = refs.pop(0), refs.pop(0)
            thin_grad[...] = dot_tn(thin_ref[...], thin3_ref[...])
            without_gap(point_grad, dot_tn(x_ref[...], dzb_ref[...]))
            for j in range(3):
                read_from["point", j] = (point_grad, j)
                read_from["thin", j] = (thin_grad, j)
        else:
            dza_ref, x_ref = operands.pop(0), operands.pop(0)
            last_grad = refs.pop(0)
            grad = dot_tn(dza_ref[...], x_ref[...])
            if grad.shape[1] == 896:
                grad = close_gap(grad)
            width = grad.shape[1]
            last_grad[0:160, 0:width] = grad[0:160]
            last_grad[160:192, 0:width] = grad[256:288]
            if width < 896:
                last_grad[:, width:896] = jnp.zeros((192, 896 - width), F32)
            for j in range(7):
                read_from["last", j] = (last_grad, j)

    def read(name, first, end):
        ref, j = read_from[name[0:2]]
        return ref[first:end, tile(j)]

    put_pieces(me_ref[0], keep_ref, send_ref, part, read)


OUT_SHAPES = [(832, 256), (160, 832), (27, 160, 320), (32, 832), (27, 32, 128), (832, 128)]
SINGLE, REDUCE, SPATIAL, SQUEEZE, NARROW, PROJECT = range(6)


def assemble(sources, targets, aliased, me_ref, *refs):
    me = me_ref[0]
    many = sum(2 if relative else 1 for _, relative in sources)
    arrived, refs = list(refs[0:many]), refs[many + (6 if aliased else 0) :]
    outs, stages, sems = refs[0:6], refs[6 : 6 + len(targets)], refs[6 + len(targets)]
    stage = {(which, block): (ref, first) for (which, block, first, _), ref in zip(targets, stages)}

    def put_wide(block, k, lanes_at, first, value):
        ref, offset = stage[SPATIAL, block]
        done = 0
        while done < value.shape[0]:
            row = first + done
            if row < 1152:
                tap, channel = row // 128, row % 128
                take = min(128 - channel, value.shape[0] - done)
            else:
                tap, channel = (row - 1152) // 32, 128 + (row - 1152) % 32
                take = min(160 - channel, value.shape[0] - done)
            ref[k * 9 + tap - offset, channel : channel + take, lanes_at] = value[done : done + take]
            done += take

    def put(name, first, end, value):
        kind, j, block = name
        if kind == "wide":
            if j < 6:
                put_wide(block, j // 2, tile(j % 2), first, value)
            elif j == 6:
                put_wide(block, 0, slice(256, 320), first, value[:, 0:64])
                put_wide(block, 1, slice(256, 320), first, pltpu.roll(value, 64, 1)[:, 0:64])
            else:
                put_wide(block, 2, slice(256, 320), first, value[:, 0:64])
        elif kind == "point":
            if j < 2:
                stage[SINGLE, block][0][first:end, tile(j)] = value
            else:
                stage[PROJECT, block][0][first:end, :] = value
        elif kind == "thin":
            done = 0
            while done < end - first:
                tap, channel = (first + done) // 32, (first + done) % 32
                take = min(32 - channel, end - first - done)
                stage[NARROW, block][0][j * 9 + tap, channel : channel + take, :] = value[done : done + take]
                done += take
        else:
            lanes_at = tile(j) if j < 6 else slice(768, 832)
            for which, low, high in ((REDUCE, 0, 160), (SQUEEZE, 160, 192)):
                begin, stop = max(first, low), min(end, high)
                if begin < stop:
                    part = value[begin - first : stop - first]
                    stage[which, block][0][begin - low : stop - low, lanes_at] = part if j < 6 else part[:, 0:64]

    for (rows, pieces), relative in sources:
        held = [arrived.pop(0) for _ in range(2 if relative else 1)]
        for pair in range(16):
            if relative:
                both = get_pair(me, *held, pair, slice(0, rows))
            else:
                both = [held[0][2 * pair + i] for i in (0, 1)]
            for i in (0, 1):
                for name, first, end, row in pieces[2 * pair + i]:
                    put(name, first, end, both[i][row : row + end - first])
    copies = []
    for i, ((which, block, first, count), ref) in enumerate(zip(targets, stages)):
        to = outs[which].at[block]
        if count < OUT_SHAPES[which][0]:
            to = to.at[pl.ds(first, count)]
        copies.append(pltpu.make_async_copy(ref, to, sems.at[i]))
        copies[-1].start()
    for copy in copies:
        copy.wait()


def assemble_call(me, sources, targets, outs):
    anywhere = pl.BlockSpec(memory_space=pl.ANY)
    arrays = sum((list(found) for _, found in sources), [])
    targets = [(which, block, first, count or OUT_SHAPES[which][0]) for which, block, first, count in targets]
    scratch = [pltpu.VMEM((count,) + OUT_SHAPES[which][1:], F32) for which, _, _, count in targets]
    return pl.pallas_call(
        functools.partial(assemble, [(part, len(found) == 2) for part, found in sources], targets, outs is not None),
        out_shape=tuple(struct((2,) + shape, F32) for shape in OUT_SHAPES),
        in_specs=[SMEM] + [VMEM] * len(arrays) + [anywhere] * (0 if outs is None else 6),
        out_specs=tuple([anywhere] * 6),
        scratch_shapes=scratch + [pltpu.SemaphoreType.DMA((len(targets),))],
        input_output_aliases={} if outs is None else {1 + len(arrays) + i: i for i in range(6)},
        compiler_params=pltpu.CompilerParams(vmem_limit_bytes=scoped(scratch, 8)),
        cost_estimate=pl.CostEstimate(
            flops=0, bytes_accessed=2 * scoped(scratch, 0), transcendentals=0
        ),
        name="assemble",
    )(me, *arrays, *([] if outs is None else outs))


def unfit_vectors(sums_a, sums):
    return jnp.concatenate(
        [sums[:, 0:256], sums_a[:, 0:160], sums[:, 384:704], sums_a[:, 256:288], sums[:, 768:896], sums[:, 256:384]], axis=1
    )


def open_gap(value):
    value = value.astype(F32)
    tiles = [value[:, tile(j)] for j in range(6)]
    tiles.append(jnp.concatenate([value[:, 768:832], jnp.zeros((value.shape[0], 64), F32)], axis=1))
    low_half = lanes() < 64
    turned = [pltpu.roll(part, 64, 1) for part in tiles[4:7]]
    tiles[4] = jnp.where(low_half, tiles[4], 0.0)
    tiles[5] = jnp.where(low_half, turned[0], turned[1])
    tiles[6] = jnp.where(low_half, turned[1], turned[2])
    return jnp.concatenate(tiles, axis=1).astype(LOW)


def close_gap(value):
    low_half = lanes() < 64
    tiles = [value[:, tile(j)] for j in range(7)]
    turned = [pltpu.roll(part, 64, 1) for part in tiles[5:7]]
    tiles[4] = jnp.where(low_half, tiles[4], turned[0])
    tiles[5] = jnp.where(low_half, turned[0], turned[1])
    tiles[6] = turned[1]
    return jnp.concatenate(tiles, axis=1)


def fit_points(single_ref, project_ref, reduce_ref, squeeze_ref, wa_ref, wb_ref):
    gap = wa_ref.shape[1] == 896
    if gap:
        spans = [(slice(0, 576), slice(0, 576)), (slice(640, 896), slice(576, 832))]
        wb_ref[576:640, :] = jnp.zeros((64, 384), LOW)
    else:
        spans = [(slice(0, 832), slice(0, 832))]
    for to, source in spans:
        wb_ref[to, 0:256] = single_ref[0, source, :]
        wb_ref[to, 256:384] = project_ref[0, source, :]
    reduce, squeeze = reduce_ref[0], squeeze_ref[0]
    if gap:
        reduce, squeeze = open_gap(reduce), open_gap(squeeze)
    wa_ref[0:128, :] = reduce[0:128]
    for i in range(4):
        wa_ref[128 + 32 * i : 160 + 32 * i, :] = reduce[128:160]
        wa_ref[256 + 32 * i : 288 + 32 * i, :] = squeeze


def pair_lanes(left, right):
    parts = [jnp.zeros((max(p.shape[0] for p in (left, right) if p is not None), 64), F32) if p is None else p.astype(F32) for p in (left, right)]
    return jnp.concatenate(parts, axis=1).astype(LOW)


def fit_convs(
    index, scale_ref, shift_ref, spatial_ref, narrow_ref, w_ref, wn_ref, wt_ref, wnt_ref, para_ref, par_ref
):
    spans = [(0, 128, 128 * tap, tap) for tap in range(9)] + [(128, 160, 1152 + 32 * tap, tap) for tap in range(9)]
    w_ref[1440:1536, :] = jnp.zeros((96, 1024), LOW)
    for first, end, row, tap in spans:
        rows = slice(row, row + end - first)
        rest = [spatial_ref[0, 9 * k + tap, first:end, 256:320] for k in range(3)]
        for k in range(3):
            w_ref[rows, k * 256 : (k + 1) * 256] = spatial_ref[0, 9 * k + tap, first:end, 0:256]
        w_ref[rows, 768:896] = pair_lanes(rest[0], rest[1])
        w_ref[rows, 896:1024] = pair_lanes(rest[2], None)
    wt_ref[480:512, :] = jnp.zeros((32, 2944), LOW)
    for k in range(3):
        for first, end, row in ((0, 128, 128 * k), (128, 160, 384 + 32 * k)):
            rows = slice(row, row + end - first)
            for tap in range(9):
                wt_ref[rows, tap * 256 : (tap + 1) * 256] = spatial_ref[0, 9 * k + tap, first:end, 0:256]
            for g in range(5):
                left = spatial_ref[0, 9 * k + 2 * g, first:end, 256:320]
                right = spatial_ref[0, 9 * k + 2 * g + 1, first:end, 256:320] if g < 4 else None
                wt_ref[rows, tile(18 + g)] = pair_lanes(left, right)
    wn_ref[288:384, :] = jnp.zeros((96, 384), LOW)
    wnt_ref[96:128, :] = jnp.zeros((32, 1152), LOW)
    for k in range(3):
        for tap in range(9):
            part = narrow_ref[0, 9 * k + tap]
            wn_ref[32 * tap : 32 * tap + 32, tile(k)] = part
            wnt_ref[32 * k : 32 * k + 32, tile(tap)] = part
    for row, ref in ((0, scale_ref), (1, shift_ref)):
        vector = ref[index : index + 1, :]
        rest = vector[:, 384:416]
        squeeze = vector[:, 736:768]
        para_ref[row : row + 1, 0:128] = vector[:, 256:384]
        para_ref[row : row + 1, 128:256] = jnp.concatenate([rest] * 4, axis=1)
        para_ref[row : row + 1, 256:384] = jnp.concatenate([squeeze] * 4, axis=1)
        par_ref[row : row + 1, 0:256] = vector[:, 0:256]
        par_ref[row : row + 1, 256:384] = vector[:, 896:1024]
        par_ref[row : row + 1, 384:768] = jnp.concatenate([vector[:, 416:736], jnp.zeros((1, 64), F32)], axis=1)
        par_ref[row : row + 1, 768:896] = vector[:, 768:896]


def fetch_block(body, index, held, made, *refs):
    whole, refs = refs[0 : len(refs) - 2 * held - made - 1], refs[len(refs) - 2 * held - made - 1 :]
    split, outs, parts, sems = refs[0:held], refs[held : held + made], refs[held + made : -1], refs[-1]
    copies = [pltpu.make_async_copy(ref.at[pl.ds(index, 1)], part, sems.at[i]) for i, (ref, part) in enumerate(zip(split, parts))]
    for copy in copies:
        copy.start()
    for copy in copies:
        copy.wait()
    body(*whole, *parts, *outs)


def layer_call(body, index, split, whole, outs, name=None):
    scratch = [pltpu.VMEM((1,) + x.shape[1:], x.dtype) for x in split]
    return pl.pallas_call(
        functools.partial(fetch_block, body, index, len(split), len(outs)),
        out_shape=tuple(outs),
        in_specs=[VMEM] * len(whole) + [pl.BlockSpec(memory_space=pl.ANY)] * len(split),
        out_specs=tuple([VMEM] * len(outs)),
        scratch_shapes=scratch + [pltpu.SemaphoreType.DMA((len(split),))],
        compiler_params=pltpu.CompilerParams(vmem_limit_bytes=scoped(scratch, 4)),
        cost_estimate=pl.CostEstimate(
            flops=0, bytes_accessed=2 * sum(x.size * x.dtype.itemsize for x in outs), transcendentals=0
        ),
        name=name,
    )(*whole, *split)


def exchange(value, sizes, bits):
    total = sizes[0] * sizes[1]

    def swap(mask):
        return lax.ppermute(value, AXES, [(i, i ^ mask) for i in range(total)])

    if len(bits) == 1:
        return value + swap(1 << bits[0])
    one, two = 1 << bits[0], 1 << bits[1]
    return (value + swap(one)) + (swap(two) + swap(one | two))


class Sum:
    def __init__(self, value, sizes):
        self.value, self.sizes, self.at = value, sizes, 0
        total = sizes[0] * sizes[1]
        bits = list(range(total.bit_length() - 1))
        self.stages = [bits[:1]] + [bits[at : at + 2] for at in range(1, len(bits), 2)]
        self.able = not (total & (total - 1))
        if not self.able:
            self.stages = []
            self.value = lax.psum(value, AXES)

    def step(self):
        if self.at < len(self.stages):
            self.value = exchange(self.value, self.sizes, self.stages[self.at])
            self.at += 1
        return self.value

    def result(self):
        while self.at < len(self.stages):
            self.step()
        return self.value


def sum_all(value, sizes):
    return Sum(value, sizes).result()


def meet(*holders):
    names = ("value",), ("keep", "send"), ("array",)
    found = [next(n for n in names if hasattr(holder, n[0])) for holder in holders]
    values = lax.optimization_barrier([[getattr(h, n) for n in ns] for h, ns in zip(holders, found)])
    for holder, ns, got in zip(holders, found, values):
        for n, value in zip(ns, got):
            setattr(holder, n, value)


class Held:
    def __init__(self, array):
        self.array = array


class Sharing:
    def __init__(self, sizes):
        dp, rep = sizes
        self.sizes = sizes
        self.total = dp * rep
        self.able = not (self.total & (self.total - 1)) and dp >= 8 and rep >= 4
        low = rep.bit_length() - 1
        self.bits = [0, 1, low, low + 1, low + 2]
        self.other = [bit for bit in range(self.total.bit_length() - 1) if bit not in self.bits]

    def me(self):
        if not self.able:
            return jnp.zeros((1,), jnp.int32)
        flat = lax.axis_index("dp") * self.sizes[1] + lax.axis_index("rep")
        index = sum(((flat >> bit) & 1) << i for i, bit in enumerate(self.bits))
        return index.reshape(1).astype(jnp.int32)

    def swap(self, value, even, odd=None):
        masks = [sum(1 << self.bits[i] for i in bits) for bits in (even, even if odd is None else odd)]
        return lax.ppermute(value, AXES, [(i, i ^ masks[i & 1]) for i in range(self.total)])

    def chain(self, keep, send):
        return Chain(self, keep, send)


class Chain:
    def __init__(self, sharing, keep, send, short=False):
        self.sharing, self.keep, self.send, self.stage = sharing, keep, send, 0
        self.short = short
        if not sharing.able:
            self.keep, self.send = lax.psum(keep, AXES), lax.psum(send, AXES)

    def step(self):
        if not self.sharing.able:
            return
        swap = self.sharing.swap
        send = self.send
        if self.short and self.stage == 1:
            kept = self.keep
            got = [swap(send[0:4], (1,), (2,)), swap(kept[4:8], (2,), (1,)), swap(send[4:8], (1, 2))]
            parts = [(kept[i] + got[0][i]) + (got[1][i] + got[2][i]) for i in range(4)]
            self.keep, self.send = parts[0], parts[1:]
            self.stage += 1
        elif self.short and self.stage == 5:
            self.send = jnp.concatenate([send, swap(send, (2,), (1,)), swap(send, (1,), (2,)), swap(send, (1, 2))])
            self.stage += 1
        elif self.stage < 3:
            got = swap(send, *(((0,),), ((1,), (2,)), ((2,), (1,)))[self.stage])
            half = 8 >> self.stage
            if self.stage < 2:
                self.keep, self.send = self.keep[0:half] + got[0:half], self.keep[half:] + got[half:]
            else:
                parts = [self.keep[i] + got[i] for i in range(4)]
                self.keep, self.send = parts[0], parts[1:]
        elif self.stage == 3:
            got = [swap(send[0], (4,)), swap(send[1], (3,)), swap(send[2], (3, 4))]
            whole = (self.keep + got[0]) + (got[1] + got[2])
            for bit in self.sharing.other:
                whole = exchange(whole, self.sharing.sizes, [bit])
            self.send = whole
            self.keep = ()
            self.whole = True
        elif self.stage == 4:
            self.send = jnp.stack([send, swap(send, (4,)), swap(send, (3,)), swap(send, (3, 4))])
        elif self.stage < 7:
            self.send = jnp.concatenate([send, swap(send, *(((2,), (1,)), ((1,), (2,)))[self.stage - 5])])
        else:
            self.keep, self.send = send, swap(send, (0,))
        self.stage += 1

    def join(self, other):
        if self.sharing.able:
            self.send = jnp.concatenate([self.send, other.send], axis=0)
        else:
            self.keep = jnp.concatenate([self.keep, other.keep], axis=1)
            self.send = jnp.concatenate([self.send, other.send], axis=1)

    def result(self):
        return [self.keep, self.send]


def shards(sizes, *arguments):
    clip_input, cotangent, clip_group, crop_sides = arguments[:4]
    kernels, bn_scale, bn_shift = arguments[4:10], arguments[10], arguments[11]
    w_single, w_reduce, w_spatial, w_squeeze, w_narrow, w_project = kernels
    _, frames, side, _, width = clip_input.shape
    lower, upper = Layer(frames, side, False), Layer(frames // 2, side // 2, True)
    where = [clip_group, crop_sides]
    merged = [w_spatial.reshape(2, 27, 160, 320), w_narrow.reshape(2, 27, 32, 128)]
    turned = [jnp.swapaxes(w_reduce, 1, 2), jnp.swapaxes(w_squeeze, 1, 2)]
    points = [
        layer_call(
            fit_points, i, [w_single, w_project] + turned, [],
            [struct((384, 832 + 64 * i), LOW), struct((832 + 64 * i, 384), LOW)], name="fit_points",
        )
        for i in (0, 1)
    ]
    fitted = [
        layer_call(
            functools.partial(fit_convs, i),
            i,
            merged,
            [bn_scale, bn_shift],
            [struct((1536, 1024), LOW), struct((384, 384), LOW), struct((512, 2944), LOW), struct((128, 1152), LOW)]
            + [struct((2, 384), F32), struct((2, 896), F32)],
            name="fit_convs",
        )
        for i in (0, 1)
    ]
    pars = [item[4:6] for item in fitted]
    spatials = [(item[0], item[2]) for item in fitted]
    narrows = [(item[1], item[3]) for item in fitted]
    def frames_first(value, layer):
        value = jnp.transpose(value, (0, 2, 3, 1, 4)).reshape(layer.side * layer.side, layer.frames, width)
        return jnp.transpose(value, (1, 0, 2))

    def frames_back(value, layer):
        value = jnp.transpose(value, (1, 0, 2)).reshape(1, layer.side, layer.side, layer.frames, width)
        return jnp.transpose(value, (0, 3, 1, 2, 4))

    x = frames_first(clip_input, lower).reshape(lower.rows, width)
    cot = frames_first(cotangent, upper)
    cot = jnp.concatenate(
        [cot[..., 0:576], jnp.zeros(cot.shape[:2] + (64,), LOW), cot[..., 576:832]], axis=2
    )
    cot = jnp.pad(cot, ((0, 0), (0, upper.frame - upper.side * upper.side), (0, 0))).reshape(upper.rows, 896)

    def around(layer, tiles):
        return pltpu.VMEM((layer.frame + 2 * EDGE, 128 * tiles), F32)

    def forward(layer, za, suma, sumb, index):
        r = layer.rows
        return call(
            functools.partial(conv_forward, layer),
            where + [za, suma, pars[index][0], sumb, spatials[index][0], narrows[index][0]],
            [struct((r, 1536), LOW), struct((r, 384), LOW), struct((r, 512), F32), struct((2, 896), F32)],
            [around(layer, 3), pltpu.VMEM((r, 256), F32)],
            flops=2 * r * 27 * 160 * 320,
            name="conv_forward",
        )

    def unit_back(layer, gu, zb, zc, suma, sums, back, index):
        r = layer.rows
        return call(
            functools.partial(unit_backward, layer),
            where + [gu, zb, zc, suma, sums, back, pars[index][1]],
            [struct((r, 384), LOW), struct((r, 1024), LOW), struct((r, 384), LOW)],
            [around(layer, 1), pltpu.VMEM((r, 128), F32)],
            name="unit_backward",
        )

    def conv_back(layer, three, thin3, za, suma, index):
        r = layer.rows
        return call(
            functools.partial(conv_backward, layer),
            where + [three, thin3, za, suma, pars[index][0], spatials[index][1], narrows[index][1]],
            [struct((r, 384), F32), struct((2, 384), F32)],
            [
                around(layer, 4),
                pltpu.VMEM((layer.frame, 2944), LOW),
                pltpu.VMEM((layer.frame, 1152), LOW),
                pltpu.VMEM((r, 256), F32),
                pltpu.VMEM((r, 128), F32),
            ],
            flops=2 * r * 27 * 160 * 320,
            name="conv_backward",
        )

    sharing = Sharing(sizes)
    me = sharing.me()

    def make_weights(index, columns, kinds, *operands, short=False):
        part = PARTS[index]
        scratch = []
        for kind in kinds:
            if kind == "w":
                scratch.append((1440, 128 * sum(count for _, count in columns)))
            elif kind == "o":
                scratch += [(384, 384), (832, 384)]
            else:
                scratch.append((192, 896))
        made = call(
            functools.partial(weights, part, columns, kinds),
            [me, *operands],
            [struct((16, part[0], 128), F32)] * 2,
            [pltpu.VMEM(shape, F32) for shape in scratch],
            scalars=1,
            flops=2 * operands[0].shape[0] * 32 * part[0] * 128,
            name="weights",
        )
        return Chain(sharing, *made, short=short)

    r0, r1 = lower.rows, upper.rows
    za, suma = call(
        functools.partial(first_a, lower), where + [x, points[0][0]],
        [struct((r0, 384), F32), struct((3, 384), F32)], flops=2 * r0 * 832 * 384, name="first_a",
    )
    suma = sum_all(suma, sizes)
    zb, sumb = call(
        functools.partial(first_b, lower), where + [x, points[0][1]],
        [struct((r0, 384), F32), struct((2, 384), F32)], [around(lower, 1)], flops=2 * r0 * 832 * 384, name="first_b",
    )
    wide, thin, zc, sums = forward(lower, za, suma, sumb, 0)
    sums = sum_all(sums, sizes)
    q, za2, zb2, suma2, sumb2 = call(
        functools.partial(finish_lower, lower, upper),
        where + [zb, zc, suma, sums, pars[0][1], *points[1]],
        [struct((r1, 896), LOW), struct((r1, 384), F32), struct((r1, 384), F32), struct((3, 384), F32), struct((2, 384), F32)],
        [around(upper, 1), pltpu.VMEM((lower.frame, 1792), LOW)],
        flops=2 * r1 * 832 * 768,
        name="finish_lower",
    )
    suma2 = sum_all(suma2, sizes)
    wide2, thin2, zc2, sums2 = forward(upper, za2, suma2, sumb2, 1)
    sums2 = sum_all(sums2, sizes)
    out, gu2, back2 = call(
        functools.partial(finish_upper, upper),
        where + [zb2, zc2, suma2, sums2, pars[1][1], cot],
        [struct((r1, 896), LOW), struct((r1, 896), F32), struct((2, 896), F32)],
        name="finish_upper",
    )
    back2 = sum_all(back2, sizes)
    dzb2, three2, thin32 = unit_back(upper, gu2, zb2, zc2, suma2, sums2, back2, 1)
    gua2, backa2 = conv_back(upper, three2, thin32, za2, suma2, 1)
    small = Sum(backa2, sizes)
    small.step()
    one = make_weights(0, [(0, 2), (2, 2), (4, 2), (6, 2)], "wo", wide2, three2, thin2, thin32, q, dzb2)
    meet(small, one)
    small.step()
    one.step()
    meet(small, one)
    backa2 = small.result()
    one.step()
    dza2, gu, back = call(
        functools.partial(join_blocks, upper, lower),
        where + [gua2, za2, suma2, backa2, pars[1][0], dzb2, *points[1], zb, zc, suma, sums, pars[0][1]],
        [struct((r1, 384), LOW), struct((r0, 896), F32), struct((2, 896), F32)],
        [pltpu.VMEM((lower.frame, 896), F32)],
        flops=2 * r1 * 832 * 768,
        name="join_blocks",
    )
    held = Held(sum_all(back, sizes))
    meet(held, one)
    back = held.array
    one.step()
    dzb, three, thin3 = unit_back(lower, gu, zb, zc, suma, sums, back, 0)
    two = make_weights(1, [(0, 2), (2, 2), (6, 1)], "wl", wide, three, dza2, q)
    held = Held(three)
    meet(one, two, held)
    one.step()
    two.step()
    two.step()
    gua, backa = conv_back(lower, held.array, thin3, za, suma, 0)
    held = Held(three), Held(backa)
    meet(two, *held)
    more = make_weights(2, [(4, 2), (7, 1)], "wo", wide, held[0].array, thin, thin3, x, dzb)
    meet(one, more)
    one.step()
    two.step()
    more.step()
    more.step()
    backa = sum_all(held[1].array, sizes)
    dza, da = call(
        functools.partial(last_back, lower),
        where + [gua, za, suma, backa, pars[0][0], dzb, *points[0]],
        [struct((r0, 384), LOW), struct((r0, 832), LOW)],
        flops=2 * r0 * 832 * 768,
        name="last_back",
    )
    final = make_weights(3, [], "l", dza, x, short=True)
    meet(one, two, more, final)
    one.step()
    two.step()
    more.step()
    final.step()
    final.step()
    da = Held(frames_back(da.reshape(lower.frames, lower.frame, width), lower))
    out = jnp.concatenate([out[:, 0:576], out[:, 640:896]], axis=1)
    out = out.reshape(upper.frames, upper.frame, width)[:, 0 : upper.side * upper.side]
    out = Held(frames_back(out, upper))
    meet(one, two, more, final, da, out)
    one.step()
    two.step()
    more.step()
    final.step()
    meet(one, two, more, final)
    more.join(final)
    one.step()
    two.step()
    two.step()
    more.step()
    meet(one, two, more)
    joined = Held(assemble_call(me, [(PARTS[0], one.result())], [(which, 1, 0, 0) for which in (SINGLE, SPATIAL, NARROW, PROJECT)], None))
    two.step()
    more.step()
    more.step()
    meet(two, more, joined)
    joined.array = assemble_call(
        me, [(PARTS[1], two.result())], [(SPATIAL, 0, 0, 18), (REDUCE, 1, 0, 0), (SQUEEZE, 1, 0, 0)], list(joined.array)
    )
    more.step()
    meet(more, joined)
    joined = list(joined.array)
    joined = list(assemble_call(
        me,
        [(joined_part(PARTS[2], PARTS[3]), more.result())],
        [(SPATIAL, 0, 18, 9)] + [(which, 0, 0, 0) for which in (SINGLE, REDUCE, SQUEEZE, NARROW, PROJECT)],
        joined,
    ))
    joined[REDUCE], joined[SQUEEZE] = (jnp.swapaxes(joined[which], 1, 2) for which in (REDUCE, SQUEEZE))
    joined = [value.reshape(kernel.shape) for value, kernel in zip(joined, kernels)]
    both = jnp.stack([unfit_vectors(backa, back), unfit_vectors(backa2, back2)])
    return (
        out.array,
        da.array,
        *joined,
        both[:, 1],
        both[:, 0],
    )


def solution(mesh):
    split = P(AXES, None, None, None, None)
    sizes = tuple(mesh.shape[axis] for axis in AXES)
    return jax.shard_map(
        functools.partial(shards, sizes),
        mesh=mesh,
        in_specs=(split, split, P(AXES)) + (P(),) * 9,
        out_specs=(split, split) + (P(),) * 8,
        check_vma=False,
    )
```

```python
import functools

import jax
import jax.numpy as jnp
from jax import lax
from jax.experimental import pallas as pl
from jax.experimental.pallas import tpu as pltpu
from jax.sharding import PartitionSpec as P

AXES = ("dp", "rep")
F32 = jnp.float32
LOW = jnp.bfloat16
EDGE = 32
TAPS = [(dh, dw) for dh in (-1, 0, 1) for dw in (-1, 0, 1)]
UNIT_TILES = [("b", 0), ("b", 1), ("c", 0), ("c", 1), ("c", 2), ("c", 3), ("b", 2)]
VMEM = pl.BlockSpec(memory_space=pltpu.VMEM)
SMEM = pl.BlockSpec(memory_space=pltpu.SMEM)
MIB = 1024 * 1024


def struct(shape, kind):
    return jax.ShapeDtypeStruct(shape, kind)


def scoped(scratch, room):
    total = 0
    for item in scratch:
        if isinstance(item, jax.core.ShapedArray) or hasattr(item, "shape"):
            shape = item.shape
            if len(shape) >= 2:
                size = -(-shape[-1] // 128) * 128 * -(-shape[-2] // 8) * 8 * jnp.dtype(item.dtype).itemsize
                for n in shape[:-2]:
                    size *= n
                total += size
    return total + room * MIB


def with_fetch(body, scalars, fetch, late, many_ins, many_outs, *refs):
    ins, outs = list(refs[0:many_ins]), refs[many_ins : many_ins + many_outs]
    scratch = list(refs[many_ins + many_outs :])
    sems = scratch.pop()
    moved = fetch + late
    parts = scratch[len(scratch) - len(moved) :]
    scratch = scratch[0 : len(scratch) - len(moved)]
    copies = [pltpu.make_async_copy(ins[i], part, sems.at[k]) for k, (i, part) in enumerate(zip(moved, parts))]
    for copy in copies:
        copy.start()
    for copy in copies[0 : len(fetch)]:
        copy.wait()
    for i, part in zip(moved, parts):
        ins[i] = part

    def ready():
        for copy in copies[len(fetch) :]:
            copy.wait()

    body(*ins, *outs, *scratch, **({"ready": ready} if late else {}))


def call(body, ins, outs, scratch=(), scalars=2, room=3, name=None, fetch=(), late=()):
    fetch, late, scratch = list(fetch), list(late), list(scratch)
    specs = [SMEM] * scalars + [VMEM] * (len(ins) - scalars)
    if fetch or late:
        body = functools.partial(with_fetch, body, scalars, fetch, late, len(ins), len(outs))
        for i in fetch + late:
            specs[i] = pl.BlockSpec(memory_space=pl.ANY)
            scratch.append(pltpu.VMEM(ins[i].shape, ins[i].dtype))
    limit = scoped(scratch, room)
    if fetch or late:
        scratch.append(pltpu.SemaphoreType.DMA((len(fetch) + len(late),)))
    return pl.pallas_call(
        body,
        out_shape=tuple(outs),
        in_specs=specs,
        out_specs=tuple([VMEM] * len(outs)),
        scratch_shapes=scratch,
        compiler_params=pltpu.CompilerParams(vmem_limit_bytes=limit),
        cost_estimate=pl.CostEstimate(flops=1, bytes_accessed=1, transcendentals=0),
        name=name,
    )(*ins)


def tile(index, width=1):
    return slice(index * 128, (index + width) * 128)


def lanes():
    return lax.broadcasted_iota(jnp.int32, (1, 128), 1)


def sigmoid(v):
    return 0.5 * jnp.tanh(0.5 * v) + 0.5


def places(frame, side):
    at = lax.broadcasted_iota(jnp.int32, (frame, 1), 0).astype(F32)
    row = jnp.floor((at + 0.5) * (1.0 / side))
    return row, at - row * side


def crop_mask(frame, side, crop):
    row, column = places(frame, side)
    return jnp.where((row < crop) & (column < crop), 1.0, 0.0).astype(F32)


def column_mask(frame, side, step):
    row, column = places(frame, side)
    inside = (column + step > -0.5) & (column + step < side - 0.5)
    return jnp.where(inside, 1.0, 0.0).astype(F32)


def crop_of(group_ref, sides_ref, halved):
    crop = sides_ref[group_ref[0]]
    if halved:
        crop = lax.shift_right_logical(crop, 1)
    return crop.astype(F32)


def moments(sums, count):
    mean = sums[0:1] / count
    square = sums[1:2] / count
    return mean, lax.rsqrt(square - mean * mean + 1e-05)


def back_terms(sums, count, gamma, inverse):
    scale = gamma * inverse
    return scale, scale * (sums[0:1] / count), scale * (sums[1:2] / count)


def add_sums(ref, at, first, second):
    ref[0:1, at] += jnp.sum(first, axis=0, keepdims=True)
    ref[1:2, at] += jnp.sum(second, axis=0, keepdims=True)


def neighbour_sum(values, around, frame, side, put):
    frames = len(values)
    left = column_mask(frame, side, -1)
    right = column_mask(frame, side, 1)
    for t in range(frames):
        total = values[t]
        if t > 0:
            total = total + values[t - 1]
        if t < frames - 1:
            total = total + values[t + 1]
        around[EDGE : EDGE + frame, tile(0)] = total
        total = (
            total
            + around[EDGE - side : EDGE - side + frame, tile(0)]
            + around[EDGE + side : EDGE + side + frame, tile(0)]
        )
        around[EDGE : EDGE + frame, tile(0)] = total
        total = (
            total
            + around[EDGE - 1 : EDGE - 1 + frame, tile(0)] * left
            + around[EDGE + 1 : EDGE + 1 + frame, tile(0)] * right
        )
        put(t, total * (1.0 / 27.0))


def clear_edges(around, frame):
    width = around.shape[1]
    around[0:EDGE, :] = jnp.zeros((EDGE, width), F32)
    around[EDGE + frame : 2 * EDGE + frame, :] = jnp.zeros((EDGE, width), F32)


def dot(a, b):
    return lax.dot_general(a, b, (((1,), (0,)), ((), ())), preferred_element_type=F32)


def dot_nt(a, b):
    return lax.dot_general(a, b, (((1,), (1,)), ((), ())), preferred_element_type=F32)


def dot_tn(a, b):
    return lax.dot_general(a, b, (((0,), (0,)), ((), ())), preferred_element_type=F32)


class Layer:
    def __init__(self, frames, side, halved):
        self.frames = frames
        self.side = side
        self.halved = halved
        self.frame = -(-side * side // 16) * 16
        self.rows = frames * self.frame

    def at(self, t):
        return slice(t * self.frame, (t + 1) * self.frame)


def point_a(layer, mask, x_ref, w_ref, za_ref, sums_ref):
    sums_ref[...] = jnp.zeros(sums_ref.shape, F32)
    for t in range(layer.frames):
        z = dot_nt(x_ref[layer.at(t), :], w_ref[...])
        za_ref[layer.at(t), :] = z
        for j in range(3):
            part = z[:, tile(j)] * mask
            add_sums(sums_ref, tile(j), part, part * z[:, tile(j)])
    cells = jnp.sum(mask, axis=0, keepdims=True) * layer.frames
    sums_ref[2:3, :] = jnp.broadcast_to(cells, (1, 384))


def point_b(layer, mask, x_ref, w_ref, zb_ref, sums_ref, around):
    sums_ref[...] = jnp.zeros(sums_ref.shape, F32)
    clear_edges(around, layer.frame)
    flat = []
    for t in range(layer.frames):
        z = dot(x_ref[layer.at(t), :], w_ref[...])
        zb_ref[layer.at(t), 0:256] = z[:, 0:256]
        zb_ref[layer.at(t), tile(2)] = z[:, tile(2)] * mask
        for j in range(2):
            part = z[:, tile(j)] * mask
            add_sums(sums_ref, tile(j), part, part * z[:, tile(j)])
    flat = [zb_ref[layer.at(t), tile(2)] for t in range(layer.frames)]

    def put(t, value):
        zb_ref[layer.at(t), tile(2)] = value
        part = value * mask
        add_sums(sums_ref, tile(2), part, part * value)

    neighbour_sum(flat, around, layer.frame, layer.side, put)


def first_a(layer, group_ref, sides_ref, x_ref, w_ref, za_ref, sums_ref):
    mask = crop_mask(layer.frame, layer.side, crop_of(group_ref, sides_ref, layer.halved))
    point_a(layer, mask, x_ref, w_ref, za_ref, sums_ref)


def first_b(layer, group_ref, sides_ref, x_ref, w_ref, zb_ref, sums_ref, around):
    mask = crop_mask(layer.frame, layer.side, crop_of(group_ref, sides_ref, layer.halved))
    point_b(layer, mask, x_ref, w_ref, zb_ref, sums_ref, around)


def conv_forward(
    layer, group_ref, sides_ref, za_ref, suma_ref, para_ref, sumb_ref, w_ref, wn_ref,
    wide_ref, thin_ref, zc_ref, sums_ref, around, rem,
):
    frames, frame, side = layer.frames, layer.frame, layer.side
    mask = crop_mask(frame, side, crop_of(group_ref, sides_ref, layer.halved))
    count = suma_ref[2:3, :]
    mean, inverse = moments(suma_ref, count)
    gain = para_ref[0:1, :] * inverse
    offset = para_ref[1:2, :] - mean * gain
    column = [column_mask(frame, side, dw) for dw in (-1, 0, 1)]
    part_of = lanes() // 32
    clear_edges(around, frame)
    for t in range(frames):
        rows = layer.at(t)
        for j in range(3):
            u = za_ref[rows, tile(j)] * gain[:, tile(j)] + offset[:, tile(j)]
            around[EDGE : EDGE + frame, tile(j)] = u * sigmoid(u) * mask
        mixed = {1: [None] * 3, 2: [None] * 3}
        for k, (dh, dw) in enumerate(TAPS):
            start = EDGE + dh * side + dw
            shifted = around[start : start + frame, tile(0)]
            if dw:
                shifted = shifted * column[dw + 1]
            wide_ref[rows, tile(k)] = shifted.astype(LOW)
            for j in (1, 2):
                shifted = around[start : start + frame, tile(j)]
                if dw:
                    shifted = shifted * column[dw + 1]
                shifted = jnp.where(part_of == k % 4, shifted, 0.0)
                held = mixed[j][k // 4]
                mixed[j][k // 4] = shifted if held is None else held + shifted
        for g in range(3):
            wide_ref[rows, tile(9 + g)] = mixed[1][g].astype(LOW)
            thin_ref[rows, tile(g)] = mixed[2][g].astype(LOW)
    sums_ref[:, 0:384] = sumb_ref[...]
    sums_ref[:, 384:896] = jnp.zeros((2, 512), F32)
    zc_ref[...] = jnp.zeros(zc_ref.shape, F32)
    for t in range(frames):
        source = wide_ref[layer.at(t), :]
        thin = thin_ref[layer.at(t), :]
        for k in range(3):
            to = t + 1 - k
            if 0 <= to < frames:
                rows = layer.at(to)
                zc_ref[rows, 0:256] += dot(source, w_ref[:, k * 256 : (k + 1) * 256])
                zc_ref[rows, tile(3)] += dot(thin, wn_ref[:, tile(k)])
        rem[layer.at(t), :] = dot(source, w_ref[:, 768:1024])
    for t in range(frames):
        rows = layer.at(t)
        total = pltpu.roll(rem[rows, 0:128], 64, 1)
        if t > 0:
            total = total + rem[layer.at(t - 1), 0:128]
        if t < frames - 1:
            total = total + rem[layer.at(t + 1), 128:256]
        zc_ref[rows, tile(2)] = jnp.where(lanes() < 64, total, 0.0)
        for j in range(4):
            z = zc_ref[rows, tile(j)]
            part = z * mask
            add_sums(sums_ref, tile(3 + j), part, part * z)


class Norms:
    def __init__(self, sums_ref, par_ref, count):
        mean, inverse = moments(sums_ref, count)
        self.mean, self.inverse = mean, inverse
        self.gamma, self.beta = par_ref[0:1, :], par_ref[1:2, :]

    def lane(self, kind, j):
        return tile(j if kind == "b" else 3 + j)

    def normed(self, z, at):
        return (z - self.mean[:, at]) * self.inverse[:, at]

    def shifted(self, n, at):
        return self.gamma[:, at] * n + self.beta[:, at]


def finish_lower(
    lower, upper, group_ref, sides_ref, zb_ref, zc_ref, suma_ref, sums_ref, par_ref, wa_ref, wb_ref,
    q_ref, za2_ref, zb2_ref, suma2_ref, sumb2_ref, around, y_ref,
):
    crop = crop_of(group_ref, sides_ref, False)
    mask = crop_mask(lower.frame, lower.side, crop)
    norms = Norms(sums_ref, par_ref, suma_ref[2:3, 0:1])
    pick = pair_matrix(upper, lower)
    for t in range(upper.frames):
        for index, (kind, j) in enumerate(UNIT_TILES):
            at = norms.lane(kind, j)
            z_ref = zb_ref if kind == "b" else zc_ref
            total = None
            for source in (2 * t, 2 * t + 1):
                u = norms.shifted(norms.normed(z_ref[lower.at(source), tile(j)], at), at)
                out = u * sigmoid(u) * mask
                total = out if total is None else total + out
            high = total.astype(LOW)
            y_ref[:, tile(index)] = high
            y_ref[:, tile(7 + index)] = (total - high.astype(F32)).astype(LOW)
        both = dot(pick, y_ref[...])
        q_ref[upper.at(t), :] = (both[:, 0:896] + both[:, 896:1792]).astype(LOW)
    small = crop_mask(upper.frame, upper.side, crop_of(group_ref, sides_ref, True))
    point_a(upper, small, q_ref, wa_ref, za2_ref, suma2_ref)
    point_b(upper, small, q_ref, wb_ref, zb2_ref, sumb2_ref, around)


def pair_matrix(upper, lower):
    at = lax.broadcasted_iota(jnp.int32, (upper.frame, lower.frame), 1).astype(F32)
    row = jnp.floor((at + 0.5) * (1.0 / lower.side))
    column = at - row * lower.side
    group = jnp.floor(row * 0.5 + 0.25) * upper.side + jnp.floor(column * 0.5 + 0.25)
    mine = lax.broadcasted_iota(jnp.int32, (upper.frame, lower.frame), 0).astype(F32)
    return jnp.where(jnp.abs(group - mine) < 0.5, 0.125, 0.0).astype(LOW)


def spread_matrix(upper, lower):
    at = lax.broadcasted_iota(jnp.int32, (lower.frame, upper.frame), 0).astype(F32)
    row = jnp.floor((at + 0.5) * (1.0 / lower.side))
    column = at - row * lower.side
    group = jnp.floor(row * 0.5 + 0.25) * upper.side + jnp.floor(column * 0.5 + 0.25)
    mine = lax.broadcasted_iota(jnp.int32, (lower.frame, upper.frame), 1).astype(F32)
    return jnp.where(jnp.abs(group - mine) < 0.5, 0.125, 0.0).astype(LOW)


def finish_upper(
    layer, group_ref, sides_ref, zb_ref, zc_ref, suma_ref, sums_ref, par_ref, cot_ref,
    out_ref, gu_ref, back_ref,
):
    mask = crop_mask(layer.frame, layer.side, crop_of(group_ref, sides_ref, layer.halved))
    norms = Norms(sums_ref, par_ref, suma_ref[2:3, 0:1])
    back_ref[...] = jnp.zeros(back_ref.shape, F32)
    for t in range(layer.frames):
        rows = layer.at(t)
        for index, (kind, j) in enumerate(UNIT_TILES):
            at = norms.lane(kind, j)
            z_ref = zb_ref if kind == "b" else zc_ref
            n = norms.normed(z_ref[rows, tile(j)], at)
            u = norms.shifted(n, at)
            s = sigmoid(u)
            out_ref[rows, tile(index)] = (u * s * mask).astype(LOW)
            gu = cot_ref[rows, tile(index)].astype(F32) * mask * (s * (1.0 + u * (1.0 - s)))
            gu_ref[rows, tile(index)] = gu
            add_sums(back_ref, at, gu, gu * n)


def unit_backward(
    layer, group_ref, sides_ref, gu_ref, zb_ref, zc_ref, suma_ref, sums_ref, back_ref, par_ref,
    dzb_ref, three_ref, thin3_ref, around, flat,
):
    frames, frame, side = layer.frames, layer.frame, layer.side
    mask = crop_mask(frame, side, crop_of(group_ref, sides_ref, layer.halved))
    count = suma_ref[2:3, 0:1]
    norms = Norms(sums_ref, par_ref, count)
    c0, c1, c2 = back_terms(back_ref, count, norms.gamma, norms.inverse)
    low_half = lanes() < 64

    def dz_of(t, index):
        kind, j = UNIT_TILES[index]
        at = norms.lane(kind, j)
        z_ref = zb_ref if kind == "b" else zc_ref
        rows = layer.at(t)
        n = norms.normed(z_ref[rows, tile(j)], at)
        return (gu_ref[rows, tile(index)] * c0[:, at] - c1[:, at] - n * c2[:, at]) * mask

    clear_edges(around, frame)
    for t in range(frames):
        for index in (0, 1):
            dzb_ref[layer.at(t), tile(index)] = dz_of(t, index).astype(LOW)
        flat[layer.at(t), :] = dz_of(t, 6)

    def put(t, value):
        dzb_ref[layer.at(t), tile(2)] = (value * mask).astype(LOW)

    neighbour_sum([flat[layer.at(t), :] for t in range(frames)], around, frame, side, put)
    for t in range(frames):
        flat[layer.at(t), :] = jnp.where(low_half, dz_of(t, 4), 0.0)
    empty = jnp.zeros((frame, 128), LOW)
    for t in range(frames):
        parts = [dz_of(t, index).astype(LOW) for index in (2, 3, 5)]
        for k in range(3):
            to = t - 1 + k
            if 0 <= to < frames:
                rows = layer.at(to)
                three_ref[rows, tile(2 * k)] = parts[0]
                three_ref[rows, tile(2 * k + 1)] = parts[1]
                thin3_ref[rows, tile(k)] = parts[2]
        rest = pltpu.roll(flat[layer.at(t), :], 64, 1)
        if t < frames - 1:
            rest = rest + flat[layer.at(t + 1), :]
        three_ref[layer.at(t), tile(6)] = rest.astype(LOW)
        three_ref[layer.at(t), tile(7)] = flat[layer.at(t - 1), :].astype(LOW) if t else empty
    for rows, k in ((layer.at(0), 2), (layer.at(frames - 1), 0)):
        three_ref[rows, tile(2 * k)] = empty
        three_ref[rows, tile(2 * k + 1)] = empty
        thin3_ref[rows, tile(k)] = empty


def unit_and_weights(
    layer, parts, columns, group_ref, sides_ref, me_ref, gu_ref, zb_ref, zc_ref, suma_ref, sums_ref, back_ref, par_ref,
    wide_ref, dza_ref, q_ref, thin_ref, x_ref, dzb_ref, three_ref, thin3_ref, keep_ref, send_ref, other_keep_ref,
    other_send_ref, around, flat, wide_grad, last_grad, other_wide_grad, thin_grad, point_grad,
):
    unit_backward(
        layer, group_ref, sides_ref, gu_ref, zb_ref, zc_ref, suma_ref, sums_ref, back_ref, par_ref,
        dzb_ref, three_ref, thin3_ref, around, flat,
    )
    weights(
        parts[0], columns[0], "wl", me_ref, wide_ref, three_ref, dza_ref, q_ref, keep_ref, send_ref, wide_grad, last_grad
    )
    weights(
        parts[1], columns[1], "wo", me_ref, wide_ref, three_ref, thin_ref, thin3_ref, x_ref, dzb_ref, other_keep_ref,
        other_send_ref, other_wide_grad, thin_grad, point_grad,
    )


def conv_backward(
    layer, group_ref, sides_ref, three_ref, thin3_ref, za_ref, suma_ref, para_ref, wt_ref, wnt_ref,
    gua_ref, backa_ref, around, shifts, thins, rem, main, ready=lambda: None,
):
    frames, frame, side = layer.frames, layer.frame, layer.side
    mask = crop_mask(frame, side, crop_of(group_ref, sides_ref, layer.halved))
    column = [column_mask(frame, side, dw) for dw in (-1, 0, 1)]
    low_half = lanes() < 64
    first_part = lanes() < 32
    clear_edges(around, frame)
    main[...] = jnp.zeros(main.shape, F32)
    rem[...] = jnp.zeros(rem.shape, F32)
    for t in range(frames):
        rows = layer.at(t)
        rest = jnp.where(low_half, 0.0, three_ref[rows, tile(6)].astype(F32))
        parts = [
            three_ref[rows, tile(2)].astype(F32),
            three_ref[rows, tile(3)].astype(F32),
            rest + pltpu.roll(rest, 64, 1),
            thin3_ref[rows, tile(1)].astype(F32),
        ]
        for j in range(4):
            around[EDGE : EDGE + frame, tile(j)] = parts[j]
        mixed = [None] * 5
        for k, (dh, dw) in enumerate(TAPS):
            start = EDGE - dh * side - dw
            for j in range(4):
                shifted = around[start : start + frame, tile(j)]
                if dw:
                    shifted = shifted * column[1 - dw]
                if j < 2:
                    shifts[:, tile(2 * k + j)] = shifted.astype(LOW)
                elif j == 3:
                    thins[:, tile(k)] = shifted.astype(LOW)
                else:
                    shifted = jnp.where(low_half if k % 2 == 0 else ~low_half, shifted, 0.0)
                    held = mixed[k // 2]
                    mixed[k // 2] = shifted if held is None else held + shifted
        for g in range(5):
            shifts[:, tile(18 + g)] = mixed[g].astype(LOW)
        if t == 0:
            ready()
        product = dot_nt(shifts[...], wt_ref[...])
        thin = dot_nt(thins[...], wnt_ref[...])
        for k in range(3):
            to = t - 1 + k
            if 0 <= to < frames:
                rows = layer.at(to)
                main[rows, :] += product[:, tile(k)]
                turn = (128 - 32 * k) % 128
                last = product[:, tile(3)]
                rem[rows, 0:128] += last if turn == 0 else pltpu.roll(last, turn, 1)
                rem[rows, 128:256] += thin if turn == 0 else pltpu.roll(thin, turn, 1)
    mean, inverse = moments(suma_ref, suma_ref[2:3, :])
    backa_ref[...] = jnp.zeros(backa_ref.shape, F32)
    for t in range(frames):
        rows = layer.at(t)
        for j in range(3):
            grad = main[rows, :] if j == 0 else rem[rows, tile(j - 1)]
            n = (za_ref[rows, tile(j)] - mean[:, tile(j)]) * inverse[:, tile(j)]
            u = para_ref[0:1, tile(j)] * n + para_ref[1:2, tile(j)]
            s = sigmoid(u)
            gu = grad * mask * (s * (1.0 + u * (1.0 - s)))
            if j:
                gu = jnp.where(first_part, gu, 0.0)
            gua_ref[rows, tile(j)] = gu
            add_sums(backa_ref, tile(j), gu, gu * n)


def point_back(layer, mask, gua_ref, za_ref, suma_ref, backa_ref, para_ref, dza_ref):
    count = suma_ref[2:3, :]
    mean, inverse = moments(suma_ref, count)
    c0, c1, c2 = back_terms(backa_ref, count, para_ref[0:1, :], inverse)
    for t in range(layer.frames):
        rows = layer.at(t)
        for j in range(3):
            at = tile(j)
            n = (za_ref[rows, at] - mean[:, at]) * inverse[:, at]
            dz = (gua_ref[rows, at] * c0[:, at] - c1[:, at] - n * c2[:, at]) * mask
            if j:
                dz = jnp.where(lanes() < 32, dz, 0.0)
            dza_ref[rows, at] = dz.astype(LOW)


def join_blocks(
    upper, lower, group_ref, sides_ref, gua_ref, za_ref, suma_ref, backa_ref, para_ref, dzb_ref, wa_ref, wb_ref,
    zb_ref, zc_ref, suma1_ref, sums1_ref, par1_ref, dza_ref, gu_ref, back_ref, wide,
):
    small = crop_mask(upper.frame, upper.side, crop_of(group_ref, sides_ref, True))
    point_back(upper, small, gua_ref, za_ref, suma_ref, backa_ref, para_ref, dza_ref)
    mask = crop_mask(lower.frame, lower.side, crop_of(group_ref, sides_ref, False))
    norms = Norms(sums1_ref, par1_ref, suma1_ref[2:3, 0:1])
    back_ref[...] = jnp.zeros(back_ref.shape, F32)
    pick = spread_matrix(upper, lower)
    for t in range(upper.frames):
        rows = upper.at(t)
        dq = dot_nt(dzb_ref[rows, :], wb_ref[...]) + dot(dza_ref[rows, :], wa_ref[...])
        high = dq.astype(LOW)
        rest = (dq - high.astype(F32)).astype(LOW)
        wide[...] = dot(pick, high) + dot(pick, rest)
        for source in (2 * t, 2 * t + 1):
            at_rows = lower.at(source)
            for index, (kind, j) in enumerate(UNIT_TILES):
                at = norms.lane(kind, j)
                z_ref = zb_ref if kind == "b" else zc_ref
                n = norms.normed(z_ref[at_rows, tile(j)], at)
                u = norms.shifted(n, at)
                s = sigmoid(u)
                gu = wide[:, tile(index)] * mask * (s * (1.0 + u * (1.0 - s)))
                gu_ref[at_rows, tile(index)] = gu
                add_sums(back_ref, at, gu, gu * n)


def last_back(
    layer, group_ref, sides_ref, gua_ref, za_ref, suma_ref, backa_ref, para_ref, dzb_ref, wa_ref, wb_ref, dza_ref, grad_ref,
):
    mask = crop_mask(layer.frame, layer.side, crop_of(group_ref, sides_ref, layer.halved))
    point_back(layer, mask, gua_ref, za_ref, suma_ref, backa_ref, para_ref, dza_ref)
    for t in range(layer.frames):
        rows = layer.at(t)
        total = dot_nt(dzb_ref[rows, :], wb_ref[...]) + dot(dza_ref[rows, :], wa_ref[...])
        grad_ref[rows, :] = (total * mask).astype(LOW)


def place(me, pair, core):
    bits = lax.shift_right_logical(me, 1) ^ pair
    x, y = bits & 1, lax.shift_right_logical(bits, 1) & 1
    near, far = lax.shift_right_logical(bits, 2) & 1, lax.shift_right_logical(bits, 3) & 1
    first = x + core * (y - x)
    second = y + core * (x - y)
    return first * 8 + second * 4 + near * 2 + far


def put_pair(me, keep_ref, send_ref, pair, rows, even, odd):
    core = me & 1
    mine = core == 0
    keep_ref[place(me, pair, core), rows, :] = jnp.where(mine, even, odd)
    send_ref[place(me, pair, 1 - core), rows, :] = jnp.where(mine, odd, even)


def get_pair(me, own_ref, other_ref, pair, rows):
    core = me & 1
    mine = core == 0
    own = own_ref[place(me, pair, core), rows, :]
    other = other_ref[place(me, pair, 1 - core), rows, :]
    return jnp.where(mine, own, other), jnp.where(mine, other, own)


def segments(blocks):
    rows = -(-sum(length for _, length in blocks) // 256) * 8
    pieces, piece, room = [], [], rows
    for name, length in blocks:
        at = 0
        while at < length:
            take = min(room, length - at)
            piece.append((name, at, at + take, rows - room))
            at += take
            room -= take
            if not room:
                pieces.append(piece)
                piece, room = [], rows
    if piece:
        pieces.append(piece)
    return rows, pieces + [[]] * (32 - len(pieces))


def wide(layer, *tiles):
    return [(("wide", j, layer), 1440) for j in tiles]


def point_and_thin(layer):
    return [(("point", j, layer), 832) for j in range(3)] + [(("thin", j, layer), 288) for j in range(3)]


def last(layer):
    return [(("last", j, layer), 192) for j in range(7)]


PARTS = [
    segments(wide(1, *range(8)) + point_and_thin(1)),
    segments(wide(0, 0, 1, 2, 3, 6) + last(1)),
    segments(wide(0, 4, 5, 7) + point_and_thin(0)),
    segments(last(0)),
]


def piece_value(piece, rows, read):
    parts = [read(name, first, end) for name, first, end, _ in piece]
    filled = sum(end - first for _, first, end, _ in piece)
    if filled < rows:
        parts.append(jnp.zeros((rows - filled, 128), F32))
    return parts[0] if len(parts) == 1 else jnp.concatenate(parts, axis=0)


def put_pieces(me, keep_ref, send_ref, part, read):
    rows, pieces = part
    for pair in range(16):
        even, odd = (piece_value(pieces[2 * pair + i], rows, read) for i in (0, 1))
        put_pair(me, keep_ref, send_ref, pair, slice(0, rows), even, odd)


def without_gap(ref, grad):
    if grad.shape[0] == 896:
        ref[0:576, :] = grad[0:576]
        ref[576:832, :] = grad[640:896]
    else:
        ref[...] = grad


def weights(part, columns, kinds, me_ref, *refs):
    refs = list(refs)
    read_from = {}
    operands = [refs.pop(0) for _ in range({"w": 2, "o": 4, "l": 2}[kinds[0]] + (0 if len(kinds) == 1 else {"o": 4, "l": 2}[kinds[1]]))]
    keep_ref, send_ref = refs.pop(0), refs.pop(0)
    for kind in kinds:
        if kind == "w":
            wide_ref, three_ref = operands.pop(0), operands.pop(0)
            grad = refs.pop(0)
            at = 0
            for first, count in columns:
                grad[:, tile(at, count)] = dot_tn(wide_ref[:, 0:1440], three_ref[:, tile(first, count)])
                for j in range(count):
                    read_from["wide", first + j] = (grad, at + j)
                at += count
        elif kind == "o":
            thin_ref, thin3_ref, x_ref, dzb_ref = (operands.pop(0) for _ in range(4))
            thin_grad, point_grad = refs.pop(0), refs.pop(0)
            thin_grad[...] = dot_tn(thin_ref[...], thin3_ref[...])
            without_gap(point_grad, dot_tn(x_ref[...], dzb_ref[...]))
            for j in range(3):
                read_from["point", j] = (point_grad, j)
                read_from["thin", j] = (thin_grad, j)
        else:
            dza_ref, x_ref = operands.pop(0), operands.pop(0)
            last_grad = refs.pop(0)
            grad = dot_tn(dza_ref[...], x_ref[...])
            if grad.shape[1] == 896:
                grad = close_gap(grad)
            width = grad.shape[1]
            last_grad[0:160, 0:width] = grad[0:160]
            last_grad[160:192, 0:width] = grad[256:288]
            if width < 896:
                last_grad[:, width:896] = jnp.zeros((192, 896 - width), F32)
            for j in range(7):
                read_from["last", j] = (last_grad, j)

    def read(name, first, end):
        ref, j = read_from[name[0:2]]
        return ref[first:end, tile(j)]

    put_pieces(me_ref[0], keep_ref, send_ref, part, read)


OUT_SHAPES = [(832, 256), (160, 832), (27, 160, 320), (32, 832), (27, 32, 128), (832, 128)]
SINGLE, REDUCE, SPATIAL, SQUEEZE, NARROW, PROJECT = range(6)


def assemble(sources, targets, aliased, me_ref, *refs):
    me = me_ref[0]
    many = sum(2 if relative else 1 for _, relative in sources)
    arrived, refs = list(refs[0:many]), refs[many + (6 if aliased else 0) :]
    outs, stages, sems = refs[0:6], refs[6 : 6 + len(targets)], refs[6 + len(targets)]
    stage = {(which, block): (ref, first) for (which, block, first, _), ref in zip(targets, stages)}

    def put_wide(block, k, lanes_at, first, value):
        ref, offset = stage[SPATIAL, block]
        done = 0
        while done < value.shape[0]:
            row = first + done
            if row < 1152:
                tap, channel = row // 128, row % 128
                take = min(128 - channel, value.shape[0] - done)
            else:
                tap, channel = (row - 1152) // 32, 128 + (row - 1152) % 32
                take = min(160 - channel, value.shape[0] - done)
            ref[k * 9 + tap - offset, channel : channel + take, lanes_at] = value[done : done + take]
            done += take

    def put(name, first, end, value):
        kind, j, block = name
        if kind == "wide":
            if j < 6:
                put_wide(block, j // 2, tile(j % 2), first, value)
            elif j == 6:
                put_wide(block, 0, slice(256, 320), first, value[:, 0:64])
                put_wide(block, 1, slice(256, 320), first, pltpu.roll(value, 64, 1)[:, 0:64])
            else:
                put_wide(block, 2, slice(256, 320), first, value[:, 0:64])
        elif kind == "point":
            if j < 2:
                stage[SINGLE, block][0][first:end, tile(j)] = value
            else:
                stage[PROJECT, block][0][first:end, :] = value
        elif kind == "thin":
            done = 0
            while done < end - first:
                tap, channel = (first + done) // 32, (first + done) % 32
                take = min(32 - channel, end - first - done)
                stage[NARROW, block][0][j * 9 + tap, channel : channel + take, :] = value[done : done + take]
                done += take
        else:
            lanes_at = tile(j) if j < 6 else slice(768, 832)
            for which, low, high in ((REDUCE, 0, 160), (SQUEEZE, 160, 192)):
                begin, stop = max(first, low), min(end, high)
                if begin < stop:
                    part = value[begin - first : stop - first]
                    stage[which, block][0][begin - low : stop - low, lanes_at] = part if j < 6 else part[:, 0:64]

    for (rows, pieces), relative in sources:
        held = [arrived.pop(0) for _ in range(2 if relative else 1)]
        for pair in range(16):
            if relative:
                both = get_pair(me, *held, pair, slice(0, rows))
            else:
                both = [held[0][2 * pair + i] for i in (0, 1)]
            for i in (0, 1):
                for name, first, end, row in pieces[2 * pair + i]:
                    put(name, first, end, both[i][row : row + end - first])
    copies = []
    for i, ((which, block, first, count), ref) in enumerate(zip(targets, stages)):
        to = outs[which].at[block]
        if count < OUT_SHAPES[which][0]:
            to = to.at[pl.ds(first, count)]
        copies.append(pltpu.make_async_copy(ref, to, sems.at[i]))
        copies[-1].start()
    for copy in copies:
        copy.wait()


def assemble_call(me, sources, targets, outs):
    anywhere = pl.BlockSpec(memory_space=pl.ANY)
    arrays = sum((list(found) for _, found in sources), [])
    targets = [(which, block, first, count or OUT_SHAPES[which][0]) for which, block, first, count in targets]
    scratch = [pltpu.VMEM((count,) + OUT_SHAPES[which][1:], F32) for which, _, _, count in targets]
    return pl.pallas_call(
        functools.partial(assemble, [(part, len(found) == 2) for part, found in sources], targets, outs is not None),
        out_shape=tuple(struct((2,) + shape, F32) for shape in OUT_SHAPES),
        in_specs=[SMEM] + [VMEM] * len(arrays) + [anywhere] * (0 if outs is None else 6),
        out_specs=tuple([anywhere] * 6),
        scratch_shapes=scratch + [pltpu.SemaphoreType.DMA((len(targets),))],
        input_output_aliases={} if outs is None else {1 + len(arrays) + i: i for i in range(6)},
        compiler_params=pltpu.CompilerParams(vmem_limit_bytes=scoped(scratch, 3)),
        cost_estimate=pl.CostEstimate(flops=1, bytes_accessed=1, transcendentals=0),
        name="assemble",
    )(me, *arrays, *([] if outs is None else outs))


def unfit_vectors(sums_a, sums):
    return jnp.concatenate(
        [sums[:, 0:256], sums_a[:, 0:160], sums[:, 384:704], sums_a[:, 256:288], sums[:, 768:896], sums[:, 256:384]], axis=1
    )


def open_gap(value):
    value = value.astype(F32)
    tiles = [value[:, tile(j)] for j in range(6)]
    tiles.append(jnp.concatenate([value[:, 768:832], jnp.zeros((value.shape[0], 64), F32)], axis=1))
    low_half = lanes() < 64
    turned = [pltpu.roll(part, 64, 1) for part in tiles[4:7]]
    tiles[4] = jnp.where(low_half, tiles[4], 0.0)
    tiles[5] = jnp.where(low_half, turned[0], turned[1])
    tiles[6] = jnp.where(low_half, turned[1], turned[2])
    return jnp.concatenate(tiles, axis=1).astype(LOW)


def close_gap(value):
    low_half = lanes() < 64
    tiles = [value[:, tile(j)] for j in range(7)]
    turned = [pltpu.roll(part, 64, 1) for part in tiles[5:7]]
    tiles[4] = jnp.where(low_half, tiles[4], turned[0])
    tiles[5] = jnp.where(low_half, turned[0], turned[1])
    tiles[6] = turned[1]
    return jnp.concatenate(tiles, axis=1)


def fit_points(single_ref, project_ref, reduce_ref, squeeze_ref, wa_ref, wb_ref):
    gap = wa_ref.shape[1] == 896
    if gap:
        spans = [(slice(0, 576), slice(0, 576)), (slice(640, 896), slice(576, 832))]
        wb_ref[576:640, :] = jnp.zeros((64, 384), LOW)
    else:
        spans = [(slice(0, 832), slice(0, 832))]
    for to, source in spans:
        wb_ref[to, 0:256] = single_ref[0, source, :]
        wb_ref[to, 256:384] = project_ref[0, source, :]
    reduce, squeeze = reduce_ref[0], squeeze_ref[0]
    if gap:
        reduce, squeeze = open_gap(reduce), open_gap(squeeze)
    wa_ref[0:128, :] = reduce[0:128]
    for i in range(4):
        wa_ref[128 + 32 * i : 160 + 32 * i, :] = reduce[128:160]
        wa_ref[256 + 32 * i : 288 + 32 * i, :] = squeeze


def pair_lanes(left, right):
    parts = [jnp.zeros((max(p.shape[0] for p in (left, right) if p is not None), 64), F32) if p is None else p.astype(F32) for p in (left, right)]
    return jnp.concatenate(parts, axis=1).astype(LOW)


def fit_convs(
    index, scale_ref, shift_ref, spatial_ref, narrow_ref, w_ref, wn_ref, wt_ref, wnt_ref, para_ref, par_ref
):
    spans = [(0, 128, 128 * tap, tap) for tap in range(9)] + [(128, 160, 1152 + 32 * tap, tap) for tap in range(9)]
    w_ref[1440:1536, :] = jnp.zeros((96, 1024), LOW)
    for first, end, row, tap in spans:
        rows = slice(row, row + end - first)
        rest = [spatial_ref[0, 9 * k + tap, first:end, 256:320] for k in range(3)]
        for k in range(3):
            w_ref[rows, k * 256 : (k + 1) * 256] = spatial_ref[0, 9 * k + tap, first:end, 0:256]
        w_ref[rows, 768:896] = pair_lanes(rest[0], rest[1])
        w_ref[rows, 896:1024] = pair_lanes(rest[2], None)
    wt_ref[480:512, :] = jnp.zeros((32, 2944), LOW)
    for k in range(3):
        for first, end, row in ((0, 128, 128 * k), (128, 160, 384 + 32 * k)):
            rows = slice(row, row + end - first)
            for tap in range(9):
                wt_ref[rows, tap * 256 : (tap + 1) * 256] = spatial_ref[0, 9 * k + tap, first:end, 0:256]
            for g in range(5):
                left = spatial_ref[0, 9 * k + 2 * g, first:end, 256:320]
                right = spatial_ref[0, 9 * k + 2 * g + 1, first:end, 256:320] if g < 4 else None
                wt_ref[rows, tile(18 + g)] = pair_lanes(left, right)
    wn_ref[288:384, :] = jnp.zeros((96, 384), LOW)
    wnt_ref[96:128, :] = jnp.zeros((32, 1152), LOW)
    for k in range(3):
        for tap in range(9):
            part = narrow_ref[0, 9 * k + tap]
            wn_ref[32 * tap : 32 * tap + 32, tile(k)] = part
            wnt_ref[32 * k : 32 * k + 32, tile(tap)] = part
    for row, ref in ((0, scale_ref), (1, shift_ref)):
        vector = ref[index : index + 1, :]
        rest = vector[:, 384:416]
        squeeze = vector[:, 736:768]
        para_ref[row : row + 1, 0:128] = vector[:, 256:384]
        para_ref[row : row + 1, 128:256] = jnp.concatenate([rest] * 4, axis=1)
        para_ref[row : row + 1, 256:384] = jnp.concatenate([squeeze] * 4, axis=1)
        par_ref[row : row + 1, 0:256] = vector[:, 0:256]
        par_ref[row : row + 1, 256:384] = vector[:, 896:1024]
        par_ref[row : row + 1, 384:768] = jnp.concatenate([vector[:, 416:736], jnp.zeros((1, 64), F32)], axis=1)
        par_ref[row : row + 1, 768:896] = vector[:, 768:896]


def fetch_block(body, index, held, made, *refs):
    whole, refs = refs[0 : len(refs) - 2 * held - made - 1], refs[len(refs) - 2 * held - made - 1 :]
    split, outs, parts, sems = refs[0:held], refs[held : held + made], refs[held + made : -1], refs[-1]
    copies = [pltpu.make_async_copy(ref.at[pl.ds(index, 1)], part, sems.at[i]) for i, (ref, part) in enumerate(zip(split, parts))]
    for copy in copies:
        copy.start()
    for copy in copies:
        copy.wait()
    body(*whole, *parts, *outs)


def layer_call(body, index, split, whole, outs, name=None):
    scratch = [pltpu.VMEM((1,) + x.shape[1:], x.dtype) for x in split]
    return pl.pallas_call(
        functools.partial(fetch_block, body, index, len(split), len(outs)),
        out_shape=tuple(outs),
        in_specs=[VMEM] * len(whole) + [pl.BlockSpec(memory_space=pl.ANY)] * len(split),
        out_specs=tuple([VMEM] * len(outs)),
        scratch_shapes=scratch + [pltpu.SemaphoreType.DMA((len(split),))],
        compiler_params=pltpu.CompilerParams(vmem_limit_bytes=scoped(scratch, 4)),
        cost_estimate=pl.CostEstimate(flops=1, bytes_accessed=1, transcendentals=0),
        name=name,
    )(*whole, *split)


def exchange(value, sizes, bits):
    total = sizes[0] * sizes[1]

    def swap(mask):
        return lax.ppermute(value, AXES, [(i, i ^ mask) for i in range(total)])

    if len(bits) == 1:
        return value + swap(1 << bits[0])
    one, two = 1 << bits[0], 1 << bits[1]
    return (value + swap(one)) + (swap(two) + swap(one | two))


class Sum:
    def __init__(self, value, sizes):
        self.value, self.sizes, self.at = value, sizes, 0
        total = sizes[0] * sizes[1]
        bits = list(range(total.bit_length() - 1))
        self.stages = [bits[:1]] + [bits[at : at + 2] for at in range(1, len(bits), 2)]
        self.able = not (total & (total - 1))
        if not self.able:
            self.stages = []
            self.value = lax.psum(value, AXES)

    def step(self):
        if self.at < len(self.stages):
            self.value = exchange(self.value, self.sizes, self.stages[self.at])
            self.at += 1
        return self.value

    def result(self):
        while self.at < len(self.stages):
            self.step()
        return self.value


def sum_all(value, sizes):
    return Sum(value, sizes).result()


def meet(*holders):
    names = [[n for n in ("value", "keep", "send", "ready", "array") if getattr(holder, n, None) is not None] for holder in holders]
    values = lax.optimization_barrier([[getattr(h, n) for n in ns] for h, ns in zip(holders, names)])
    for holder, ns, got in zip(holders, names, values):
        for n, value in zip(ns, got):
            setattr(holder, n, value)


class Held:
    def __init__(self, array):
        self.array = array


class Sharing:
    def __init__(self, sizes):
        dp, rep = sizes
        self.sizes = sizes
        self.total = dp * rep
        self.able = not (self.total & (self.total - 1)) and dp >= 8 and rep >= 4
        low = rep.bit_length() - 1
        self.bits = [0, 1, low, low + 1, low + 2]
        self.other = [bit for bit in range(self.total.bit_length() - 1) if bit not in self.bits]

    def me(self):
        if not self.able:
            return jnp.zeros((1,), jnp.int32)
        flat = lax.axis_index("dp") * self.sizes[1] + lax.axis_index("rep")
        index = sum(((flat >> bit) & 1) << i for i, bit in enumerate(self.bits))
        return index.reshape(1).astype(jnp.int32)

    def swap(self, value, even, odd=None):
        masks = [sum(1 << self.bits[i] for i in bits) for bits in (even, even if odd is None else odd)]
        return lax.ppermute(value, AXES, [(i, i ^ masks[i & 1]) for i in range(self.total)])

    def chain(self, keep, send):
        return Chain(self, keep, send)


CORE, FIRST, SECOND, BOTH = ((0,), (0,)), ((1,), (2,)), ((2,), (1,)), ((1, 2), (1, 2))
FAR, NEAR, ENDS = ((4,), (4,)), ((3,), (3,)), ((3, 4), (3, 4))


class Chain:
    def __init__(self, sharing, keep, send, short=False):
        self.sharing, self.keep, self.send, self.short = sharing, keep, send, short
        self.ready = None
        names = ["core", "both" if short else "first", None if short else "second", "depth"]
        self.stages = [n for n in names + ["up_depth"] + ["up_" + n for n in reversed(names[0:3]) if n] if n]
        if not sharing.able:
            self.keep, self.send, self.stages = lax.psum(keep, AXES), lax.psum(send, AXES), []

    def offers(self):
        stage, send, keep = self.stages[0], self.send, self.keep
        if stage in ("core", "up_core"):
            return [(CORE, send)]
        if stage in ("first", "up_first"):
            return [(FIRST, send)]
        if stage in ("second", "up_second"):
            return [(SECOND, send)]
        if stage == "both":
            return [(FIRST, send[0:4]), (SECOND, keep[4:8]), (BOTH, send[4:8])]
        if stage == "up_both":
            return [(SECOND, send), (FIRST, send), (BOTH, send)]
        if stage == "depth":
            return [(FAR, send[0]), (NEAR, send[1]), (ENDS, send[2])]
        return [(FAR, send), (NEAR, send), (ENDS, send)]

    def accept(self, got):
        stage, send, keep = self.stages.pop(0), self.send, self.keep
        if stage in ("core", "first"):
            half = keep.shape[0] // 2
            self.keep, self.send = keep[0:half] + got[0][0:half], keep[half:] + got[0][half:]
        elif stage == "second":
            self.split([keep[i] + got[0][i] for i in range(4)])
        elif stage == "both":
            self.split([(keep[i] + got[0][i]) + (got[1][i] + got[2][i]) for i in range(4)])
        elif stage == "depth":
            whole = (keep + got[0]) + (got[1] + got[2])
            for bit in self.sharing.other:
                whole = exchange(whole, self.sharing.sizes, [bit])
            self.keep, self.send = None, whole
        elif stage == "up_depth":
            self.send = jnp.stack([send, *got])
        elif stage == "up_core":
            self.keep, self.send = send, got[0]
        else:
            self.send = jnp.concatenate([send, *got])

    def split(self, parts):
        self.keep, self.send = parts[0], parts[1:]

    def half(self):
        if not self.stages:
            return
        if self.ready is None:
            self.ready = self.keep[4:8] + self.sharing.swap(self.send[4:8], *FIRST)
            self.keep, self.send = self.keep[0:4], self.send[0:4]
        else:
            self.keep = self.keep + self.sharing.swap(self.send, *FIRST)
            self.send, self.ready = self.ready, None
            self.stages.pop(0)

    def result(self):
        return [self.keep, self.send]


def advance(*chains):
    chains = [chain for chain in chains if chain.stages]
    offered = [chain.offers() for chain in chains]
    got = [[None] * len(offers) for offers in offered]
    partners = {}
    for i, offers in enumerate(offered):
        for j, (partner, _) in enumerate(offers):
            partners.setdefault((partner, i if partner == CORE else 0), []).append((i, j))
    for (partner, _), places in partners.items():
        values = [offered[i][j][1] for i, j in places]
        flat = [value.reshape(-1, 128) for value in values]
        arrived = chains[0].sharing.swap(flat[0] if len(flat) == 1 else jnp.concatenate(flat), *partner)
        at = 0
        for (i, j), value, rows in zip(places, values, flat):
            got[i][j] = arrived[at : at + rows.shape[0]].reshape(value.shape)
            at += rows.shape[0]
    for chain, received in zip(chains, got):
        chain.accept(received)


def shards(sizes, *arguments):
    clip_input, cotangent, clip_group, crop_sides = arguments[:4]
    kernels, bn_scale, bn_shift = arguments[4:10], arguments[10], arguments[11]
    w_single, w_reduce, w_spatial, w_squeeze, w_narrow, w_project = kernels
    _, frames, side, _, width = clip_input.shape
    lower, upper = Layer(frames, side, False), Layer(frames // 2, side // 2, True)
    where = [clip_group, crop_sides]
    merged = [w_spatial.reshape(2, 27, 160, 320), w_narrow.reshape(2, 27, 32, 128)]
    turned = [jnp.swapaxes(w_reduce, 1, 2), jnp.swapaxes(w_squeeze, 1, 2)]
    points = [
        layer_call(
            fit_points, i, [w_single, w_project] + turned, [],
            [struct((384, 832 + 64 * i), LOW), struct((832 + 64 * i, 384), LOW)], name="fit_points",
        )
        for i in (0, 1)
    ]
    fitted = [
        layer_call(
            functools.partial(fit_convs, i),
            i,
            merged,
            [bn_scale, bn_shift],
            [struct((1536, 1024), LOW), struct((384, 384), LOW), struct((512, 2944), LOW), struct((128, 1152), LOW)]
            + [struct((2, 384), F32), struct((2, 896), F32)],
            name="fit_convs",
        )
        for i in (0, 1)
    ]
    pars = [item[4:6] for item in fitted]
    spatials = [(item[0], item[2]) for item in fitted]
    narrows = [(item[1], item[3]) for item in fitted]
    def frames_first(value, layer):
        value = jnp.transpose(value, (0, 2, 3, 1, 4)).reshape(layer.side * layer.side, layer.frames, width)
        return jnp.transpose(value, (1, 0, 2))

    def frames_back(value, layer):
        value = jnp.transpose(value, (1, 0, 2)).reshape(1, layer.side, layer.side, layer.frames, width)
        return jnp.transpose(value, (0, 3, 1, 2, 4))

    x = frames_first(clip_input, lower).reshape(lower.rows, width)
    cot = frames_first(cotangent, upper)
    cot = jnp.concatenate(
        [cot[..., 0:576], jnp.zeros(cot.shape[:2] + (64,), LOW), cot[..., 576:832]], axis=2
    )
    cot = jnp.pad(cot, ((0, 0), (0, upper.frame - upper.side * upper.side), (0, 0))).reshape(upper.rows, 896)

    def around(layer, tiles):
        return pltpu.VMEM((layer.frame + 2 * EDGE, 128 * tiles), F32)

    def forward(layer, za, suma, sumb, index):
        r = layer.rows
        return call(
            functools.partial(conv_forward, layer),
            where + [za, suma, pars[index][0], sumb, spatials[index][0], narrows[index][0]],
            [struct((r, 1536), LOW), struct((r, 384), LOW), struct((r, 512), F32), struct((2, 896), F32)],
            [around(layer, 3), pltpu.VMEM((r, 256), F32)],
            name="conv_forward",
        )

    def unit_back(layer, gu, zb, zc, suma, sums, back, index):
        r = layer.rows
        return call(
            functools.partial(unit_backward, layer),
            where + [gu, zb, zc, suma, sums, back, pars[index][1]],
            [struct((r, 384), LOW), struct((r, 1024), LOW), struct((r, 384), LOW)],
            [around(layer, 1), pltpu.VMEM((r, 128), F32)],
            fetch=[2, 3, 4] if layer.halved else [],
            name="unit_backward",
        )

    def conv_back(layer, three, thin3, za, suma, index):
        r = layer.rows
        return call(
            functools.partial(conv_backward, layer),
            where + [three, thin3, za, suma, pars[index][0], spatials[index][1], narrows[index][1]],
            [struct((r, 384), F32), struct((2, 384), F32)],
            [
                around(layer, 4),
                pltpu.VMEM((layer.frame, 2944), LOW),
                pltpu.VMEM((layer.frame, 1152), LOW),
                pltpu.VMEM((r, 256), F32),
                pltpu.VMEM((r, 128), F32),
            ],
            late=[7, 8] if layer.halved else [],
            name="conv_backward",
        )

    sharing = Sharing(sizes)
    me = sharing.me()

    def make_weights(index, columns, kinds, *operands, short=False, fetch=False):
        part = PARTS[index]
        scratch = []
        for kind in kinds:
            if kind == "w":
                scratch.append((1440, 128 * sum(count for _, count in columns)))
            elif kind == "o":
                scratch += [(384, 384), (832, 384)]
            else:
                scratch.append((192, 896))
        made = call(
            functools.partial(weights, part, columns, kinds),
            [me, *operands],
            [struct((16, part[0], 128), F32)] * 2,
            [pltpu.VMEM(shape, F32) for shape in scratch],
            scalars=1,
            fetch=range(1, 1 + len(operands)) if fetch else [],
            name="weights",
        )
        return Chain(sharing, *made, short=short)

    def unit_and_first(layer, gu, zb, zc, suma, sums, back, index, wide, dza, upper_source, thin, source):
        r = layer.rows
        parts, columns = PARTS[1:3], ([(0, 2), (2, 2), (6, 1)], [(4, 2), (7, 1)])
        pieces = [struct((16, part[0], 128), F32) for part in parts for _ in (0, 1)]
        grads = [(1440, 640), (192, 896), (1440, 384), (384, 384), (832, 384)]
        *made, keep, send, other_keep, other_send = call(
            functools.partial(unit_and_weights, layer, parts, columns),
            where + [me, gu, zb, zc, suma, sums, back, pars[index][1], wide, dza, upper_source, thin, source],
            [struct((r, 384), LOW), struct((r, 1024), LOW), struct((r, 384), LOW)] + pieces,
            [around(layer, 1), pltpu.VMEM((r, 128), F32)] + [pltpu.VMEM(shape, F32) for shape in grads],
            scalars=3,
            name="unit_and_weights",
        )
        return made, Chain(sharing, keep, send), Chain(sharing, other_keep, other_send)

    r0, r1 = lower.rows, upper.rows
    za, suma = call(
        functools.partial(first_a, lower), where + [x, points[0][0]],
        [struct((r0, 384), F32), struct((3, 384), F32)], name="first_a",
    )
    suma = sum_all(suma, sizes)
    zb, sumb = call(
        functools.partial(first_b, lower), where + [x, points[0][1]],
        [struct((r0, 384), F32), struct((2, 384), F32)], [around(lower, 1)], name="first_b",
    )
    wide, thin, zc, sums = forward(lower, za, suma, sumb, 0)
    sums = sum_all(sums, sizes)
    q, za2, zb2, suma2, sumb2 = call(
        functools.partial(finish_lower, lower, upper),
        where + [zb, zc, suma, sums, pars[0][1], *points[1]],
        [struct((r1, 896), LOW), struct((r1, 384), F32), struct((r1, 384), F32), struct((3, 384), F32), struct((2, 384), F32)],
        [around(upper, 1), pltpu.VMEM((lower.frame, 1792), LOW)],
        name="finish_lower",
    )
    suma2 = sum_all(suma2, sizes)
    wide2, thin2, zc2, sums2 = forward(upper, za2, suma2, sumb2, 1)
    sums2 = sum_all(sums2, sizes)
    out, gu2, back2 = call(
        functools.partial(finish_upper, upper),
        where + [zb2, zc2, suma2, sums2, pars[1][1], cot],
        [struct((r1, 896), LOW), struct((r1, 896), F32), struct((2, 896), F32)],
        name="finish_upper",
    )
    back2 = sum_all(back2, sizes)
    dzb2, three2, thin32 = unit_back(upper, gu2, zb2, zc2, suma2, sums2, back2, 1)
    gua2, backa2 = conv_back(upper, three2, thin32, za2, suma2, 1)
    small = Sum(backa2, sizes)
    small.step()
    one = make_weights(0, [(0, 2), (2, 2), (4, 2), (6, 2)], "wo", wide2, three2, thin2, thin32, q, dzb2)
    meet(small, one)
    small.step()
    advance(one)
    meet(small, one)
    backa2 = small.result()
    advance(one)
    dza2, gu, back = call(
        functools.partial(join_blocks, upper, lower),
        where + [gua2, za2, suma2, backa2, pars[1][0], dzb2, *points[1], zb, zc, suma, sums, pars[0][1]],
        [struct((r1, 384), LOW), struct((r0, 896), F32), struct((2, 896), F32)],
        [pltpu.VMEM((lower.frame, 896), F32)],
        name="join_blocks",
    )
    held = Held(sum_all(back, sizes))
    meet(held, one)
    back = held.array
    advance(one)
    (dzb, three, thin3), two, more = unit_and_first(
        lower, gu, zb, zc, suma, sums, back, 0, wide, dza2, q, thin, x
    )
    held = Held(three)
    meet(one, two, more, held)
    advance(one)
    advance(two)
    advance(more)
    advance(two)
    gua, backa = conv_back(lower, held.array, thin3, za, suma, 0)
    small = Sum(backa, sizes)
    meet(two, more, small)
    more.half()
    small.step()
    small.step()
    meet(one, more, small)
    advance(one)
    more.half()
    advance(two)
    backa = small.result()
    dza, da = call(
        functools.partial(last_back, lower),
        where + [gua, za, suma, backa, pars[0][0], dzb, *points[0]],
        [struct((r0, 384), LOW), struct((r0, 832), LOW)],
        name="last_back",
    )
    held = Held(dza)
    meet(one, two, more, held)
    final = make_weights(3, [], "l", held.array, x, short=True)
    advance(one, two, more)
    advance(final)
    meet(one, two, more, final)
    advance(one, two, more, final)
    meet(one, two, more, final)
    advance(one, more, final)
    advance(two)
    advance(two)
    meet(one, two, more, final)
    joined = Held(assemble_call(me, [(PARTS[0], one.result())], [(which, 1, 0, 0) for which in (SINGLE, SPATIAL, NARROW, PROJECT)], None))
    advance(two, more, final)
    meet(two, more, final, joined)
    joined.array = assemble_call(
        me, [(PARTS[1], two.result())], [(SPATIAL, 0, 0, 18), (REDUCE, 1, 0, 0), (SQUEEZE, 1, 0, 0)], list(joined.array)
    )
    da = Held(frames_back(da.reshape(lower.frames, lower.frame, width), lower))
    out = jnp.concatenate([out[:, 0:576], out[:, 640:896]], axis=1)
    out = out.reshape(upper.frames, upper.frame, width)[:, 0 : upper.side * upper.side]
    out = Held(frames_back(out, upper))
    advance(more, final)
    meet(more, final, joined, da, out)
    advance(more, final)
    joined = list(joined.array)
    joined = list(assemble_call(
        me,
        [(PARTS[2], more.result()), (PARTS[3], final.result())],
        [(SPATIAL, 0, 18, 9)] + [(which, 0, 0, 0) for which in (SINGLE, REDUCE, SQUEEZE, NARROW, PROJECT)],
        joined,
    ))
    joined[REDUCE], joined[SQUEEZE] = (jnp.swapaxes(joined[which], 1, 2) for which in (REDUCE, SQUEEZE))
    joined = [value.reshape(kernel.shape) for value, kernel in zip(joined, kernels)]
    both = jnp.stack([unfit_vectors(backa, back), unfit_vectors(backa2, back2)])
    return (
        out.array,
        da.array,
        *joined,
        both[:, 1],
        both[:, 0],
    )


def solution(mesh):
    split = P(AXES, None, None, None, None)
    sizes = tuple(mesh.shape[axis] for axis in AXES)
    return jax.shard_map(
        functools.partial(shards, sizes),
        mesh=mesh,
        in_specs=(split, split, P(AXES)) + (P(),) * 9,
        out_specs=(split, split) + (P(),) * 8,
        check_vma=False,
    )
```

```python
import functools

import jax
import jax.numpy as jnp
from jax import lax
from jax.experimental import pallas as pl
from jax.experimental.pallas import tpu as pltpu
from jax.sharding import PartitionSpec as P

AXES = ("dp", "rep")
F32 = jnp.float32
LOW = jnp.bfloat16
EDGE = 32
TAPS = [(dh, dw) for dh in (-1, 0, 1) for dw in (-1, 0, 1)]
UNIT_TILES = [("b", 0), ("b", 1), ("c", 0), ("c", 1), ("c", 2), ("c", 3), ("b", 2)]
VMEM = pl.BlockSpec(memory_space=pltpu.VMEM)
SMEM = pl.BlockSpec(memory_space=pltpu.SMEM)
MIB = 1024 * 1024


def struct(shape, kind):
    return jax.ShapeDtypeStruct(shape, kind)


def scoped(scratch, room):
    total = 0
    for item in scratch:
        if isinstance(item, jax.core.ShapedArray) or hasattr(item, "shape"):
            shape = item.shape
            if len(shape) >= 2:
                size = -(-shape[-1] // 128) * 128 * -(-shape[-2] // 8) * 8 * jnp.dtype(item.dtype).itemsize
                for n in shape[:-2]:
                    size *= n
                total += size
    return total + room * MIB


def with_fetch(body, scalars, fetch, late, many_ins, many_outs, *refs):
    ins, outs = list(refs[0:many_ins]), refs[many_ins : many_ins + many_outs]
    scratch = list(refs[many_ins + many_outs :])
    sems = scratch.pop()
    moved = fetch + late
    parts = scratch[len(scratch) - len(moved) :]
    scratch = scratch[0 : len(scratch) - len(moved)]
    copies = [pltpu.make_async_copy(ins[i], part, sems.at[k]) for k, (i, part) in enumerate(zip(moved, parts))]
    for copy in copies:
        copy.start()
    for copy in copies[0 : len(fetch)]:
        copy.wait()
    for i, part in zip(moved, parts):
        ins[i] = part

    def ready():
        for copy in copies[len(fetch) :]:
            copy.wait()

    body(*ins, *outs, *scratch, **({"ready": ready} if late else {}))


def call(body, ins, outs, scratch=(), scalars=2, room=3, name=None, fetch=(), late=()):
    fetch, late, scratch = list(fetch), list(late), list(scratch)
    specs = [SMEM] * scalars + [VMEM] * (len(ins) - scalars)
    if fetch or late:
        body = functools.partial(with_fetch, body, scalars, fetch, late, len(ins), len(outs))
        for i in fetch + late:
            specs[i] = pl.BlockSpec(memory_space=pl.ANY)
            scratch.append(pltpu.VMEM(ins[i].shape, ins[i].dtype))
    limit = scoped(scratch, room)
    if fetch or late:
        scratch.append(pltpu.SemaphoreType.DMA((len(fetch) + len(late),)))
    return pl.pallas_call(
        body,
        out_shape=tuple(outs),
        in_specs=specs,
        out_specs=tuple([VMEM] * len(outs)),
        scratch_shapes=scratch,
        compiler_params=pltpu.CompilerParams(vmem_limit_bytes=limit),
        cost_estimate=pl.CostEstimate(flops=1, bytes_accessed=1, transcendentals=0),
        name=name,
    )(*ins)


def tile(index, width=1):
    return slice(index * 128, (index + width) * 128)


def lanes():
    return lax.broadcasted_iota(jnp.int32, (1, 128), 1)


def sigmoid(v):
    return 0.5 * jnp.tanh(0.5 * v) + 0.5


def places(frame, side):
    at = lax.broadcasted_iota(jnp.int32, (frame, 1), 0).astype(F32)
    row = jnp.floor((at + 0.5) * (1.0 / side))
    return row, at - row * side


def crop_mask(frame, side, crop):
    row, column = places(frame, side)
    return jnp.where((row < crop) & (column < crop), 1.0, 0.0).astype(F32)


def column_mask(frame, side, step):
    row, column = places(frame, side)
    inside = (column + step > -0.5) & (column + step < side - 0.5)
    return jnp.where(inside, 1.0, 0.0).astype(F32)


def crop_of(group_ref, sides_ref, halved):
    crop = sides_ref[group_ref[0]]
    if halved:
        crop = lax.shift_right_logical(crop, 1)
    return crop.astype(F32)


def moments(sums, count):
    mean = sums[0:1] / count
    square = sums[1:2] / count
    return mean, lax.rsqrt(square - mean * mean + 1e-05)


def back_terms(sums, count, gamma, inverse):
    scale = gamma * inverse
    return scale, scale * (sums[0:1] / count), scale * (sums[1:2] / count)


def add_sums(ref, at, first, second):
    ref[0:1, at] += jnp.sum(first, axis=0, keepdims=True)
    ref[1:2, at] += jnp.sum(second, axis=0, keepdims=True)


def neighbour_sum(values, around, frame, side, put):
    frames = len(values)
    left = column_mask(frame, side, -1)
    right = column_mask(frame, side, 1)
    for t in range(frames):
        total = values[t]
        if t > 0:
            total = total + values[t - 1]
        if t < frames - 1:
            total = total + values[t + 1]
        around[0, EDGE : EDGE + frame, :] = total
        total = (
            total
            + around[0, EDGE - side : EDGE - side + frame, :]
            + around[0, EDGE + side : EDGE + side + frame, :]
        )
        around[0, EDGE : EDGE + frame, :] = total
        total = (
            total
            + around[0, EDGE - 1 : EDGE - 1 + frame, :] * left
            + around[0, EDGE + 1 : EDGE + 1 + frame, :] * right
        )
        put(t, total * (1.0 / 27.0))


def clear_edges(around, frame):
    tiles = around.shape[0]
    around[:, 0:EDGE, :] = jnp.zeros((tiles, EDGE, 128), F32)
    around[:, EDGE + frame : 2 * EDGE + frame, :] = jnp.zeros((tiles, EDGE, 128), F32)


def dot(a, b):
    return lax.dot_general(a, b, (((1,), (0,)), ((), ())), preferred_element_type=F32)


def dot_nt(a, b):
    return lax.dot_general(a, b, (((1,), (1,)), ((), ())), preferred_element_type=F32)


def dot_tn(a, b):
    return lax.dot_general(a, b, (((0,), (0,)), ((), ())), preferred_element_type=F32)


class Layer:
    def __init__(self, frames, side, halved):
        self.frames = frames
        self.side = side
        self.halved = halved
        self.frame = -(-side * side // 16) * 16
        self.rows = frames * self.frame

    def at(self, t):
        return slice(t * self.frame, (t + 1) * self.frame)


def point_a(layer, mask, x_ref, w_ref, za_ref, sums_ref):
    sums_ref[...] = jnp.zeros(sums_ref.shape, F32)
    for t in range(layer.frames):
        z = dot_nt(x_ref[layer.at(t), :], w_ref[...])
        za_ref[layer.at(t), :] = z
        for j in range(3):
            part = z[:, tile(j)] * mask
            add_sums(sums_ref, tile(j), part, part * z[:, tile(j)])
    cells = jnp.sum(mask, axis=0, keepdims=True) * layer.frames
    sums_ref[2:3, :] = jnp.broadcast_to(cells, (1, 384))


def point_b(layer, mask, x_ref, kernels, zb_ref, sums_ref, around):
    sums_ref[...] = jnp.zeros(sums_ref.shape, F32)
    clear_edges(around, layer.frame)
    flat = []
    for t in range(layer.frames):
        source = x_ref[layer.at(t), :]
        z = dot(source, kernels[0])
        zb_ref[layer.at(t), 0:256] = z
        zb_ref[layer.at(t), tile(2)] = dot(source, kernels[1]) * mask
        for j in range(2):
            part = z[:, tile(j)] * mask
            add_sums(sums_ref, tile(j), part, part * z[:, tile(j)])
    flat = [zb_ref[layer.at(t), tile(2)] for t in range(layer.frames)]

    def put(t, value):
        zb_ref[layer.at(t), tile(2)] = value
        part = value * mask
        add_sums(sums_ref, tile(2), part, part * value)

    neighbour_sum(flat, around, layer.frame, layer.side, put)


def first_a(layer, group_ref, sides_ref, x_ref, reduce_ref, squeeze_ref, za_ref, sums_ref, wa_ref):
    mask = crop_mask(layer.frame, layer.side, crop_of(group_ref, sides_ref, layer.halved))
    side_by_side(reduce_ref[0], squeeze_ref[0], wa_ref)
    point_a(layer, mask, x_ref, wa_ref, za_ref, sums_ref)


def first_b(layer, group_ref, sides_ref, x_ref, single_ref, project_ref, zb_ref, sums_ref, around):
    mask = crop_mask(layer.frame, layer.side, crop_of(group_ref, sides_ref, layer.halved))
    point_b(layer, mask, x_ref, [single_ref[0], project_ref[0]], zb_ref, sums_ref, around)


def conv_forward(
    layer, group_ref, sides_ref, za_ref, suma_ref, para_ref, sumb_ref, w_ref, wn_ref,
    wide_ref, thin_ref, zc_ref, sums_ref, around, rem,
):
    frames, frame, side = layer.frames, layer.frame, layer.side
    mask = crop_mask(frame, side, crop_of(group_ref, sides_ref, layer.halved))
    count = suma_ref[2:3, :]
    mean, inverse = moments(suma_ref, count)
    gain = para_ref[0:1, :] * inverse
    offset = para_ref[1:2, :] - mean * gain
    column = [column_mask(frame, side, dw) for dw in (-1, 0, 1)]
    part_of = lanes() // 32
    clear_edges(around, frame)
    for t in range(frames):
        rows = layer.at(t)
        for j in range(3):
            u = za_ref[rows, tile(j)] * gain[:, tile(j)] + offset[:, tile(j)]
            around[j, EDGE : EDGE + frame, :] = u * sigmoid(u) * mask
        mixed = {1: [None] * 3, 2: [None] * 3}
        for k, (dh, dw) in enumerate(TAPS):
            start = EDGE + dh * side + dw
            shifted = around[0, start : start + frame, :]
            if dw:
                shifted = shifted * column[dw + 1]
            wide_ref[rows, tile(k)] = shifted.astype(LOW)
            for j in (1, 2):
                shifted = around[j, start : start + frame, :]
                if dw:
                    shifted = shifted * column[dw + 1]
                shifted = jnp.where(part_of == k % 4, shifted, 0.0)
                held = mixed[j][k // 4]
                mixed[j][k // 4] = shifted if held is None else held + shifted
        for g in range(3):
            wide_ref[rows, tile(9 + g)] = mixed[1][g].astype(LOW)
            thin_ref[rows, tile(g)] = mixed[2][g].astype(LOW)
    sums_ref[:, 0:384] = sumb_ref[...]
    sums_ref[:, 384:896] = jnp.zeros((2, 512), F32)
    zc_ref[...] = jnp.zeros(zc_ref.shape, F32)
    for t in range(frames):
        source = wide_ref[layer.at(t), :]
        thin = thin_ref[layer.at(t), :]
        for k in range(3):
            to = t + 1 - k
            if 0 <= to < frames:
                rows = layer.at(to)
                zc_ref[rows, 0:256] += dot(source, w_ref[:, k * 256 : (k + 1) * 256])
                zc_ref[rows, tile(3)] += dot(thin, wn_ref[:, tile(k)])
        rem[layer.at(t), :] = dot(source, w_ref[:, 768:1024])
    for t in range(frames):
        rows = layer.at(t)
        total = pltpu.roll(rem[rows, 0:128], 64, 1)
        if t > 0:
            total = total + rem[layer.at(t - 1), 0:128]
        if t < frames - 1:
            total = total + rem[layer.at(t + 1), 128:256]
        zc_ref[rows, tile(2)] = jnp.where(lanes() < 64, total, 0.0)
        for j in range(4):
            z = zc_ref[rows, tile(j)]
            part = z * mask
            add_sums(sums_ref, tile(3 + j), part, part * z)


class Norms:
    def __init__(self, sums_ref, par_ref, count):
        mean, inverse = moments(sums_ref, count)
        self.mean, self.inverse = mean, inverse
        self.gamma, self.beta = par_ref[0:1, :], par_ref[1:2, :]

    def lane(self, kind, j):
        return tile(j if kind == "b" else 3 + j)

    def normed(self, z, at):
        return (z - self.mean[:, at]) * self.inverse[:, at]

    def shifted(self, n, at):
        return self.gamma[:, at] * n + self.beta[:, at]


def finish_lower(
    lower, upper, group_ref, sides_ref, zb_ref, zc_ref, suma_ref, sums_ref, par_ref, wa_ref, wb_ref,
    q_ref, za2_ref, zb2_ref, suma2_ref, sumb2_ref, around, y_ref,
):
    crop = crop_of(group_ref, sides_ref, False)
    mask = crop_mask(lower.frame, lower.side, crop)
    norms = Norms(sums_ref, par_ref, suma_ref[2:3, 0:1])
    pick = pair_matrix(upper, lower)
    for t in range(upper.frames):
        for index, (kind, j) in enumerate(UNIT_TILES):
            at = norms.lane(kind, j)
            z_ref = zb_ref if kind == "b" else zc_ref
            total = None
            for source in (2 * t, 2 * t + 1):
                u = norms.shifted(norms.normed(z_ref[lower.at(source), tile(j)], at), at)
                out = u * sigmoid(u) * mask
                total = out if total is None else total + out
            high = total.astype(LOW)
            y_ref[:, tile(index)] = high
            y_ref[:, tile(7 + index)] = (total - high.astype(F32)).astype(LOW)
        both = dot(pick, y_ref[...])
        q_ref[upper.at(t), :] = (both[:, 0:896] + both[:, 896:1792]).astype(LOW)
    small = crop_mask(upper.frame, upper.side, crop_of(group_ref, sides_ref, True))
    point_a(upper, small, q_ref, wa_ref, za2_ref, suma2_ref)
    point_b(upper, small, q_ref, [wb_ref[:, 0:256], wb_ref[:, 256:384]], zb2_ref, sumb2_ref, around)


def pair_matrix(upper, lower):
    at = lax.broadcasted_iota(jnp.int32, (upper.frame, lower.frame), 1).astype(F32)
    row = jnp.floor((at + 0.5) * (1.0 / lower.side))
    column = at - row * lower.side
    group = jnp.floor(row * 0.5 + 0.25) * upper.side + jnp.floor(column * 0.5 + 0.25)
    mine = lax.broadcasted_iota(jnp.int32, (upper.frame, lower.frame), 0).astype(F32)
    return jnp.where(jnp.abs(group - mine) < 0.5, 0.125, 0.0).astype(LOW)


def spread_matrix(upper, lower):
    at = lax.broadcasted_iota(jnp.int32, (lower.frame, upper.frame), 0).astype(F32)
    row = jnp.floor((at + 0.5) * (1.0 / lower.side))
    column = at - row * lower.side
    group = jnp.floor(row * 0.5 + 0.25) * upper.side + jnp.floor(column * 0.5 + 0.25)
    mine = lax.broadcasted_iota(jnp.int32, (lower.frame, upper.frame), 1).astype(F32)
    return jnp.where(jnp.abs(group - mine) < 0.5, 0.125, 0.0).astype(LOW)


def finish_upper(
    layer, group_ref, sides_ref, zb_ref, zc_ref, suma_ref, sums_ref, par_ref, cot_ref,
    out_ref, gu_ref, back_ref,
):
    mask = crop_mask(layer.frame, layer.side, crop_of(group_ref, sides_ref, layer.halved))
    norms = Norms(sums_ref, par_ref, suma_ref[2:3, 0:1])
    back_ref[...] = jnp.zeros(back_ref.shape, F32)
    for t in range(layer.frames):
        rows = layer.at(t)
        for index, (kind, j) in enumerate(UNIT_TILES):
            at = norms.lane(kind, j)
            z_ref = zb_ref if kind == "b" else zc_ref
            n = norms.normed(z_ref[rows, tile(j)], at)
            u = norms.shifted(n, at)
            s = sigmoid(u)
            out_ref[rows, tile(index)] = (u * s * mask).astype(LOW)
            gu = cot_ref[rows, tile(index)].astype(F32) * mask * (s * (1.0 + u * (1.0 - s)))
            gu_ref[rows, tile(index)] = gu
            add_sums(back_ref, at, gu, gu * n)


def unit_backward(
    layer, group_ref, sides_ref, gu_ref, zb_ref, zc_ref, suma_ref, sums_ref, back_ref, par_ref,
    dzb_ref, three_ref, thin3_ref, around, flat,
):
    frames, frame, side = layer.frames, layer.frame, layer.side
    mask = crop_mask(frame, side, crop_of(group_ref, sides_ref, layer.halved))
    count = suma_ref[2:3, 0:1]
    norms = Norms(sums_ref, par_ref, count)
    c0, c1, c2 = back_terms(back_ref, count, norms.gamma, norms.inverse)
    low_half = lanes() < 64

    def dz_of(t, index):
        kind, j = UNIT_TILES[index]
        at = norms.lane(kind, j)
        z_ref = zb_ref if kind == "b" else zc_ref
        rows = layer.at(t)
        n = norms.normed(z_ref[rows, tile(j)], at)
        return (gu_ref[rows, tile(index)] * c0[:, at] - c1[:, at] - n * c2[:, at]) * mask

    clear_edges(around, frame)
    for t in range(frames):
        for index in (0, 1):
            dzb_ref[layer.at(t), tile(index)] = dz_of(t, index).astype(LOW)
        flat[layer.at(t), :] = dz_of(t, 6)

    def put(t, value):
        dzb_ref[layer.at(t), tile(2)] = (value * mask).astype(LOW)

    neighbour_sum([flat[layer.at(t), :] for t in range(frames)], around, frame, side, put)
    for t in range(frames):
        flat[layer.at(t), :] = jnp.where(low_half, dz_of(t, 4), 0.0)
    empty = jnp.zeros((frame, 128), LOW)
    for t in range(frames):
        parts = [dz_of(t, index).astype(LOW) for index in (2, 3, 5)]
        for k in range(3):
            to = t - 1 + k
            if 0 <= to < frames:
                rows = layer.at(to)
                three_ref[rows, tile(2 * k)] = parts[0]
                three_ref[rows, tile(2 * k + 1)] = parts[1]
                thin3_ref[rows, tile(k)] = parts[2]
        rest = pltpu.roll(flat[layer.at(t), :], 64, 1)
        if t < frames - 1:
            rest = rest + flat[layer.at(t + 1), :]
        three_ref[layer.at(t), tile(6)] = rest.astype(LOW)
        three_ref[layer.at(t), tile(7)] = flat[layer.at(t - 1), :].astype(LOW) if t else empty
    for rows, k in ((layer.at(0), 2), (layer.at(frames - 1), 0)):
        three_ref[rows, tile(2 * k)] = empty
        three_ref[rows, tile(2 * k + 1)] = empty
        thin3_ref[rows, tile(k)] = empty


def unit_and_weights(
    layer, parts, columns, group_ref, sides_ref, me_ref, gu_ref, zb_ref, zc_ref, suma_ref, sums_ref, back_ref, par_ref,
    wide_ref, dza_ref, q_ref, thin_ref, x_ref, dzb_ref, three_ref, thin3_ref, keep_ref, send_ref, other_keep_ref,
    other_send_ref, around, flat, wide_grad, last_grad, other_wide_grad, thin_grad, point_grad,
):
    unit_backward(
        layer, group_ref, sides_ref, gu_ref, zb_ref, zc_ref, suma_ref, sums_ref, back_ref, par_ref,
        dzb_ref, three_ref, thin3_ref, around, flat,
    )
    weights(
        parts[0], columns[0], "wl", me_ref, wide_ref, three_ref, dza_ref, q_ref, keep_ref, send_ref, wide_grad, last_grad
    )
    weights(
        parts[1], columns[1], "wo", me_ref, wide_ref, three_ref, thin_ref, thin3_ref, x_ref, dzb_ref, other_keep_ref,
        other_send_ref, other_wide_grad, thin_grad, point_grad,
    )


def conv_backward(
    layer, group_ref, sides_ref, three_ref, thin3_ref, za_ref, suma_ref, para_ref, wt_ref, wnt_ref,
    gua_ref, backa_ref, around, shifts, thins, rem, main, ready=lambda: None,
):
    frames, frame, side = layer.frames, layer.frame, layer.side
    mask = crop_mask(frame, side, crop_of(group_ref, sides_ref, layer.halved))
    column = [column_mask(frame, side, dw) for dw in (-1, 0, 1)]
    low_half = lanes() < 64
    first_part = lanes() < 32
    clear_edges(around, frame)
    main[...] = jnp.zeros(main.shape, F32)
    rem[...] = jnp.zeros(rem.shape, F32)
    for t in range(frames):
        rows = layer.at(t)
        rest = jnp.where(low_half, 0.0, three_ref[rows, tile(6)].astype(F32))
        parts = [
            three_ref[rows, tile(2)].astype(F32),
            three_ref[rows, tile(3)].astype(F32),
            rest + pltpu.roll(rest, 64, 1),
            thin3_ref[rows, tile(1)].astype(F32),
        ]
        for j in range(4):
            around[j, EDGE : EDGE + frame, :] = parts[j]
        mixed = [None] * 5
        for k, (dh, dw) in enumerate(TAPS):
            start = EDGE - dh * side - dw
            for j in range(4):
                shifted = around[j, start : start + frame, :]
                if dw:
                    shifted = shifted * column[1 - dw]
                if j < 2:
                    shifts[:, tile(2 * k + j)] = shifted.astype(LOW)
                elif j == 3:
                    thins[:, tile(k)] = shifted.astype(LOW)
                else:
                    shifted = jnp.where(low_half if k % 2 == 0 else ~low_half, shifted, 0.0)
                    held = mixed[k // 2]
                    mixed[k // 2] = shifted if held is None else held + shifted
        for g in range(5):
            shifts[:, tile(18 + g)] = mixed[g].astype(LOW)
        if t == 0:
            ready()
        product = dot_nt(shifts[...], wt_ref[...])
        thin = dot_nt(thins[...], wnt_ref[...])
        for k in range(3):
            to = t - 1 + k
            if 0 <= to < frames:
                rows = layer.at(to)
                main[rows, :] += product[:, tile(k)]
                turn = (128 - 32 * k) % 128
                last = product[:, tile(3)]
                rem[rows, 0:128] += last if turn == 0 else pltpu.roll(last, turn, 1)
                rem[rows, 128:256] += thin if turn == 0 else pltpu.roll(thin, turn, 1)
    mean, inverse = moments(suma_ref, suma_ref[2:3, :])
    backa_ref[...] = jnp.zeros(backa_ref.shape, F32)
    for t in range(frames):
        rows = layer.at(t)
        for j in range(3):
            grad = main[rows, :] if j == 0 else rem[rows, tile(j - 1)]
            n = (za_ref[rows, tile(j)] - mean[:, tile(j)]) * inverse[:, tile(j)]
            u = para_ref[0:1, tile(j)] * n + para_ref[1:2, tile(j)]
            s = sigmoid(u)
            gu = grad * mask * (s * (1.0 + u * (1.0 - s)))
            if j:
                gu = jnp.where(first_part, gu, 0.0)
            gua_ref[rows, tile(j)] = gu
            add_sums(backa_ref, tile(j), gu, gu * n)


def point_back(layer, mask, gua_ref, za_ref, suma_ref, backa_ref, para_ref, dza_ref):
    count = suma_ref[2:3, :]
    mean, inverse = moments(suma_ref, count)
    c0, c1, c2 = back_terms(backa_ref, count, para_ref[0:1, :], inverse)
    for t in range(layer.frames):
        rows = layer.at(t)
        for j in range(3):
            at = tile(j)
            n = (za_ref[rows, at] - mean[:, at]) * inverse[:, at]
            dz = (gua_ref[rows, at] * c0[:, at] - c1[:, at] - n * c2[:, at]) * mask
            if j:
                dz = jnp.where(lanes() < 32, dz, 0.0)
            dza_ref[rows, at] = dz.astype(LOW)


def join_blocks(
    upper, lower, group_ref, sides_ref, gua_ref, za_ref, suma_ref, backa_ref, para_ref, dzb_ref, wa_ref, wb_ref,
    zb_ref, zc_ref, suma1_ref, sums1_ref, par1_ref, dza_ref, gu_ref, back_ref, wide,
):
    small = crop_mask(upper.frame, upper.side, crop_of(group_ref, sides_ref, True))
    point_back(upper, small, gua_ref, za_ref, suma_ref, backa_ref, para_ref, dza_ref)
    mask = crop_mask(lower.frame, lower.side, crop_of(group_ref, sides_ref, False))
    norms = Norms(sums1_ref, par1_ref, suma1_ref[2:3, 0:1])
    back_ref[...] = jnp.zeros(back_ref.shape, F32)
    pick = spread_matrix(upper, lower)
    for t in range(upper.frames):
        rows = upper.at(t)
        dq = dot_nt(dzb_ref[rows, :], wb_ref[...]) + dot(dza_ref[rows, :], wa_ref[...])
        high = dq.astype(LOW)
        rest = (dq - high.astype(F32)).astype(LOW)
        wide[...] = dot(pick, high) + dot(pick, rest)
        for source in (2 * t, 2 * t + 1):
            at_rows = lower.at(source)
            for index, (kind, j) in enumerate(UNIT_TILES):
                at = norms.lane(kind, j)
                z_ref = zb_ref if kind == "b" else zc_ref
                n = norms.normed(z_ref[at_rows, tile(j)], at)
                u = norms.shifted(n, at)
                s = sigmoid(u)
                gu = wide[:, tile(index)] * mask * (s * (1.0 + u * (1.0 - s)))
                gu_ref[at_rows, tile(index)] = gu
                add_sums(back_ref, at, gu, gu * n)


def last_back(
    layer, group_ref, sides_ref, gua_ref, za_ref, suma_ref, backa_ref, para_ref, dzb_ref, wa_ref, single_ref, project_ref, dza_ref, grad_ref,
):
    mask = crop_mask(layer.frame, layer.side, crop_of(group_ref, sides_ref, layer.halved))
    point_back(layer, mask, gua_ref, za_ref, suma_ref, backa_ref, para_ref, dza_ref)
    for t in range(layer.frames):
        rows = layer.at(t)
        total = dot_nt(dzb_ref[rows, 0:256], single_ref[0]) + dot_nt(dzb_ref[rows, 256:384], project_ref[0])
        total = total + dot(dza_ref[rows, :], wa_ref[...])
        grad_ref[rows, :] = (total * mask).astype(LOW)


def place(me, pair, core):
    bits = lax.shift_right_logical(me, 1) ^ pair
    x, y = bits & 1, lax.shift_right_logical(bits, 1) & 1
    near, far = lax.shift_right_logical(bits, 2) & 1, lax.shift_right_logical(bits, 3) & 1
    first = x + core * (y - x)
    second = y + core * (x - y)
    return first * 8 + second * 4 + near * 2 + far


def put_pair(me, keep_ref, send_ref, pair, rows, even, odd):
    core = me & 1
    mine = core == 0
    keep_ref[place(me, pair, core), rows, :] = jnp.where(mine, even, odd)
    send_ref[place(me, pair, 1 - core), rows, :] = jnp.where(mine, odd, even)


def get_pair(me, own_ref, other_ref, pair, rows):
    core = me & 1
    mine = core == 0
    own = own_ref[place(me, pair, core), rows, :]
    other = other_ref[place(me, pair, 1 - core), rows, :]
    return jnp.where(mine, own, other), jnp.where(mine, other, own)


def segments(blocks):
    rows = -(-sum(length for _, length in blocks) // 256) * 8
    pieces, piece, room = [], [], rows
    for name, length in blocks:
        at = 0
        while at < length:
            take = min(room, length - at)
            piece.append((name, at, at + take, rows - room))
            at += take
            room -= take
            if not room:
                pieces.append(piece)
                piece, room = [], rows
    if piece:
        pieces.append(piece)
    return rows, pieces + [[]] * (32 - len(pieces))


def wide(layer, *tiles):
    return [(("wide", j, layer), 720 if j == 7 else 1440) for j in tiles]


def point_and_thin(layer):
    return [(("point", j, layer), 832) for j in range(3)] + [(("thin", j, layer), 288) for j in range(3)]


def last(layer):
    return [(("last", j, layer), 96 if j == 6 else 192) for j in range(7)]


PARTS = [
    segments(wide(1, *range(8)) + point_and_thin(1)),
    segments(wide(0, 0, 1, 2, 3, 6) + last(1)),
    segments(wide(0, 4, 5, 7) + point_and_thin(0)),
    segments(last(0)),
]


def piece_value(piece, rows, read):
    parts = [read(name, first, end) for name, first, end, _ in piece]
    filled = sum(end - first for _, first, end, _ in piece)
    if filled < rows:
        parts.append(jnp.zeros((rows - filled, 128), F32))
    return parts[0] if len(parts) == 1 else jnp.concatenate(parts, axis=0)


def put_pieces(me, keep_ref, send_ref, part, read):
    rows, pieces = part
    for pair in range(16):
        even, odd = (piece_value(pieces[2 * pair + i], rows, read) for i in (0, 1))
        put_pair(me, keep_ref, send_ref, pair, slice(0, rows), even, odd)


def fold(ref, at, rows):
    value = jnp.where(lanes() < 64, ref[0 : 2 * rows, at], 0.0)
    ref[0:rows, at] = value[0:rows] + pltpu.roll(value[rows : 2 * rows], 64, 1)


def without_gap(ref, grad):
    if grad.shape[0] == 896:
        ref[0:576, :] = grad[0:576]
        ref[576:832, :] = grad[640:896]
    else:
        ref[...] = grad


def weights(part, columns, kinds, me_ref, *refs):
    refs = list(refs)
    read_from = {}
    operands = [refs.pop(0) for _ in range({"w": 2, "o": 4, "l": 2}[kinds[0]] + (0 if len(kinds) == 1 else {"o": 4, "l": 2}[kinds[1]]))]
    keep_ref, send_ref = refs.pop(0), refs.pop(0)
    for kind in kinds:
        if kind == "w":
            wide_ref, three_ref = operands.pop(0), operands.pop(0)
            grad = refs.pop(0)
            at = 0
            for first, count in columns:
                grad[:, tile(at, count)] = dot_tn(wide_ref[:, 0:1440], three_ref[:, tile(first, count)])
                for j in range(count):
                    read_from["wide", first + j] = (grad, at + j)
                    if first + j == 7:
                        fold(grad, tile(at + j), 720)
                at += count
        elif kind == "o":
            thin_ref, thin3_ref, x_ref, dzb_ref = (operands.pop(0) for _ in range(4))
            thin_grad, point_grad = refs.pop(0), refs.pop(0)
            thin_grad[...] = dot_tn(thin_ref[...], thin3_ref[...])
            without_gap(point_grad, dot_tn(x_ref[...], dzb_ref[...]))
            for j in range(3):
                read_from["point", j] = (point_grad, j)
                read_from["thin", j] = (thin_grad, j)
        else:
            dza_ref, x_ref = operands.pop(0), operands.pop(0)
            last_grad = refs.pop(0)
            grad = dot_tn(dza_ref[...], x_ref[...])
            if grad.shape[1] == 896:
                grad = close_gap(grad)
            width = grad.shape[1]
            last_grad[0:160, 0:width] = grad[0:160]
            last_grad[160:192, 0:width] = grad[256:288]
            if width < 896:
                last_grad[:, width:896] = jnp.zeros((192, 896 - width), F32)
            fold(last_grad, tile(6), 96)
            for j in range(7):
                read_from["last", j] = (last_grad, j)

    def read(name, first, end):
        ref, j = read_from[name[0:2]]
        return ref[first:end, tile(j)]

    put_pieces(me_ref[0], keep_ref, send_ref, part, read)


OUT_SHAPES = [(832, 256), (160, 832), (27, 160, 320), (32, 832), (27, 32, 128), (832, 128)]
SINGLE, REDUCE, SPATIAL, SQUEEZE, NARROW, PROJECT = range(6)


def assemble(sources, targets, aliased, me_ref, *refs):
    me = me_ref[0]
    many = sum(2 if relative else 1 for _, relative in sources)
    arrived, refs = list(refs[0:many]), refs[many + (6 if aliased else 0) :]
    outs, stages, sems = refs[0:6], refs[6 : 6 + len(targets)], refs[6 + len(targets)]
    stage = {(which, block): (ref, first) for (which, block, first, _), ref in zip(targets, stages)}

    def put_wide(block, k, lanes_at, first, value):
        ref, offset = stage[SPATIAL, block]
        done = 0
        while done < value.shape[0]:
            row = first + done
            if row < 1152:
                tap, channel = row // 128, row % 128
                take = min(128 - channel, value.shape[0] - done)
            else:
                tap, channel = (row - 1152) // 32, 128 + (row - 1152) % 32
                take = min(160 - channel, value.shape[0] - done)
            ref[k * 9 + tap - offset, channel : channel + take, lanes_at] = value[done : done + take]
            done += take

    def put_last(block, lanes_at, first, value):
        for which, low, high in ((REDUCE, 0, 160), (SQUEEZE, 160, 192)):
            begin, stop = max(first, low), min(first + value.shape[0], high)
            if begin < stop:
                stage[which, block][0][begin - low : stop - low, lanes_at] = value[begin - first : stop - first]

    def put(name, first, end, value):
        kind, j, block = name
        if kind == "wide":
            if j < 6:
                put_wide(block, j // 2, tile(j % 2), first, value)
            elif j == 6:
                put_wide(block, 0, slice(256, 320), first, value[:, 0:64])
                put_wide(block, 1, slice(256, 320), first, pltpu.roll(value, 64, 1)[:, 0:64])
            else:
                put_wide(block, 2, slice(256, 320), first, value[:, 0:64])
                put_wide(block, 2, slice(256, 320), first + 720, pltpu.roll(value, 64, 1)[:, 0:64])
        elif kind == "point":
            if j < 2:
                stage[SINGLE, block][0][first:end, tile(j)] = value
            else:
                stage[PROJECT, block][0][first:end, :] = value
        elif kind == "thin":
            done = 0
            while done < end - first:
                tap, channel = (first + done) // 32, (first + done) % 32
                take = min(32 - channel, end - first - done)
                stage[NARROW, block][0][j * 9 + tap, channel : channel + take, :] = value[done : done + take]
                done += take
        elif j < 6:
            put_last(block, tile(j), first, value)
        else:
            put_last(block, slice(768, 832), first, value[:, 0:64])
            put_last(block, slice(768, 832), first + 96, pltpu.roll(value, 64, 1)[:, 0:64])

    for (rows, pieces), relative in sources:
        held = [arrived.pop(0) for _ in range(2 if relative else 1)]
        for pair in range(16):
            if relative:
                both = get_pair(me, *held, pair, slice(0, rows))
            else:
                both = [held[0][2 * pair + i] for i in (0, 1)]
            for i in (0, 1):
                for name, first, end, row in pieces[2 * pair + i]:
                    put(name, first, end, both[i][row : row + end - first])
    copies = []
    for i, ((which, block, first, count), ref) in enumerate(zip(targets, stages)):
        to = outs[which].at[block]
        if count < OUT_SHAPES[which][0]:
            to = to.at[pl.ds(first, count)]
        copies.append(pltpu.make_async_copy(ref, to, sems.at[i]))
        copies[-1].start()
    for copy in copies:
        copy.wait()


def assemble_call(me, sources, targets, outs):
    anywhere = pl.BlockSpec(memory_space=pl.ANY)
    arrays = sum((list(found) for _, found in sources), [])
    targets = [(which, block, first, count or OUT_SHAPES[which][0]) for which, block, first, count in targets]
    scratch = [pltpu.VMEM((count,) + OUT_SHAPES[which][1:], F32) for which, _, _, count in targets]
    return pl.pallas_call(
        functools.partial(assemble, [(part, len(found) == 2) for part, found in sources], targets, outs is not None),
        out_shape=tuple(struct((2,) + shape, F32) for shape in OUT_SHAPES),
        in_specs=[SMEM] + [VMEM] * len(arrays) + [anywhere] * (0 if outs is None else 6),
        out_specs=tuple([anywhere] * 6),
        scratch_shapes=scratch + [pltpu.SemaphoreType.DMA((len(targets),))],
        input_output_aliases={} if outs is None else {1 + len(arrays) + i: i for i in range(6)},
        compiler_params=pltpu.CompilerParams(vmem_limit_bytes=scoped(scratch, 3)),
        cost_estimate=pl.CostEstimate(flops=1, bytes_accessed=1, transcendentals=0),
        name="assemble",
    )(me, *arrays, *([] if outs is None else outs))


def unfit_vectors(sums_a, sums):
    return jnp.concatenate(
        [sums[:, 0:256], sums_a[:, 0:160], sums[:, 384:704], sums_a[:, 256:288], sums[:, 768:896], sums[:, 256:384]], axis=1
    )


def open_gap(value):
    value = value.astype(F32)
    tiles = [value[:, tile(j)] for j in range(6)]
    tiles.append(jnp.concatenate([value[:, 768:832], jnp.zeros((value.shape[0], 64), F32)], axis=1))
    low_half = lanes() < 64
    turned = [pltpu.roll(part, 64, 1) for part in tiles[4:7]]
    tiles[4] = jnp.where(low_half, tiles[4], 0.0)
    tiles[5] = jnp.where(low_half, turned[0], turned[1])
    tiles[6] = jnp.where(low_half, turned[1], turned[2])
    return jnp.concatenate(tiles, axis=1).astype(LOW)


def close_gap(value):
    low_half = lanes() < 64
    tiles = [value[:, tile(j)] for j in range(7)]
    turned = [pltpu.roll(part, 64, 1) for part in tiles[5:7]]
    tiles[4] = jnp.where(low_half, tiles[4], turned[0])
    tiles[5] = jnp.where(low_half, turned[0], turned[1])
    tiles[6] = turned[1]
    return jnp.concatenate(tiles, axis=1)


def side_by_side(reduce, squeeze, wa_ref):
    wa_ref[0:128, :] = reduce[0:128]
    for i in range(4):
        wa_ref[128 + 32 * i : 160 + 32 * i, :] = reduce[128:160]
        wa_ref[256 + 32 * i : 288 + 32 * i, :] = squeeze


def fit_points(single_ref, project_ref, reduce_ref, squeeze_ref, wa_ref, wb_ref):
    gap = wa_ref.shape[1] == 896
    if gap:
        spans = [(slice(0, 576), slice(0, 576)), (slice(640, 896), slice(576, 832))]
        wb_ref[576:640, :] = jnp.zeros((64, 384), LOW)
    else:
        spans = [(slice(0, 832), slice(0, 832))]
    for to, source in spans:
        wb_ref[to, 0:256] = single_ref[0, source, :]
        wb_ref[to, 256:384] = project_ref[0, source, :]
    reduce, squeeze = reduce_ref[0], squeeze_ref[0]
    if gap:
        reduce, squeeze = open_gap(reduce), open_gap(squeeze)
    side_by_side(reduce, squeeze, wa_ref)


def pair_lanes(left, right):
    parts = [jnp.zeros((max(p.shape[0] for p in (left, right) if p is not None), 64), F32) if p is None else p.astype(F32) for p in (left, right)]
    return jnp.concatenate(parts, axis=1).astype(LOW)


def fit_forward(index, scale_ref, shift_ref, spatial_ref, narrow_ref, w_ref, wn_ref, para_ref, par_ref):
    spans = [(0, 128, 128 * tap, tap) for tap in range(9)] + [(128, 160, 1152 + 32 * tap, tap) for tap in range(9)]
    w_ref[1440:1536, :] = jnp.zeros((96, 1024), LOW)
    for first, end, row, tap in spans:
        rows = slice(row, row + end - first)
        rest = [spatial_ref[0, 9 * k + tap, first:end, 256:320] for k in range(3)]
        for k in range(3):
            w_ref[rows, k * 256 : (k + 1) * 256] = spatial_ref[0, 9 * k + tap, first:end, 0:256]
        w_ref[rows, 768:896] = pair_lanes(rest[0], rest[1])
        w_ref[rows, 896:1024] = pair_lanes(rest[2], None)
    wn_ref[288:384, :] = jnp.zeros((96, 384), LOW)
    for k in range(3):
        for tap in range(9):
            wn_ref[32 * tap : 32 * tap + 32, tile(k)] = narrow_ref[0, 9 * k + tap]
    for row, ref in ((0, scale_ref), (1, shift_ref)):
        vector = ref[index : index + 1, :]
        rest = vector[:, 384:416]
        squeeze = vector[:, 736:768]
        para_ref[row : row + 1, 0:128] = vector[:, 256:384]
        para_ref[row : row + 1, 128:256] = jnp.concatenate([rest] * 4, axis=1)
        para_ref[row : row + 1, 256:384] = jnp.concatenate([squeeze] * 4, axis=1)
        par_ref[row : row + 1, 0:256] = vector[:, 0:256]
        par_ref[row : row + 1, 256:384] = vector[:, 896:1024]
        par_ref[row : row + 1, 384:768] = jnp.concatenate([vector[:, 416:736], jnp.zeros((1, 64), F32)], axis=1)
        par_ref[row : row + 1, 768:896] = vector[:, 768:896]


def fit_backward(spatial_ref, narrow_ref, wt_ref, wnt_ref):
    wt_ref[480:512, :] = jnp.zeros((32, 2944), LOW)
    for k in range(3):
        for first, end, row in ((0, 128, 128 * k), (128, 160, 384 + 32 * k)):
            rows = slice(row, row + end - first)
            for tap in range(9):
                wt_ref[rows, tap * 256 : (tap + 1) * 256] = spatial_ref[0, 9 * k + tap, first:end, 0:256]
            for g in range(5):
                left = spatial_ref[0, 9 * k + 2 * g, first:end, 256:320]
                right = spatial_ref[0, 9 * k + 2 * g + 1, first:end, 256:320] if g < 4 else None
                wt_ref[rows, tile(18 + g)] = pair_lanes(left, right)
    wnt_ref[96:128, :] = jnp.zeros((32, 1152), LOW)
    for k in range(3):
        for tap in range(9):
            wnt_ref[32 * k : 32 * k + 32, tile(tap)] = narrow_ref[0, 9 * k + tap]


def fetch_block(body, index, held, made, *refs):
    whole, refs = refs[0 : len(refs) - 2 * held - made - 1], refs[len(refs) - 2 * held - made - 1 :]
    split, outs, parts, sems = refs[0:held], refs[held : held + made], refs[held + made : -1], refs[-1]
    copies = [pltpu.make_async_copy(ref.at[pl.ds(index, 1)], part, sems.at[i]) for i, (ref, part) in enumerate(zip(split, parts))]
    for copy in copies:
        copy.start()
    for copy in copies:
        copy.wait()
    body(*whole, *parts, *outs)


def layer_call(body, index, split, whole, outs, name=None, room=4):
    scratch = [pltpu.VMEM((1,) + x.shape[1:], x.dtype) for x in split]
    return pl.pallas_call(
        functools.partial(fetch_block, body, index, len(split), len(outs)),
        out_shape=tuple(outs),
        in_specs=[VMEM] * len(whole) + [pl.BlockSpec(memory_space=pl.ANY)] * len(split),
        out_specs=tuple([VMEM] * len(outs)),
        scratch_shapes=scratch + [pltpu.SemaphoreType.DMA((len(split),))],
        compiler_params=pltpu.CompilerParams(vmem_limit_bytes=scoped(scratch, room)),
        cost_estimate=pl.CostEstimate(flops=1, bytes_accessed=1, transcendentals=0),
        name=name,
    )(*whole, *split)


def exchange(value, sizes, bits):
    total = sizes[0] * sizes[1]

    def swap(mask):
        return lax.ppermute(value, AXES, [(i, i ^ mask) for i in range(total)])

    if len(bits) == 1:
        return value + swap(1 << bits[0])
    one, two = 1 << bits[0], 1 << bits[1]
    return (value + swap(one)) + (swap(two) + swap(one | two))


class Sum:
    def __init__(self, value, sizes):
        self.value, self.sizes, self.at = value, sizes, 0
        total = sizes[0] * sizes[1]
        bits = list(range(total.bit_length() - 1))
        self.stages = [bits[:1]] + [bits[at : at + 2] for at in range(1, len(bits), 2)]
        self.able = not (total & (total - 1))
        if not self.able:
            self.stages = []
            self.value = lax.psum(value, AXES)

    def step(self):
        if self.at < len(self.stages):
            self.value = exchange(self.value, self.sizes, self.stages[self.at])
            self.at += 1
        return self.value

    def result(self):
        while self.at < len(self.stages):
            self.step()
        return self.value


def sum_all(value, sizes):
    return Sum(value, sizes).result()


def meet(*holders):
    names = [[n for n in ("value", "keep", "send", "ready", "array") if getattr(holder, n, None) is not None] for holder in holders]
    values = lax.optimization_barrier([[getattr(h, n) for n in ns] for h, ns in zip(holders, names)])
    for holder, ns, got in zip(holders, names, values):
        for n, value in zip(ns, got):
            setattr(holder, n, value)


class Held:
    def __init__(self, array):
        self.array = array


class Sharing:
    def __init__(self, sizes):
        dp, rep = sizes
        self.sizes = sizes
        self.total = dp * rep
        self.able = not (self.total & (self.total - 1)) and dp >= 8 and rep >= 4
        low = rep.bit_length() - 1
        self.bits = [0, 1, low, low + 1, low + 2]
        self.other = [bit for bit in range(self.total.bit_length() - 1) if bit not in self.bits]

    def me(self):
        if not self.able:
            return jnp.zeros((1,), jnp.int32)
        flat = lax.axis_index("dp") * self.sizes[1] + lax.axis_index("rep")
        index = sum(((flat >> bit) & 1) << i for i, bit in enumerate(self.bits))
        return index.reshape(1).astype(jnp.int32)

    def swap(self, value, even, odd=None):
        masks = [sum(1 << self.bits[i] for i in bits) for bits in (even, even if odd is None else odd)]
        return lax.ppermute(value, AXES, [(i, i ^ masks[i & 1]) for i in range(self.total)])

    def chain(self, keep, send):
        return Chain(self, keep, send)


CORE, FIRST, SECOND, BOTH = ((0,), (0,)), ((1,), (2,)), ((2,), (1,)), ((1, 2), (1, 2))
FAR, NEAR, ENDS = ((4,), (4,)), ((3,), (3,)), ((3, 4), (3, 4))


class Chain:
    def __init__(self, sharing, keep, send, short=False):
        self.sharing, self.keep, self.send, self.short = sharing, keep, send, short
        self.ready = None
        names = ["core", "both" if short else "first", None if short else "second", "depth"]
        self.stages = [n for n in names + ["up_depth"] + ["up_" + n for n in reversed(names[0:3]) if n] if n]
        if not sharing.able:
            self.keep, self.send, self.stages = lax.psum(keep, AXES), lax.psum(send, AXES), []

    def offers(self):
        stage, send, keep = self.stages[0], self.send, self.keep
        if stage in ("core", "up_core"):
            return [(CORE, send)]
        if stage in ("first", "up_first"):
            return [(FIRST, send)]
        if stage in ("second", "up_second"):
            return [(SECOND, send)]
        if stage == "both":
            return [(FIRST, send[0:4]), (SECOND, keep[4:8]), (BOTH, send[4:8])]
        if stage == "up_both":
            return [(SECOND, send), (FIRST, send), (BOTH, send)]
        if stage == "depth":
            return [(FAR, send[0]), (NEAR, send[1]), (ENDS, send[2])]
        return [(FAR, send), (NEAR, send), (ENDS, send)]

    def accept(self, got):
        stage, send, keep = self.stages.pop(0), self.send, self.keep
        if stage in ("core", "first"):
            half = keep.shape[0] // 2
            self.keep, self.send = keep[0:half] + got[0][0:half], keep[half:] + got[0][half:]
        elif stage == "second":
            self.split([keep[i] + got[0][i] for i in range(4)])
        elif stage == "both":
            self.split([(keep[i] + got[0][i]) + (got[1][i] + got[2][i]) for i in range(4)])
        elif stage == "depth":
            whole = (keep + got[0]) + (got[1] + got[2])
            for bit in self.sharing.other:
                whole = exchange(whole, self.sharing.sizes, [bit])
            self.keep, self.send = None, whole
        elif stage == "up_depth":
            self.send = jnp.stack([send, *got])
        elif stage == "up_core":
            self.keep, self.send = send, got[0]
        else:
            self.send = jnp.concatenate([send, *got])

    def rest(self):
        if not self.stages:
            return
        first, second = self.sharing.swap(self.send, *FIRST), self.sharing.swap(self.ready, *SECOND)
        self.split([(self.keep[i] + first[i]) + second[i] for i in range(4)])
        self.ready = None
        self.stages = self.stages[2:]

    def split(self, parts):
        self.keep, self.send = parts[0], parts[1:]

    def half(self):
        if not self.stages:
            return
        if self.ready is None:
            self.ready = self.keep[4:8] + self.sharing.swap(self.send[4:8], *FIRST)
            self.keep, self.send = self.keep[0:4], self.send[0:4]
        else:
            self.keep = self.keep + self.sharing.swap(self.send, *FIRST)
            self.send, self.ready = self.ready, None
            self.stages.pop(0)

    def result(self):
        return [self.keep, self.send]


def advance(*chains):
    chains = [chain for chain in chains if chain.stages]
    offered = [chain.offers() for chain in chains]
    got = [[None] * len(offers) for offers in offered]
    partners = {}
    for i, offers in enumerate(offered):
        for j, (partner, _) in enumerate(offers):
            partners.setdefault((partner, i if partner == CORE else 0), []).append((i, j))
    for (partner, _), places in partners.items():
        values = [offered[i][j][1] for i, j in places]
        flat = [value.reshape(-1, 128) for value in values]
        arrived = chains[0].sharing.swap(flat[0] if len(flat) == 1 else jnp.concatenate(flat), *partner)
        at = 0
        for (i, j), value, rows in zip(places, values, flat):
            got[i][j] = arrived[at : at + rows.shape[0]].reshape(value.shape)
            at += rows.shape[0]
    for chain, received in zip(chains, got):
        chain.accept(received)


def shards(sizes, *arguments):
    clip_input, cotangent, clip_group, crop_sides = arguments[:4]
    kernels, bn_scale, bn_shift = arguments[4:10], arguments[10], arguments[11]
    w_single, w_reduce, w_spatial, w_squeeze, w_narrow, w_project = kernels
    _, frames, side, _, width = clip_input.shape
    lower, upper = Layer(frames, side, False), Layer(frames // 2, side // 2, True)
    where = [clip_group, crop_sides]
    merged = [w_spatial.reshape(2, 27, 160, 320), w_narrow.reshape(2, 27, 32, 128)]
    turned = [jnp.swapaxes(w_reduce, 1, 2), jnp.swapaxes(w_squeeze, 1, 2)]
    points = layer_call(
        fit_points, 1, [w_single, w_project] + turned, [],
        [struct((384, 896), LOW), struct((896, 384), LOW)], name="fit_points",
    )
    fitted = [
        layer_call(
            functools.partial(fit_forward, i),
            i,
            merged,
            [bn_scale, bn_shift],
            [struct((1536, 1024), LOW), struct((384, 384), LOW), struct((2, 384), F32), struct((2, 896), F32)],
            name="fit_forward",
        )
        for i in (0, 1)
    ]
    pars = [item[2:4] for item in fitted]

    def turned_weights(index, kernels):
        return layer_call(
            fit_backward, index, kernels, [], [struct((512, 2944), LOW), struct((128, 1152), LOW)], name="fit_backward"
        )

    def frames_first(value, layer):
        value = jnp.transpose(value, (0, 2, 3, 1, 4)).reshape(layer.side * layer.side, layer.frames, width)
        return jnp.transpose(value, (1, 0, 2))

    def frames_back(value, layer):
        value = jnp.transpose(value, (1, 0, 2)).reshape(1, layer.side, layer.side, layer.frames, width)
        return jnp.transpose(value, (0, 3, 1, 2, 4))

    x = frames_first(clip_input, lower).reshape(lower.rows, width)
    cot = frames_first(cotangent, upper)
    cot = jnp.concatenate(
        [cot[..., 0:576], jnp.zeros(cot.shape[:2] + (64,), LOW), cot[..., 576:832]], axis=2
    )
    cot = jnp.pad(cot, ((0, 0), (0, upper.frame - upper.side * upper.side), (0, 0))).reshape(upper.rows, 896)

    def around(layer, tiles):
        return pltpu.VMEM((tiles, layer.frame + 2 * EDGE, 128), F32)

    def forward(layer, za, suma, sumb, index):
        r = layer.rows
        return call(
            functools.partial(conv_forward, layer),
            where + [za, suma, pars[index][0], sumb, *fitted[index][0:2]],
            [struct((r, 1536), LOW), struct((r, 384), LOW), struct((r, 512), F32), struct((2, 896), F32)],
            [around(layer, 3), pltpu.VMEM((r, 256), F32)],
            name="conv_forward",
        )

    def unit_back(layer, gu, zb, zc, suma, sums, back, index):
        r = layer.rows
        return call(
            functools.partial(unit_backward, layer),
            where + [gu, zb, zc, suma, sums, back, pars[index][1]],
            [struct((r, 384), LOW), struct((r, 1024), LOW), struct((r, 384), LOW)],
            [around(layer, 1), pltpu.VMEM((r, 128), F32)],
            fetch=[2, 3, 4] if layer.halved else [],
            name="unit_backward",
        )

    def conv_back(layer, three, thin3, za, suma, index, turned):
        r = layer.rows
        return call(
            functools.partial(conv_backward, layer),
            where + [three, thin3, za, suma, pars[index][0], *turned],
            [struct((r, 384), F32), struct((2, 384), F32)],
            [
                around(layer, 4),
                pltpu.VMEM((layer.frame, 2944), LOW),
                pltpu.VMEM((layer.frame, 1152), LOW),
                pltpu.VMEM((r, 256), F32),
                pltpu.VMEM((r, 128), F32),
            ],
            late=[7, 8] if layer.halved else [],
            name="conv_backward",
        )

    sharing = Sharing(sizes)
    me = sharing.me()

    def make_weights(index, columns, kinds, *operands, short=False, fetch=False):
        part = PARTS[index]
        scratch = []
        for kind in kinds:
            if kind == "w":
                scratch.append((1440, 128 * sum(count for _, count in columns)))
            elif kind == "o":
                scratch += [(384, 384), (832, 384)]
            else:
                scratch.append((192, 896))
        made = call(
            functools.partial(weights, part, columns, kinds),
            [me, *operands],
            [struct((16, part[0], 128), F32)] * 2,
            [pltpu.VMEM(shape, F32) for shape in scratch],
            scalars=1,
            fetch=range(1, 1 + len(operands)) if fetch else [],
            name="weights",
        )
        return Chain(sharing, *made, short=short)

    def unit_and_first(layer, gu, zb, zc, suma, sums, back, index, wide, dza, upper_source, thin, source):
        r = layer.rows
        parts, columns = PARTS[1:3], ([(0, 2), (2, 2), (6, 1)], [(4, 2), (7, 1)])
        pieces = [struct((16, part[0], 128), F32) for part in parts for _ in (0, 1)]
        grads = [(1440, 640), (192, 896), (1440, 384), (384, 384), (832, 384)]
        *made, keep, send, other_keep, other_send = call(
            functools.partial(unit_and_weights, layer, parts, columns),
            where + [me, gu, zb, zc, suma, sums, back, pars[index][1], wide, dza, upper_source, thin, source],
            [struct((r, 384), LOW), struct((r, 1024), LOW), struct((r, 384), LOW)] + pieces,
            [around(layer, 1), pltpu.VMEM((r, 128), F32)] + [pltpu.VMEM(shape, F32) for shape in grads],
            scalars=3,
            name="unit_and_weights",
        )
        return made, Chain(sharing, keep, send), Chain(sharing, other_keep, other_send)

    r0, r1 = lower.rows, upper.rows
    za, suma, wa = call(
        functools.partial(first_a, lower),
        where + [x, *turned],
        [struct((r0, 384), F32), struct((3, 384), F32), struct((384, 832), LOW)],
        fetch=[3, 4],
        name="first_a",
    )
    small, held = Sum(suma, sizes), Held(list(fitted[0]))
    small.step()
    small.step()
    meet(small, held)
    fitted[0] = held.array
    pars[0] = fitted[0][2:4]
    suma = small.result()
    zb, sumb = call(
        functools.partial(first_b, lower),
        where + [x, w_single, w_project],
        [struct((r0, 384), F32), struct((2, 384), F32)],
        [around(lower, 1)],
        name="first_b",
    )
    wide, thin, zc, sums = forward(lower, za, suma, sumb, 0)
    sums = sum_all(sums, sizes)
    q, za2, zb2, suma2, sumb2 = call(
        functools.partial(finish_lower, lower, upper),
        where + [zb, zc, suma, sums, pars[0][1], *points],
        [struct((r1, 896), LOW), struct((r1, 384), F32), struct((r1, 384), F32), struct((3, 384), F32), struct((2, 384), F32)],
        [around(upper, 1), pltpu.VMEM((lower.frame, 1792), LOW)],
        name="finish_lower",
    )
    suma2 = sum_all(suma2, sizes)
    wide2, thin2, zc2, sums2 = forward(upper, za2, suma2, sumb2, 1)
    sums2 = sum_all(sums2, sizes)
    out, gu2, back2 = call(
        functools.partial(finish_upper, upper),
        where + [zb2, zc2, suma2, sums2, pars[1][1], cot],
        [struct((r1, 896), LOW), struct((r1, 896), F32), struct((2, 896), F32)],
        name="finish_upper",
    )
    small, held = Sum(back2, sizes), Held(list(merged))
    small.step()
    meet(small, held)
    merged = held.array
    held = Held(list(turned_weights(1, merged)))
    small.step()
    meet(small, held)
    turned2 = held.array
    back2 = small.result()
    dzb2, three2, thin32 = unit_back(upper, gu2, zb2, zc2, suma2, sums2, back2, 1)
    gua2, backa2 = conv_back(upper, three2, thin32, za2, suma2, 1, turned2)
    small = Sum(backa2, sizes)
    small.step()
    one = make_weights(0, [(0, 2), (2, 2), (4, 2), (6, 2)], "wo", wide2, three2, thin2, thin32, q, dzb2)
    meet(small, one)
    small.step()
    advance(one)
    meet(small, one)
    backa2 = small.result()
    one.half()
    dza2, gu, back = call(
        functools.partial(join_blocks, upper, lower),
        where + [gua2, za2, suma2, backa2, pars[1][0], dzb2, *points, zb, zc, suma, sums, pars[0][1]],
        [struct((r1, 384), LOW), struct((r0, 896), F32), struct((2, 896), F32)],
        [pltpu.VMEM((lower.frame, 896), F32)],
        name="join_blocks",
    )
    small, held = Sum(back, sizes), Held(list(merged))
    small.step()
    meet(small, held)
    held = Held(list(turned_weights(0, held.array)))
    small.step()
    meet(small, held)
    turned = held.array
    meet(small, one)
    one.rest()
    back = small.result()
    (dzb, three, thin3), two, more = unit_and_first(
        lower, gu, zb, zc, suma, sums, back, 0, wide, dza2, q, thin, x
    )
    held = Held(three)
    meet(one, two, more, held)
    advance(one)
    advance(two)
    meet(two, more)
    advance(two)
    advance(more)
    gua, backa = conv_back(lower, held.array, thin3, za, suma, 0, turned)
    small = Sum(backa, sizes)
    meet(two, more, small)
    more.half()
    small.step()
    small.step()
    meet(one, more, small)
    advance(one)
    more.rest()
    advance(two)
    backa = small.result()
    dza, da = call(
        functools.partial(last_back, lower),
        where + [gua, za, suma, backa, pars[0][0], dzb, wa, w_single, w_project],
        [struct((r0, 384), LOW), struct((r0, 832), LOW)],
        name="last_back",
    )
    held = Held(dza)
    meet(one, two, more, held)
    final = make_weights(3, [], "l", held.array, x, short=True)
    advance(one, two)
    advance(final)
    meet(one, two, more, final)
    advance(one, two, more, final)
    meet(one, two, more, final)
    advance(one, more, final)
    advance(two)
    advance(two)
    meet(one, two, more, final)
    joined = Held(assemble_call(me, [(PARTS[0], one.result())], [(which, 1, 0, 0) for which in (SINGLE, SPATIAL, NARROW, PROJECT)], None))
    advance(two, more, final)
    meet(two, more, final, joined)
    joined.array = assemble_call(
        me, [(PARTS[1], two.result())], [(SPATIAL, 0, 0, 18), (REDUCE, 1, 0, 0), (SQUEEZE, 1, 0, 0)], list(joined.array)
    )
    da = Held(frames_back(da.reshape(lower.frames, lower.frame, width), lower))
    out = jnp.concatenate([out[:, 0:576], out[:, 640:896]], axis=1)
    out = out.reshape(upper.frames, upper.frame, width)[:, 0 : upper.side * upper.side]
    out = Held(frames_back(out, upper))
    advance(more, final)
    meet(more, final, joined, da, out)
    advance(more, final)
    joined = list(joined.array)
    joined = list(assemble_call(
        me,
        [(PARTS[2], more.result()), (PARTS[3], final.result())],
        [(SPATIAL, 0, 18, 9)] + [(which, 0, 0, 0) for which in (SINGLE, REDUCE, SQUEEZE, NARROW, PROJECT)],
        joined,
    ))
    joined[REDUCE], joined[SQUEEZE] = (jnp.swapaxes(joined[which], 1, 2) for which in (REDUCE, SQUEEZE))
    joined = [value.reshape(kernel.shape) for value, kernel in zip(joined, kernels)]
    both = jnp.stack([unfit_vectors(backa, back), unfit_vectors(backa2, back2)])
    return (
        out.array,
        da.array,
        *joined,
        both[:, 1],
        both[:, 0],
    )


def solution(mesh):
    split = P(AXES, None, None, None, None)
    sizes = tuple(mesh.shape[axis] for axis in AXES)
    return jax.shard_map(
        functools.partial(shards, sizes),
        mesh=mesh,
        in_specs=(split, split, P(AXES)) + (P(),) * 9,
        out_specs=(split, split) + (P(),) * 8,
        check_vma=False,
    )
```

```python
import functools

import jax
import jax.numpy as jnp
from jax import lax
from jax.experimental import pallas as pl
from jax.experimental.pallas import tpu as pltpu
from jax.sharding import PartitionSpec as P

AXES = ("dp", "rep")
F32 = jnp.float32
LOW = jnp.bfloat16
EDGE = 32
TAPS = [(dh, dw) for dh in (-1, 0, 1) for dw in (-1, 0, 1)]
UNIT_TILES = [("b", 0), ("b", 1), ("c", 0), ("c", 1), ("c", 2), ("c", 3), ("b", 2)]
VMEM = pl.BlockSpec(memory_space=pltpu.VMEM)
SMEM = pl.BlockSpec(memory_space=pltpu.SMEM)
MIB = 1024 * 1024


def struct(shape, kind):
    return jax.ShapeDtypeStruct(shape, kind)


def scoped(scratch, room):
    total = 0
    for item in scratch:
        if isinstance(item, jax.core.ShapedArray) or hasattr(item, "shape"):
            shape = item.shape
            if len(shape) >= 2:
                size = -(-shape[-1] // 128) * 128 * -(-shape[-2] // 8) * 8 * jnp.dtype(item.dtype).itemsize
                for n in shape[:-2]:
                    size *= n
                total += size
    return total + room * MIB


def with_fetch(body, scalars, fetch, late, many_ins, many_outs, *refs):
    ins, outs = list(refs[0:many_ins]), refs[many_ins : many_ins + many_outs]
    scratch = list(refs[many_ins + many_outs :])
    sems = scratch.pop()
    moved = fetch + late
    parts = scratch[len(scratch) - len(moved) :]
    scratch = scratch[0 : len(scratch) - len(moved)]
    copies = [pltpu.make_async_copy(ins[i], part, sems.at[k]) for k, (i, part) in enumerate(zip(moved, parts))]
    for copy in copies:
        copy.start()
    for copy in copies[0 : len(fetch)]:
        copy.wait()
    for i, part in zip(moved, parts):
        ins[i] = part

    def ready():
        for copy in copies[len(fetch) :]:
            copy.wait()

    body(*ins, *outs, *scratch, **({"ready": ready} if late else {}))


def call(body, ins, outs, scratch=(), scalars=2, room=3, name=None, fetch=(), late=()):
    fetch, late, scratch = list(fetch), list(late), list(scratch)
    specs = [SMEM] * scalars + [VMEM] * (len(ins) - scalars)
    if fetch or late:
        body = functools.partial(with_fetch, body, scalars, fetch, late, len(ins), len(outs))
        for i in fetch + late:
            specs[i] = pl.BlockSpec(memory_space=pl.ANY)
            scratch.append(pltpu.VMEM(ins[i].shape, ins[i].dtype))
    limit = scoped(scratch, room)
    if fetch or late:
        scratch.append(pltpu.SemaphoreType.DMA((len(fetch) + len(late),)))
    return pl.pallas_call(
        body,
        out_shape=tuple(outs),
        in_specs=specs,
        out_specs=tuple([VMEM] * len(outs)),
        scratch_shapes=scratch,
        compiler_params=pltpu.CompilerParams(vmem_limit_bytes=limit),
        cost_estimate=pl.CostEstimate(flops=1, bytes_accessed=1, transcendentals=0),
        name=name,
    )(*ins)


def tile(index, width=1):
    return slice(index * 128, (index + width) * 128)


def lanes():
    return lax.broadcasted_iota(jnp.int32, (1, 128), 1)


def silu(half):
    return half * (jnp.tanh(half) + 1.0)


def double_slope(half):
    bent = jnp.tanh(half)
    return (1.0 + bent) * (1.0 + half * (1.0 - bent))


def places(frame, side):
    at = lax.broadcasted_iota(jnp.int32, (frame, 1), 0).astype(F32)
    row = jnp.floor((at + 0.5) * (1.0 / side))
    return row, at - row * side


def crop_mask(frame, side, crop):
    row, column = places(frame, side)
    return jnp.where((row < crop) & (column < crop), 1.0, 0.0).astype(F32)


def column_mask(frame, side, step):
    row, column = places(frame, side)
    inside = (column + step > -0.5) & (column + step < side - 0.5)
    return jnp.where(inside, 1.0, 0.0).astype(F32)


def crop_of(group_ref, sides_ref, halved):
    crop = sides_ref[group_ref[0]]
    if halved:
        crop = lax.shift_right_logical(crop, 1)
    return crop.astype(F32)


def moments(sums, count):
    mean = sums[0:1] / count
    square = sums[1:2] / count
    return mean, lax.rsqrt(square - mean * mean + 1e-05)


def back_terms(sums, count, gamma, mean, inverse):
    scale = gamma * inverse
    slope = scale * inverse * (sums[1:2] / count)
    return scale, scale * (sums[0:1] / count) - mean * slope, slope


def add_sums(ref, at, first, second):
    ref[0:1, at] += jnp.sum(first, axis=0, keepdims=True)
    ref[1:2, at] += jnp.sum(second, axis=0, keepdims=True)


def neighbour_sum(values, around, frame, side, put):
    frames = len(values)
    left = column_mask(frame, side, -1)
    right = column_mask(frame, side, 1)
    for t in range(frames):
        total = values[t]
        if t > 0:
            total = total + values[t - 1]
        if t < frames - 1:
            total = total + values[t + 1]
        around[0, EDGE : EDGE + frame, :] = total
        total = (
            total
            + around[0, EDGE - side : EDGE - side + frame, :]
            + around[0, EDGE + side : EDGE + side + frame, :]
        )
        around[0, EDGE : EDGE + frame, :] = total
        total = (
            total
            + around[0, EDGE - 1 : EDGE - 1 + frame, :] * left
            + around[0, EDGE + 1 : EDGE + 1 + frame, :] * right
        )
        put(t, total * (1.0 / 27.0))


def clear_edges(around, frame):
    tiles = around.shape[0]
    around[:, 0:EDGE, :] = jnp.zeros((tiles, EDGE, 128), F32)
    around[:, EDGE + frame : 2 * EDGE + frame, :] = jnp.zeros((tiles, EDGE, 128), F32)


def dot(a, b):
    return lax.dot_general(a, b, (((1,), (0,)), ((), ())), preferred_element_type=F32)


def dot_nt(a, b):
    return lax.dot_general(a, b, (((1,), (1,)), ((), ())), preferred_element_type=F32)


def dot_tn(a, b):
    return lax.dot_general(a, b, (((0,), (0,)), ((), ())), preferred_element_type=F32)


class Layer:
    def __init__(self, frames, side, halved):
        self.frames = frames
        self.side = side
        self.halved = halved
        self.frame = -(-side * side // 16) * 16
        self.rows = frames * self.frame

    def at(self, t):
        return slice(t * self.frame, (t + 1) * self.frame)


def point_a(layer, mask, x_ref, w_ref, za_ref, sums_ref):
    sums_ref[...] = jnp.zeros(sums_ref.shape, F32)
    for t in range(layer.frames):
        z = dot_nt(x_ref[layer.at(t), :], w_ref[...])
        za_ref[layer.at(t), :] = z
        for j in range(3):
            part = z[:, tile(j)] * mask
            add_sums(sums_ref, tile(j), part, part * z[:, tile(j)])
    cells = jnp.sum(mask, axis=0, keepdims=True) * layer.frames
    sums_ref[2:3, :] = jnp.broadcast_to(cells, (1, 384))


def point_b(layer, mask, x_ref, kernels, zb_ref, sums_ref, around):
    sums_ref[...] = jnp.zeros(sums_ref.shape, F32)
    clear_edges(around, layer.frame)
    flat = []
    for t in range(layer.frames):
        source = x_ref[layer.at(t), :]
        z = dot(source, kernels[0])
        zb_ref[layer.at(t), 0:256] = z
        zb_ref[layer.at(t), tile(2)] = dot(source, kernels[1]) * mask
        for j in range(2):
            part = z[:, tile(j)] * mask
            add_sums(sums_ref, tile(j), part, part * z[:, tile(j)])
    flat = [zb_ref[layer.at(t), tile(2)] for t in range(layer.frames)]

    def put(t, value):
        zb_ref[layer.at(t), tile(2)] = value
        part = value * mask
        add_sums(sums_ref, tile(2), part, part * value)

    neighbour_sum(flat, around, layer.frame, layer.side, put)


def first_a(layer, group_ref, sides_ref, x_ref, reduce_ref, squeeze_ref, za_ref, sums_ref, wa_ref):
    mask = crop_mask(layer.frame, layer.side, crop_of(group_ref, sides_ref, layer.halved))
    side_by_side(reduce_ref[0], squeeze_ref[0], wa_ref)
    point_a(layer, mask, x_ref, wa_ref, za_ref, sums_ref)


def first_b(layer, group_ref, sides_ref, x_ref, single_ref, project_ref, zb_ref, sums_ref, around):
    mask = crop_mask(layer.frame, layer.side, crop_of(group_ref, sides_ref, layer.halved))
    point_b(layer, mask, x_ref, [single_ref[0], project_ref[0]], zb_ref, sums_ref, around)


def conv_forward(
    layer, group_ref, sides_ref, za_ref, suma_ref, para_ref, sumb_ref, w_ref, wn_ref,
    wide_ref, thin_ref, zc_ref, sums_ref, around, rem,
):
    frames, frame, side = layer.frames, layer.frame, layer.side
    mask = crop_mask(frame, side, crop_of(group_ref, sides_ref, layer.halved))
    count = suma_ref[2:3, :]
    mean, inverse = moments(suma_ref, count)
    gain = 0.5 * para_ref[0:1, :] * inverse
    offset = 0.5 * para_ref[1:2, :] - mean * gain
    column = [column_mask(frame, side, dw) for dw in (-1, 0, 1)]
    part_of = lanes() // 32
    clear_edges(around, frame)
    for t in range(frames):
        rows = layer.at(t)
        for j in range(3):
            half = za_ref[rows, tile(j)] * gain[:, tile(j)] + offset[:, tile(j)]
            around[j, EDGE : EDGE + frame, :] = silu(half) * mask
        mixed = {1: [None] * 3, 2: [None] * 3}
        for k, (dh, dw) in enumerate(TAPS):
            start = EDGE + dh * side + dw
            shifted = around[0, start : start + frame, :]
            if dw:
                shifted = shifted * column[dw + 1]
            wide_ref[rows, tile(k)] = shifted.astype(LOW)
            for j in (1, 2):
                shifted = around[j, start : start + frame, :]
                if dw:
                    shifted = shifted * column[dw + 1]
                shifted = jnp.where(part_of == k % 4, shifted, 0.0)
                held = mixed[j][k // 4]
                mixed[j][k // 4] = shifted if held is None else held + shifted
        for g in range(3):
            wide_ref[rows, tile(9 + g)] = mixed[1][g].astype(LOW)
            thin_ref[rows, tile(g)] = mixed[2][g].astype(LOW)
    sums_ref[:, 0:384] = sumb_ref[...]
    sums_ref[:, 384:896] = jnp.zeros((2, 512), F32)
    zc_ref[...] = jnp.zeros(zc_ref.shape, F32)
    for t in range(frames):
        source = wide_ref[layer.at(t), :]
        thin = thin_ref[layer.at(t), :]
        for k in range(3):
            to = t + 1 - k
            if 0 <= to < frames:
                rows = layer.at(to)
                zc_ref[rows, 0:256] += dot(source, w_ref[:, k * 256 : (k + 1) * 256])
                zc_ref[rows, tile(3)] += dot(thin, wn_ref[:, tile(k)])
        rem[layer.at(t), :] = dot(source, w_ref[:, 768:1024])
    for t in range(frames):
        rows = layer.at(t)
        total = pltpu.roll(rem[rows, 0:128], 64, 1)
        if t > 0:
            total = total + rem[layer.at(t - 1), 0:128]
        if t < frames - 1:
            total = total + rem[layer.at(t + 1), 128:256]
        zc_ref[rows, tile(2)] = jnp.where(lanes() < 64, total, 0.0)
        for j in range(4):
            z = zc_ref[rows, tile(j)]
            part = z * mask
            add_sums(sums_ref, tile(3 + j), part, part * z)


class Norms:
    def __init__(self, sums_ref, par_ref, count):
        mean, inverse = moments(sums_ref, count)
        self.mean, self.inverse = mean, inverse
        self.gamma, self.beta = par_ref[0:1, :], par_ref[1:2, :]

        self.half_gain = 0.5 * self.gamma * inverse
        self.half_offset = 0.5 * self.beta - mean * self.half_gain

    def lane(self, kind, j):
        return tile(j if kind == "b" else 3 + j)

    def half(self, z, at):
        return z * self.half_gain[:, at] + self.half_offset[:, at]

    def normed(self, z, at):
        return (z - self.mean[:, at]) * self.inverse[:, at]


def finish_lower(
    lower, upper, group_ref, sides_ref, zb_ref, zc_ref, suma_ref, sums_ref, par_ref, wa_ref, wb_ref,
    q_ref, za2_ref, zb2_ref, suma2_ref, sumb2_ref, around, y_ref,
):
    crop = crop_of(group_ref, sides_ref, False)
    mask = crop_mask(lower.frame, lower.side, crop)
    norms = Norms(sums_ref, par_ref, suma_ref[2:3, 0:1])
    pick = pair_matrix(upper, lower)
    for t in range(upper.frames):
        for index, (kind, j) in enumerate(UNIT_TILES):
            at = norms.lane(kind, j)
            z_ref = zb_ref if kind == "b" else zc_ref
            total = None
            for source in (2 * t, 2 * t + 1):
                out = silu(norms.half(z_ref[lower.at(source), tile(j)], at)) * mask
                total = out if total is None else total + out
            high = total.astype(LOW)
            y_ref[:, tile(index)] = high
            y_ref[:, tile(7 + index)] = (total - high.astype(F32)).astype(LOW)
        both = dot(pick, y_ref[...])
        q_ref[upper.at(t), :] = (both[:, 0:896] + both[:, 896:1792]).astype(LOW)
    small = crop_mask(upper.frame, upper.side, crop_of(group_ref, sides_ref, True))
    point_a(upper, small, q_ref, wa_ref, za2_ref, suma2_ref)
    point_b(upper, small, q_ref, [wb_ref[:, 0:256], wb_ref[:, 256:384]], zb2_ref, sumb2_ref, around)


def pair_matrix(upper, lower):
    at = lax.broadcasted_iota(jnp.int32, (upper.frame, lower.frame), 1).astype(F32)
    row = jnp.floor((at + 0.5) * (1.0 / lower.side))
    column = at - row * lower.side
    group = jnp.floor(row * 0.5 + 0.25) * upper.side + jnp.floor(column * 0.5 + 0.25)
    mine = lax.broadcasted_iota(jnp.int32, (upper.frame, lower.frame), 0).astype(F32)
    return jnp.where(jnp.abs(group - mine) < 0.5, 0.125, 0.0).astype(LOW)


def spread_matrix(upper, lower):
    at = lax.broadcasted_iota(jnp.int32, (lower.frame, upper.frame), 0).astype(F32)
    row = jnp.floor((at + 0.5) * (1.0 / lower.side))
    column = at - row * lower.side
    group = jnp.floor(row * 0.5 + 0.25) * upper.side + jnp.floor(column * 0.5 + 0.25)
    mine = lax.broadcasted_iota(jnp.int32, (lower.frame, upper.frame), 1).astype(F32)
    return jnp.where(jnp.abs(group - mine) < 0.5, 0.0625, 0.0).astype(LOW)


def finish_upper(
    layer, group_ref, sides_ref, zb_ref, zc_ref, suma_ref, sums_ref, par_ref, cot_ref,
    out_ref, gu_ref, back_ref,
):
    mask = crop_mask(layer.frame, layer.side, crop_of(group_ref, sides_ref, layer.halved))
    half_mask = 0.5 * mask
    norms = Norms(sums_ref, par_ref, suma_ref[2:3, 0:1])
    back_ref[...] = jnp.zeros(back_ref.shape, F32)
    for t in range(layer.frames):
        rows = layer.at(t)
        for index, (kind, j) in enumerate(UNIT_TILES):
            at = norms.lane(kind, j)
            z_ref = zb_ref if kind == "b" else zc_ref
            z = z_ref[rows, tile(j)]
            n, half = norms.normed(z, at), norms.half(z, at)
            out_ref[rows, tile(index)] = (silu(half) * mask).astype(LOW)
            gu = cot_ref[rows, tile(index)].astype(F32) * half_mask * double_slope(half)
            gu_ref[rows, tile(index)] = gu
            add_sums(back_ref, at, gu, gu * n)


def unit_backward(
    layer, group_ref, sides_ref, gu_ref, zb_ref, zc_ref, suma_ref, sums_ref, back_ref, par_ref,
    dzb_ref, three_ref, thin3_ref, around, flat,
):
    frames, frame, side = layer.frames, layer.frame, layer.side
    mask = crop_mask(frame, side, crop_of(group_ref, sides_ref, layer.halved))
    count = suma_ref[2:3, 0:1]
    norms = Norms(sums_ref, par_ref, count)
    c0, c1, c2 = back_terms(back_ref, count, norms.gamma, norms.mean, norms.inverse)
    low_half = lanes() < 64

    def dz_of(t, index):
        kind, j = UNIT_TILES[index]
        at = norms.lane(kind, j)
        z_ref = zb_ref if kind == "b" else zc_ref
        rows = layer.at(t)
        return (gu_ref[rows, tile(index)] * c0[:, at] - z_ref[rows, tile(j)] * c2[:, at] - c1[:, at]) * mask

    clear_edges(around, frame)
    for t in range(frames):
        for index in (0, 1):
            dzb_ref[layer.at(t), tile(index)] = dz_of(t, index).astype(LOW)
        flat[layer.at(t), :] = dz_of(t, 6)

    def put(t, value):
        dzb_ref[layer.at(t), tile(2)] = (value * mask).astype(LOW)

    neighbour_sum([flat[layer.at(t), :] for t in range(frames)], around, frame, side, put)
    for t in range(frames):
        flat[layer.at(t), :] = jnp.where(low_half, dz_of(t, 4), 0.0)
    empty = jnp.zeros((frame, 128), LOW)
    for t in range(frames):
        parts = [dz_of(t, index).astype(LOW) for index in (2, 3, 5)]
        for k in range(3):
            to = t - 1 + k
            if 0 <= to < frames:
                rows = layer.at(to)
                three_ref[rows, tile(2 * k)] = parts[0]
                three_ref[rows, tile(2 * k + 1)] = parts[1]
                thin3_ref[rows, tile(k)] = parts[2]
        rest = pltpu.roll(flat[layer.at(t), :], 64, 1)
        if t < frames - 1:
            rest = rest + flat[layer.at(t + 1), :]
        three_ref[layer.at(t), tile(6)] = rest.astype(LOW)
        three_ref[layer.at(t), tile(7)] = flat[layer.at(t - 1), :].astype(LOW) if t else empty
    for rows, k in ((layer.at(0), 2), (layer.at(frames - 1), 0)):
        three_ref[rows, tile(2 * k)] = empty
        three_ref[rows, tile(2 * k + 1)] = empty
        thin3_ref[rows, tile(k)] = empty


def unit_and_weights(
    layer, parts, columns, group_ref, sides_ref, me_ref, gu_ref, zb_ref, zc_ref, suma_ref, sums_ref, back_ref, par_ref,
    wide_ref, dza_ref, q_ref, thin_ref, x_ref, dzb_ref, three_ref, thin3_ref, keep_ref, send_ref, other_keep_ref,
    other_send_ref, around, flat, wide_grad, last_grad, other_wide_grad, thin_grad, point_grad,
):
    unit_backward(
        layer, group_ref, sides_ref, gu_ref, zb_ref, zc_ref, suma_ref, sums_ref, back_ref, par_ref,
        dzb_ref, three_ref, thin3_ref, around, flat,
    )
    weights(
        parts[0], columns[0], "wl", me_ref, wide_ref, three_ref, dza_ref, q_ref, keep_ref, send_ref, wide_grad, last_grad
    )
    weights(
        parts[1], columns[1], "wo", me_ref, wide_ref, three_ref, thin_ref, thin3_ref, x_ref, dzb_ref, other_keep_ref,
        other_send_ref, other_wide_grad, thin_grad, point_grad,
    )


def conv_backward(
    layer, group_ref, sides_ref, three_ref, thin3_ref, za_ref, suma_ref, para_ref, wt_ref, wnt_ref,
    gua_ref, backa_ref, around, shifts, thins, rem, main, ready=lambda: None,
):
    frames, frame, side = layer.frames, layer.frame, layer.side
    mask = crop_mask(frame, side, crop_of(group_ref, sides_ref, layer.halved))
    column = [column_mask(frame, side, dw) for dw in (-1, 0, 1)]
    low_half = lanes() < 64
    first_part = lanes() < 32
    clear_edges(around, frame)
    main[...] = jnp.zeros(main.shape, F32)
    rem[...] = jnp.zeros(rem.shape, F32)
    for t in range(frames):
        rows = layer.at(t)
        rest = jnp.where(low_half, 0.0, three_ref[rows, tile(6)].astype(F32))
        parts = [
            three_ref[rows, tile(2)].astype(F32),
            three_ref[rows, tile(3)].astype(F32),
            rest + pltpu.roll(rest, 64, 1),
            thin3_ref[rows, tile(1)].astype(F32),
        ]
        for j in range(4):
            around[j, EDGE : EDGE + frame, :] = parts[j]
        mixed = [None] * 5
        for k, (dh, dw) in enumerate(TAPS):
            start = EDGE - dh * side - dw
            for j in range(4):
                shifted = around[j, start : start + frame, :]
                if dw:
                    shifted = shifted * column[1 - dw]
                if j < 2:
                    shifts[:, tile(2 * k + j)] = shifted.astype(LOW)
                elif j == 3:
                    thins[:, tile(k)] = shifted.astype(LOW)
                else:
                    shifted = jnp.where(low_half if k % 2 == 0 else ~low_half, shifted, 0.0)
                    held = mixed[k // 2]
                    mixed[k // 2] = shifted if held is None else held + shifted
        for g in range(5):
            shifts[:, tile(18 + g)] = mixed[g].astype(LOW)
        if t == 0:
            ready()
        product = dot_nt(shifts[...], wt_ref[...])
        thin = dot_nt(thins[...], wnt_ref[...])
        for k in range(3):
            to = t - 1 + k
            if 0 <= to < frames:
                rows = layer.at(to)
                main[rows, :] += product[:, tile(k)]
                turn = (128 - 32 * k) % 128
                last = product[:, tile(3)]
                rem[rows, 0:128] += last if turn == 0 else pltpu.roll(last, turn, 1)
                rem[rows, 128:256] += thin if turn == 0 else pltpu.roll(thin, turn, 1)
    mean, inverse = moments(suma_ref, suma_ref[2:3, :])
    half_mask, half_gamma, half_beta = 0.5 * mask, 0.5 * para_ref[0:1, :], 0.5 * para_ref[1:2, :]
    backa_ref[...] = jnp.zeros(backa_ref.shape, F32)
    for t in range(frames):
        rows = layer.at(t)
        for j in range(3):
            grad = main[rows, :] if j == 0 else rem[rows, tile(j - 1)]
            n = (za_ref[rows, tile(j)] - mean[:, tile(j)]) * inverse[:, tile(j)]
            gu = grad * half_mask * double_slope(half_gamma[:, tile(j)] * n + half_beta[:, tile(j)])
            if j:
                gu = jnp.where(first_part, gu, 0.0)
            gua_ref[rows, tile(j)] = gu
            add_sums(backa_ref, tile(j), gu, gu * n)


def point_back(layer, mask, gua_ref, za_ref, suma_ref, backa_ref, para_ref, dza_ref):
    count = suma_ref[2:3, :]
    mean, inverse = moments(suma_ref, count)
    c0, c1, c2 = back_terms(backa_ref, count, para_ref[0:1, :], mean, inverse)
    for t in range(layer.frames):
        rows = layer.at(t)
        for j in range(3):
            at = tile(j)
            dz = (gua_ref[rows, at] * c0[:, at] - za_ref[rows, at] * c2[:, at] - c1[:, at]) * mask
            if j:
                dz = jnp.where(lanes() < 32, dz, 0.0)
            dza_ref[rows, at] = dz.astype(LOW)


def join_blocks(
    upper, lower, group_ref, sides_ref, gua_ref, za_ref, suma_ref, backa_ref, para_ref, dzb_ref, wa_ref, wb_ref,
    zb_ref, zc_ref, suma1_ref, sums1_ref, par1_ref, dza_ref, gu_ref, back_ref, wide,
):
    small = crop_mask(upper.frame, upper.side, crop_of(group_ref, sides_ref, True))
    point_back(upper, small, gua_ref, za_ref, suma_ref, backa_ref, para_ref, dza_ref)
    mask = crop_mask(lower.frame, lower.side, crop_of(group_ref, sides_ref, False))
    norms = Norms(sums1_ref, par1_ref, suma1_ref[2:3, 0:1])
    back_ref[...] = jnp.zeros(back_ref.shape, F32)
    pick = spread_matrix(upper, lower)
    for t in range(upper.frames):
        rows = upper.at(t)
        dq = dot_nt(dzb_ref[rows, :], wb_ref[...]) + dot(dza_ref[rows, :], wa_ref[...])
        high = dq.astype(LOW)
        rest = (dq - high.astype(F32)).astype(LOW)
        wide[...] = dot(pick, high) + dot(pick, rest)
        for source in (2 * t, 2 * t + 1):
            at_rows = lower.at(source)
            for index, (kind, j) in enumerate(UNIT_TILES):
                at = norms.lane(kind, j)
                z_ref = zb_ref if kind == "b" else zc_ref
                z = z_ref[at_rows, tile(j)]
                n = norms.normed(z, at)
                gu = wide[:, tile(index)] * mask * double_slope(norms.half(z, at))
                gu_ref[at_rows, tile(index)] = gu
                add_sums(back_ref, at, gu, gu * n)


def last_back(
    layer, group_ref, sides_ref, gua_ref, za_ref, suma_ref, backa_ref, para_ref, dzb_ref, wa_ref, single_ref, project_ref, dza_ref, grad_ref,
):
    mask = crop_mask(layer.frame, layer.side, crop_of(group_ref, sides_ref, layer.halved))
    point_back(layer, mask, gua_ref, za_ref, suma_ref, backa_ref, para_ref, dza_ref)
    for t in range(layer.frames):
        rows = layer.at(t)
        total = dot_nt(dzb_ref[rows, 0:256], single_ref[0]) + dot_nt(dzb_ref[rows, 256:384], project_ref[0])
        total = total + dot(dza_ref[rows, :], wa_ref[...])
        grad_ref[rows, :] = (total * mask).astype(LOW)


def place(me, pair, core):
    bits = lax.shift_right_logical(me, 1) ^ pair
    x, y = bits & 1, lax.shift_right_logical(bits, 1) & 1
    near, far = lax.shift_right_logical(bits, 2) & 1, lax.shift_right_logical(bits, 3) & 1
    first = x + core * (y - x)
    second = y + core * (x - y)
    return first * 8 + second * 4 + near * 2 + far


def put_pair(me, keep_ref, send_ref, pair, rows, even, odd):
    core = me & 1
    mine = core == 0
    keep_ref[place(me, pair, core), rows, :] = jnp.where(mine, even, odd)
    send_ref[place(me, pair, 1 - core), rows, :] = jnp.where(mine, odd, even)


def get_pair(me, own_ref, other_ref, pair, rows):
    core = me & 1
    mine = core == 0
    own = own_ref[place(me, pair, core), rows, :]
    other = other_ref[place(me, pair, 1 - core), rows, :]
    return jnp.where(mine, own, other), jnp.where(mine, other, own)


def segments(blocks):
    rows = -(-sum(length for _, length in blocks) // 256) * 8
    pieces, piece, room = [], [], rows
    for name, length in blocks:
        at = 0
        while at < length:
            take = min(room, length - at)
            piece.append((name, at, at + take, rows - room))
            at += take
            room -= take
            if not room:
                pieces.append(piece)
                piece, room = [], rows
    if piece:
        pieces.append(piece)
    return rows, pieces + [[]] * (32 - len(pieces))


def wide(layer, *tiles):
    return [(("wide", j, layer), 720 if j == 7 else 1440) for j in tiles]


def point_and_thin(layer):
    return [(("point", j, layer), 832) for j in range(3)] + [(("thin", j, layer), 288) for j in range(3)]


def last(layer):
    return [(("last", j, layer), 96 if j == 6 else 192) for j in range(7)]


PARTS = [
    segments(wide(1, *range(8)) + point_and_thin(1)),
    segments(wide(0, 0, 1, 2, 3, 6) + last(1)),
    segments(wide(0, 4, 5, 7) + point_and_thin(0)),
    segments(last(0)),
]


def piece_value(piece, rows, read):
    parts = [read(name, first, end) for name, first, end, _ in piece]
    filled = sum(end - first for _, first, end, _ in piece)
    if filled < rows:
        parts.append(jnp.zeros((rows - filled, 128), F32))
    return parts[0] if len(parts) == 1 else jnp.concatenate(parts, axis=0)


def put_pieces(me, keep_ref, send_ref, part, read):
    rows, pieces = part
    for pair in range(16):
        even, odd = (piece_value(pieces[2 * pair + i], rows, read) for i in (0, 1))
        put_pair(me, keep_ref, send_ref, pair, slice(0, rows), even, odd)


def fold(ref, at, rows):
    value = jnp.where(lanes() < 64, ref[0 : 2 * rows, at], 0.0)
    ref[0:rows, at] = value[0:rows] + pltpu.roll(value[rows : 2 * rows], 64, 1)


def without_gap(ref, grad):
    if grad.shape[0] == 896:
        ref[0:576, :] = grad[0:576]
        ref[576:832, :] = grad[640:896]
    else:
        ref[...] = grad


def weights(part, columns, kinds, me_ref, *refs):
    refs = list(refs)
    read_from = {}
    operands = [refs.pop(0) for _ in range({"w": 2, "o": 4, "l": 2}[kinds[0]] + (0 if len(kinds) == 1 else {"o": 4, "l": 2}[kinds[1]]))]
    keep_ref, send_ref = refs.pop(0), refs.pop(0)
    for kind in kinds:
        if kind == "w":
            wide_ref, three_ref = operands.pop(0), operands.pop(0)
            grad = refs.pop(0)
            at = 0
            for first, count in columns:
                grad[:, tile(at, count)] = dot_tn(wide_ref[:, 0:1440], three_ref[:, tile(first, count)])
                for j in range(count):
                    read_from["wide", first + j] = (grad, at + j)
                    if first + j == 7:
                        fold(grad, tile(at + j), 720)
                at += count
        elif kind == "o":
            thin_ref, thin3_ref, x_ref, dzb_ref = (operands.pop(0) for _ in range(4))
            thin_grad, point_grad = refs.pop(0), refs.pop(0)
            thin_grad[...] = dot_tn(thin_ref[...], thin3_ref[...])
            without_gap(point_grad, dot_tn(x_ref[...], dzb_ref[...]))
            for j in range(3):
                read_from["point", j] = (point_grad, j)
                read_from["thin", j] = (thin_grad, j)
        else:
            dza_ref, x_ref = operands.pop(0), operands.pop(0)
            last_grad = refs.pop(0)
            grad = dot_tn(dza_ref[...], x_ref[...])
            if grad.shape[1] == 896:
                grad = close_gap(grad)
            width = grad.shape[1]
            last_grad[0:160, 0:width] = grad[0:160]
            last_grad[160:192, 0:width] = grad[256:288]
            if width < 896:
                last_grad[:, width:896] = jnp.zeros((192, 896 - width), F32)
            fold(last_grad, tile(6), 96)
            for j in range(7):
                read_from["last", j] = (last_grad, j)

    def read(name, first, end):
        ref, j = read_from[name[0:2]]
        return ref[first:end, tile(j)]

    put_pieces(me_ref[0], keep_ref, send_ref, part, read)


OUT_SHAPES = [(832, 256), (160, 832), (27, 160, 320), (32, 832), (27, 32, 128), (832, 128)]
SINGLE, REDUCE, SPATIAL, SQUEEZE, NARROW, PROJECT = range(6)


def assemble(sources, targets, aliased, me_ref, *refs):
    me = me_ref[0]
    many = sum(2 if relative else 1 for _, relative in sources)
    arrived, refs = list(refs[0:many]), refs[many + (6 if aliased else 0) :]
    outs, stages, sems = refs[0:6], refs[6 : 6 + len(targets)], refs[6 + len(targets)]
    stage = {(which, block): (ref, first) for (which, block, first, _), ref in zip(targets, stages)}

    def put_wide(block, k, lanes_at, first, value):
        ref, offset = stage[SPATIAL, block]
        done = 0
        while done < value.shape[0]:
            row = first + done
            if row < 1152:
                tap, channel = row // 128, row % 128
                take = min(128 - channel, value.shape[0] - done)
            else:
                tap, channel = (row - 1152) // 32, 128 + (row - 1152) % 32
                take = min(160 - channel, value.shape[0] - done)
            ref[k * 9 + tap - offset, channel : channel + take, lanes_at] = value[done : done + take]
            done += take

    def put_last(block, lanes_at, first, value):
        for which, low, high in ((REDUCE, 0, 160), (SQUEEZE, 160, 192)):
            begin, stop = max(first, low), min(first + value.shape[0], high)
            if begin < stop:
                stage[which, block][0][begin - low : stop - low, lanes_at] = value[begin - first : stop - first]

    def put(name, first, end, value):
        kind, j, block = name
        if kind == "wide":
            if j < 6:
                put_wide(block, j // 2, tile(j % 2), first, value)
            elif j == 6:
                put_wide(block, 0, slice(256, 320), first, value[:, 0:64])
                put_wide(block, 1, slice(256, 320), first, pltpu.roll(value, 64, 1)[:, 0:64])
            else:
                put_wide(block, 2, slice(256, 320), first, value[:, 0:64])
                put_wide(block, 2, slice(256, 320), first + 720, pltpu.roll(value, 64, 1)[:, 0:64])
        elif kind == "point":
            if j < 2:
                stage[SINGLE, block][0][first:end, tile(j)] = value
            else:
                stage[PROJECT, block][0][first:end, :] = value
        elif kind == "thin":
            done = 0
            while done < end - first:
                tap, channel = (first + done) // 32, (first + done) % 32
                take = min(32 - channel, end - first - done)
                stage[NARROW, block][0][j * 9 + tap, channel : channel + take, :] = value[done : done + take]
                done += take
        elif j < 6:
            put_last(block, tile(j), first, value)
        else:
            put_last(block, slice(768, 832), first, value[:, 0:64])
            put_last(block, slice(768, 832), first + 96, pltpu.roll(value, 64, 1)[:, 0:64])

    for (rows, pieces), relative in sources:
        held = [arrived.pop(0) for _ in range(2 if relative else 1)]
        for pair in range(16):
            if relative:
                both = get_pair(me, *held, pair, slice(0, rows))
            else:
                both = [held[0][2 * pair + i] for i in (0, 1)]
            for i in (0, 1):
                for name, first, end, row in pieces[2 * pair + i]:
                    put(name, first, end, both[i][row : row + end - first])
    copies = []
    for i, ((which, block, first, count), ref) in enumerate(zip(targets, stages)):
        to = outs[which].at[block]
        if count < OUT_SHAPES[which][0]:
            to = to.at[pl.ds(first, count)]
        copies.append(pltpu.make_async_copy(ref, to, sems.at[i]))
        copies[-1].start()
    for copy in copies:
        copy.wait()


def assemble_call(me, sources, targets, outs):
    anywhere = pl.BlockSpec(memory_space=pl.ANY)
    arrays = sum((list(found) for _, found in sources), [])
    targets = [(which, block, first, count or OUT_SHAPES[which][0]) for which, block, first, count in targets]
    scratch = [pltpu.VMEM((count,) + OUT_SHAPES[which][1:], F32) for which, _, _, count in targets]
    return pl.pallas_call(
        functools.partial(assemble, [(part, len(found) == 2) for part, found in sources], targets, outs is not None),
        out_shape=tuple(struct((2,) + shape, F32) for shape in OUT_SHAPES),
        in_specs=[SMEM] + [VMEM] * len(arrays) + [anywhere] * (0 if outs is None else 6),
        out_specs=tuple([anywhere] * 6),
        scratch_shapes=scratch + [pltpu.SemaphoreType.DMA((len(targets),))],
        input_output_aliases={} if outs is None else {1 + len(arrays) + i: i for i in range(6)},
        compiler_params=pltpu.CompilerParams(vmem_limit_bytes=scoped(scratch, 3)),
        cost_estimate=pl.CostEstimate(flops=1, bytes_accessed=1, transcendentals=0),
        name="assemble",
    )(me, *arrays, *([] if outs is None else outs))


def unfit_vectors(sums_a, sums):
    return jnp.concatenate(
        [sums[:, 0:256], sums_a[:, 0:160], sums[:, 384:704], sums_a[:, 256:288], sums[:, 768:896], sums[:, 256:384]], axis=1
    )


def open_gap(value):
    value = value.astype(F32)
    tiles = [value[:, tile(j)] for j in range(6)]
    tiles.append(jnp.concatenate([value[:, 768:832], jnp.zeros((value.shape[0], 64), F32)], axis=1))
    low_half = lanes() < 64
    turned = [pltpu.roll(part, 64, 1) for part in tiles[4:7]]
    tiles[4] = jnp.where(low_half, tiles[4], 0.0)
    tiles[5] = jnp.where(low_half, turned[0], turned[1])
    tiles[6] = jnp.where(low_half, turned[1], turned[2])
    return jnp.concatenate(tiles, axis=1).astype(LOW)


def close_gap(value):
    low_half = lanes() < 64
    tiles = [value[:, tile(j)] for j in range(7)]
    turned = [pltpu.roll(part, 64, 1) for part in tiles[5:7]]
    tiles[4] = jnp.where(low_half, tiles[4], turned[0])
    tiles[5] = jnp.where(low_half, turned[0], turned[1])
    tiles[6] = turned[1]
    return jnp.concatenate(tiles, axis=1)


def side_by_side(reduce, squeeze, wa_ref):
    wa_ref[0:128, :] = reduce[0:128]
    for i in range(4):
        wa_ref[128 + 32 * i : 160 + 32 * i, :] = reduce[128:160]
        wa_ref[256 + 32 * i : 288 + 32 * i, :] = squeeze


def fit_points(single_ref, project_ref, reduce_ref, squeeze_ref, wa_ref, wb_ref):
    gap = wa_ref.shape[1] == 896
    if gap:
        spans = [(slice(0, 576), slice(0, 576)), (slice(640, 896), slice(576, 832))]
        wb_ref[576:640, :] = jnp.zeros((64, 384), LOW)
    else:
        spans = [(slice(0, 832), slice(0, 832))]
    for to, source in spans:
        wb_ref[to, 0:256] = single_ref[0, source, :]
        wb_ref[to, 256:384] = project_ref[0, source, :]
    reduce, squeeze = reduce_ref[0], squeeze_ref[0]
    if gap:
        reduce, squeeze = open_gap(reduce), open_gap(squeeze)
    side_by_side(reduce, squeeze, wa_ref)


def pair_lanes(left, right):
    parts = [jnp.zeros((max(p.shape[0] for p in (left, right) if p is not None), 64), F32) if p is None else p.astype(F32) for p in (left, right)]
    return jnp.concatenate(parts, axis=1).astype(LOW)


def fit_forward(index, scale_ref, shift_ref, spatial_ref, narrow_ref, w_ref, wn_ref, para_ref, par_ref):
    spans = [(0, 128, 128 * tap, tap) for tap in range(9)] + [(128, 160, 1152 + 32 * tap, tap) for tap in range(9)]
    w_ref[1440:1536, :] = jnp.zeros((96, 1024), LOW)
    for first, end, row, tap in spans:
        rows = slice(row, row + end - first)
        rest = [spatial_ref[0, 9 * k + tap, first:end, 256:320] for k in range(3)]
        for k in range(3):
            w_ref[rows, k * 256 : (k + 1) * 256] = spatial_ref[0, 9 * k + tap, first:end, 0:256]
        w_ref[rows, 768:896] = pair_lanes(rest[0], rest[1])
        w_ref[rows, 896:1024] = pair_lanes(rest[2], None)
    wn_ref[288:384, :] = jnp.zeros((96, 384), LOW)
    for k in range(3):
        for tap in range(9):
            wn_ref[32 * tap : 32 * tap + 32, tile(k)] = narrow_ref[0, 9 * k + tap]
    for row, ref in ((0, scale_ref), (1, shift_ref)):
        vector = ref[index : index + 1, :]
        rest = vector[:, 384:416]
        squeeze = vector[:, 736:768]
        para_ref[row : row + 1, 0:128] = vector[:, 256:384]
        para_ref[row : row + 1, 128:256] = jnp.concatenate([rest] * 4, axis=1)
        para_ref[row : row + 1, 256:384] = jnp.concatenate([squeeze] * 4, axis=1)
        par_ref[row : row + 1, 0:256] = vector[:, 0:256]
        par_ref[row : row + 1, 256:384] = vector[:, 896:1024]
        par_ref[row : row + 1, 384:768] = jnp.concatenate([vector[:, 416:736], jnp.zeros((1, 64), F32)], axis=1)
        par_ref[row : row + 1, 768:896] = vector[:, 768:896]


def fit_backward(spatial_ref, narrow_ref, wt_ref, wnt_ref):
    wt_ref[480:512, :] = jnp.zeros((32, 2944), LOW)
    for k in range(3):
        for first, end, row in ((0, 128, 128 * k), (128, 160, 384 + 32 * k)):
            rows = slice(row, row + end - first)
            for tap in range(9):
                wt_ref[rows, tap * 256 : (tap + 1) * 256] = spatial_ref[0, 9 * k + tap, first:end, 0:256]
            for g in range(5):
                left = spatial_ref[0, 9 * k + 2 * g, first:end, 256:320]
                right = spatial_ref[0, 9 * k + 2 * g + 1, first:end, 256:320] if g < 4 else None
                wt_ref[rows, tile(18 + g)] = pair_lanes(left, right)
    wnt_ref[96:128, :] = jnp.zeros((32, 1152), LOW)
    for k in range(3):
        for tap in range(9):
            wnt_ref[32 * k : 32 * k + 32, tile(tap)] = narrow_ref[0, 9 * k + tap]


def fetch_block(body, index, held, made, *refs):
    whole, refs = refs[0 : len(refs) - 2 * held - made - 1], refs[len(refs) - 2 * held - made - 1 :]
    split, outs, parts, sems = refs[0:held], refs[held : held + made], refs[held + made : -1], refs[-1]
    copies = [pltpu.make_async_copy(ref.at[pl.ds(index, 1)], part, sems.at[i]) for i, (ref, part) in enumerate(zip(split, parts))]
    for copy in copies:
        copy.start()
    for copy in copies:
        copy.wait()
    body(*whole, *parts, *outs)


def layer_call(body, index, split, whole, outs, name=None, room=4):
    scratch = [pltpu.VMEM((1,) + x.shape[1:], x.dtype) for x in split]
    return pl.pallas_call(
        functools.partial(fetch_block, body, index, len(split), len(outs)),
        out_shape=tuple(outs),
        in_specs=[VMEM] * len(whole) + [pl.BlockSpec(memory_space=pl.ANY)] * len(split),
        out_specs=tuple([VMEM] * len(outs)),
        scratch_shapes=scratch + [pltpu.SemaphoreType.DMA((len(split),))],
        compiler_params=pltpu.CompilerParams(vmem_limit_bytes=scoped(scratch, room)),
        cost_estimate=pl.CostEstimate(flops=1, bytes_accessed=1, transcendentals=0),
        name=name,
    )(*whole, *split)


def exchange(value, sizes, bits):
    total = sizes[0] * sizes[1]

    def swap(mask):
        return lax.ppermute(value, AXES, [(i, i ^ mask) for i in range(total)])

    if len(bits) == 1:
        return value + swap(1 << bits[0])
    one, two = 1 << bits[0], 1 << bits[1]
    return (value + swap(one)) + (swap(two) + swap(one | two))


class Sum:
    def __init__(self, value, sizes):
        self.value, self.sizes, self.at = value, sizes, 0
        total = sizes[0] * sizes[1]
        bits = list(range(total.bit_length() - 1))
        self.stages = [bits[:1]] + [bits[at : at + 2] for at in range(1, len(bits), 2)]
        self.able = not (total & (total - 1))
        if not self.able:
            self.stages = []
            self.value = lax.psum(value, AXES)

    def step(self):
        if self.at < len(self.stages):
            self.value = exchange(self.value, self.sizes, self.stages[self.at])
            self.at += 1
        return self.value

    def result(self):
        while self.at < len(self.stages):
            self.step()
        return self.value


def sum_all(value, sizes):
    return Sum(value, sizes).result()


def meet(*holders):
    names = [[n for n in ("value", "keep", "send", "ready", "array") if getattr(holder, n, None) is not None] for holder in holders]
    values = lax.optimization_barrier([[getattr(h, n) for n in ns] for h, ns in zip(holders, names)])
    for holder, ns, got in zip(holders, names, values):
        for n, value in zip(ns, got):
            setattr(holder, n, value)


class Held:
    def __init__(self, array):
        self.array = array


class Sharing:
    def __init__(self, sizes):
        dp, rep = sizes
        self.sizes = sizes
        self.total = dp * rep
        self.able = not (self.total & (self.total - 1)) and dp >= 8 and rep >= 4
        low = rep.bit_length() - 1
        self.bits = [0, 1, low, low + 1, low + 2]
        self.other = [bit for bit in range(self.total.bit_length() - 1) if bit not in self.bits]

    def me(self):
        if not self.able:
            return jnp.zeros((1,), jnp.int32)
        flat = lax.axis_index("dp") * self.sizes[1] + lax.axis_index("rep")
        index = sum(((flat >> bit) & 1) << i for i, bit in enumerate(self.bits))
        return index.reshape(1).astype(jnp.int32)

    def swap(self, value, even, odd=None):
        masks = [sum(1 << self.bits[i] for i in bits) for bits in (even, even if odd is None else odd)]
        return lax.ppermute(value, AXES, [(i, i ^ masks[i & 1]) for i in range(self.total)])

    def chain(self, keep, send):
        return Chain(self, keep, send)


CORE, FIRST, SECOND, BOTH = ((0,), (0,)), ((1,), (2,)), ((2,), (1,)), ((1, 2), (1, 2))
FAR, NEAR, ENDS = ((4,), (4,)), ((3,), (3,)), ((3, 4), (3, 4))


class Chain:
    def __init__(self, sharing, keep, send, short=False):
        self.sharing, self.keep, self.send, self.short = sharing, keep, send, short
        self.ready = None
        names = ["core", "both" if short else "first", None if short else "second", "depth"]
        self.stages = [n for n in names + ["up_depth"] + ["up_" + n for n in reversed(names[0:3]) if n] if n]
        if not sharing.able:
            self.keep, self.send, self.stages = lax.psum(keep, AXES), lax.psum(send, AXES), []

    def offers(self):
        stage, send, keep = self.stages[0], self.send, self.keep
        if stage in ("core", "up_core"):
            return [(CORE, send)]
        if stage in ("first", "up_first"):
            return [(FIRST, send)]
        if stage in ("second", "up_second"):
            return [(SECOND, send)]
        if stage == "both":
            return [(FIRST, send[0:4]), (SECOND, keep[4:8]), (BOTH, send[4:8])]
        if stage == "up_both":
            return [(SECOND, send), (FIRST, send), (BOTH, send)]
        if stage == "depth":
            return [(FAR, send[0]), (NEAR, send[1]), (ENDS, send[2])]
        return [(FAR, send), (NEAR, send), (ENDS, send)]

    def accept(self, got):
        stage, send, keep = self.stages.pop(0), self.send, self.keep
        if stage in ("core", "first"):
            half = keep.shape[0] // 2
            self.keep, self.send = keep[0:half] + got[0][0:half], keep[half:] + got[0][half:]
        elif stage == "second":
            self.split([keep[i] + got[0][i] for i in range(4)])
        elif stage == "both":
            self.split([(keep[i] + got[0][i]) + (got[1][i] + got[2][i]) for i in range(4)])
        elif stage == "depth":
            whole = (keep + got[0]) + (got[1] + got[2])
            for bit in self.sharing.other:
                whole = exchange(whole, self.sharing.sizes, [bit])
            self.keep, self.send = None, whole
        elif stage == "up_depth":
            self.send = jnp.stack([send, *got])
        elif stage == "up_core":
            self.keep, self.send = send, got[0]
        else:
            self.send = jnp.concatenate([send, *got])

    def rest(self):
        if not self.stages:
            return
        first, second = self.sharing.swap(self.send, *FIRST), self.sharing.swap(self.ready, *SECOND)
        self.split([(self.keep[i] + first[i]) + second[i] for i in range(4)])
        self.ready = None
        self.stages = self.stages[2:]

    def split(self, parts):
        self.keep, self.send = parts[0], parts[1:]

    def half(self):
        if not self.stages:
            return
        if self.ready is None:
            self.ready = self.keep[4:8] + self.sharing.swap(self.send[4:8], *FIRST)
            self.keep, self.send = self.keep[0:4], self.send[0:4]
        else:
            self.keep = self.keep + self.sharing.swap(self.send, *FIRST)
            self.send, self.ready = self.ready, None
            self.stages.pop(0)

    def result(self):
        return [self.keep, self.send]


def advance(*chains):
    chains = [chain for chain in chains if chain.stages]
    offered = [chain.offers() for chain in chains]
    got = [[None] * len(offers) for offers in offered]
    partners = {}
    for i, offers in enumerate(offered):
        for j, (partner, _) in enumerate(offers):
            partners.setdefault((partner, i if partner == CORE else 0), []).append((i, j))
    for (partner, _), places in partners.items():
        values = [offered[i][j][1] for i, j in places]
        flat = [value.reshape(-1, 128) for value in values]
        arrived = chains[0].sharing.swap(flat[0] if len(flat) == 1 else jnp.concatenate(flat), *partner)
        at = 0
        for (i, j), value, rows in zip(places, values, flat):
            got[i][j] = arrived[at : at + rows.shape[0]].reshape(value.shape)
            at += rows.shape[0]
    for chain, received in zip(chains, got):
        chain.accept(received)


def shards(sizes, *arguments):
    clip_input, cotangent, clip_group, crop_sides = arguments[:4]
    kernels, bn_scale, bn_shift = arguments[4:10], arguments[10], arguments[11]
    w_single, w_reduce, w_spatial, w_squeeze, w_narrow, w_project = kernels
    _, frames, side, _, width = clip_input.shape
    lower, upper = Layer(frames, side, False), Layer(frames // 2, side // 2, True)
    where = [clip_group, crop_sides]
    merged = [w_spatial.reshape(2, 27, 160, 320), w_narrow.reshape(2, 27, 32, 128)]
    turned = [jnp.swapaxes(w_reduce, 1, 2), jnp.swapaxes(w_squeeze, 1, 2)]
    points = layer_call(
        fit_points, 1, [w_single, w_project] + turned, [],
        [struct((384, 896), LOW), struct((896, 384), LOW)], name="fit_points",
    )
    fitted = [
        layer_call(
            functools.partial(fit_forward, i),
            i,
            merged,
            [bn_scale, bn_shift],
            [struct((1536, 1024), LOW), struct((384, 384), LOW), struct((2, 384), F32), struct((2, 896), F32)],
            name="fit_forward",
        )
        for i in (0, 1)
    ]
    pars = [item[2:4] for item in fitted]

    def turned_weights(index, kernels):
        return layer_call(
            fit_backward, index, kernels, [], [struct((512, 2944), LOW), struct((128, 1152), LOW)], name="fit_backward"
        )

    def frames_first(value, layer):
        value = jnp.transpose(value, (0, 2, 3, 1, 4)).reshape(layer.side * layer.side, layer.frames, width)
        return jnp.transpose(value, (1, 0, 2))

    def frames_back(value, layer):
        value = jnp.transpose(value, (1, 0, 2)).reshape(1, layer.side, layer.side, layer.frames, width)
        return jnp.transpose(value, (0, 3, 1, 2, 4))

    x = frames_first(clip_input, lower).reshape(lower.rows, width)
    cot = frames_first(cotangent, upper)
    cot = jnp.concatenate(
        [cot[..., 0:576], jnp.zeros(cot.shape[:2] + (64,), LOW), cot[..., 576:832]], axis=2
    )
    cot = jnp.pad(cot, ((0, 0), (0, upper.frame - upper.side * upper.side), (0, 0))).reshape(upper.rows, 896)

    def around(layer, tiles):
        return pltpu.VMEM((tiles, layer.frame + 2 * EDGE, 128), F32)

    def forward(layer, za, suma, sumb, index):
        r = layer.rows
        return call(
            functools.partial(conv_forward, layer),
            where + [za, suma, pars[index][0], sumb, *fitted[index][0:2]],
            [struct((r, 1536), LOW), struct((r, 384), LOW), struct((r, 512), F32), struct((2, 896), F32)],
            [around(layer, 3), pltpu.VMEM((r, 256), F32)],
            name="conv_forward",
        )

    def unit_back(layer, gu, zb, zc, suma, sums, back, index):
        r = layer.rows
        return call(
            functools.partial(unit_backward, layer),
            where + [gu, zb, zc, suma, sums, back, pars[index][1]],
            [struct((r, 384), LOW), struct((r, 1024), LOW), struct((r, 384), LOW)],
            [around(layer, 1), pltpu.VMEM((r, 128), F32)],
            fetch=[2, 3, 4] if layer.halved else [],
            name="unit_backward",
        )

    def conv_back(layer, three, thin3, za, suma, index, turned):
        r = layer.rows
        return call(
            functools.partial(conv_backward, layer),
            where + [three, thin3, za, suma, pars[index][0], *turned],
            [struct((r, 384), F32), struct((2, 384), F32)],
            [
                around(layer, 4),
                pltpu.VMEM((layer.frame, 2944), LOW),
                pltpu.VMEM((layer.frame, 1152), LOW),
                pltpu.VMEM((r, 256), F32),
                pltpu.VMEM((r, 128), F32),
            ],
            late=[7, 8] if layer.halved else [],
            name="conv_backward",
        )

    sharing = Sharing(sizes)
    me = sharing.me()

    def make_weights(index, columns, kinds, *operands, short=False, fetch=False):
        part = PARTS[index]
        scratch = []
        for kind in kinds:
            if kind == "w":
                scratch.append((1440, 128 * sum(count for _, count in columns)))
            elif kind == "o":
                scratch += [(384, 384), (832, 384)]
            else:
                scratch.append((192, 896))
        made = call(
            functools.partial(weights, part, columns, kinds),
            [me, *operands],
            [struct((16, part[0], 128), F32)] * 2,
            [pltpu.VMEM(shape, F32) for shape in scratch],
            scalars=1,
            fetch=range(1, 1 + len(operands)) if fetch else [],
            name="weights",
        )
        return Chain(sharing, *made, short=short)

    def unit_and_first(layer, gu, zb, zc, suma, sums, back, index, wide, dza, upper_source, thin, source):
        r = layer.rows
        parts, columns = PARTS[1:3], ([(0, 2), (2, 2), (6, 1)], [(4, 2), (7, 1)])
        pieces = [struct((16, part[0], 128), F32) for part in parts for _ in (0, 1)]
        grads = [(1440, 640), (192, 896), (1440, 384), (384, 384), (832, 384)]
        *made, keep, send, other_keep, other_send = call(
            functools.partial(unit_and_weights, layer, parts, columns),
            where + [me, gu, zb, zc, suma, sums, back, pars[index][1], wide, dza, upper_source, thin, source],
            [struct((r, 384), LOW), struct((r, 1024), LOW), struct((r, 384), LOW)] + pieces,
            [around(layer, 1), pltpu.VMEM((r, 128), F32)] + [pltpu.VMEM(shape, F32) for shape in grads],
            scalars=3,
            name="unit_and_weights",
        )
        return made, Chain(sharing, keep, send), Chain(sharing, other_keep, other_send)

    r0, r1 = lower.rows, upper.rows
    za, suma, wa = call(
        functools.partial(first_a, lower),
        where + [x, *turned],
        [struct((r0, 384), F32), struct((3, 384), F32), struct((384, 832), LOW)],
        fetch=[3, 4],
        name="first_a",
    )
    small, held = Sum(suma, sizes), Held(list(fitted[0]))
    small.step()
    small.step()
    meet(small, held)
    fitted[0] = held.array
    pars[0] = fitted[0][2:4]
    suma = small.result()
    zb, sumb = call(
        functools.partial(first_b, lower),
        where + [x, w_single, w_project],
        [struct((r0, 384), F32), struct((2, 384), F32)],
        [around(lower, 1)],
        name="first_b",
    )
    wide, thin, zc, sums = forward(lower, za, suma, sumb, 0)
    sums = sum_all(sums, sizes)
    q, za2, zb2, suma2, sumb2 = call(
        functools.partial(finish_lower, lower, upper),
        where + [zb, zc, suma, sums, pars[0][1], *points],
        [struct((r1, 896), LOW), struct((r1, 384), F32), struct((r1, 384), F32), struct((3, 384), F32), struct((2, 384), F32)],
        [around(upper, 1), pltpu.VMEM((lower.frame, 1792), LOW)],
        name="finish_lower",
    )
    suma2 = sum_all(suma2, sizes)
    wide2, thin2, zc2, sums2 = forward(upper, za2, suma2, sumb2, 1)
    sums2 = sum_all(sums2, sizes)
    out, gu2, back2 = call(
        functools.partial(finish_upper, upper),
        where + [zb2, zc2, suma2, sums2, pars[1][1], cot],
        [struct((r1, 896), LOW), struct((r1, 896), F32), struct((2, 896), F32)],
        name="finish_upper",
    )
    small, held = Sum(back2, sizes), Held(list(merged))
    small.step()
    meet(small, held)
    merged = held.array
    held = Held(list(turned_weights(1, merged)))
    small.step()
    meet(small, held)
    turned2 = held.array
    back2 = small.result()
    dzb2, three2, thin32 = unit_back(upper, gu2, zb2, zc2, suma2, sums2, back2, 1)
    gua2, backa2 = conv_back(upper, three2, thin32, za2, suma2, 1, turned2)
    small = Sum(backa2, sizes)
    small.step()
    one = make_weights(0, [(0, 2), (2, 2), (4, 2), (6, 2)], "wo", wide2, three2, thin2, thin32, q, dzb2)
    meet(small, one)
    small.step()
    advance(one)
    meet(small, one)
    backa2 = small.result()
    one.half()
    dza2, gu, back = call(
        functools.partial(join_blocks, upper, lower),
        where + [gua2, za2, suma2, backa2, pars[1][0], dzb2, *points, zb, zc, suma, sums, pars[0][1]],
        [struct((r1, 384), LOW), struct((r0, 896), F32), struct((2, 896), F32)],
        [pltpu.VMEM((lower.frame, 896), F32)],
        name="join_blocks",
    )
    small, held = Sum(back, sizes), Held(list(merged))
    small.step()
    meet(small, held)
    held = Held(list(turned_weights(0, held.array)))
    small.step()
    meet(small, held)
    turned = held.array
    meet(small, one)
    one.rest()
    back = small.result()
    (dzb, three, thin3), two, more = unit_and_first(
        lower, gu, zb, zc, suma, sums, back, 0, wide, dza2, q, thin, x
    )
    held = Held(three)
    meet(one, two, more, held)
    advance(one)
    advance(two)
    meet(two, more)
    advance(two)
    advance(more)
    gua, backa = conv_back(lower, held.array, thin3, za, suma, 0, turned)
    small = Sum(backa, sizes)
    meet(two, more, small)
    more.half()
    small.step()
    small.step()
    meet(one, more, small)
    advance(one)
    more.rest()
    advance(two)
    backa = small.result()
    dza, da = call(
        functools.partial(last_back, lower),
        where + [gua, za, suma, backa, pars[0][0], dzb, wa, w_single, w_project],
        [struct((r0, 384), LOW), struct((r0, 832), LOW)],
        name="last_back",
    )
    held = Held(dza)
    meet(one, two, more, held)
    final = make_weights(3, [], "l", held.array, x, short=True)
    advance(one, two)
    advance(final)
    meet(one, two, more, final)
    advance(one, two, more, final)
    meet(one, two, more, final)
    advance(one, more, final)
    advance(two)
    advance(two)
    meet(one, two, more, final)
    joined = Held(assemble_call(me, [(PARTS[0], one.result())], [(which, 1, 0, 0) for which in (SINGLE, SPATIAL, NARROW, PROJECT)], None))
    advance(two, more, final)
    meet(two, more, final, joined)
    joined.array = assemble_call(
        me, [(PARTS[1], two.result())], [(SPATIAL, 0, 0, 18), (REDUCE, 1, 0, 0), (SQUEEZE, 1, 0, 0)], list(joined.array)
    )
    da = Held(frames_back(da.reshape(lower.frames, lower.frame, width), lower))
    out = jnp.concatenate([out[:, 0:576], out[:, 640:896]], axis=1)
    out = out.reshape(upper.frames, upper.frame, width)[:, 0 : upper.side * upper.side]
    out = Held(frames_back(out, upper))
    advance(more, final)
    meet(more, final, joined, da, out)
    advance(more, final)
    joined = list(joined.array)
    joined = list(assemble_call(
        me,
        [(PARTS[2], more.result()), (PARTS[3], final.result())],
        [(SPATIAL, 0, 18, 9)] + [(which, 0, 0, 0) for which in (SINGLE, REDUCE, SQUEEZE, NARROW, PROJECT)],
        joined,
    ))
    joined[REDUCE], joined[SQUEEZE] = (jnp.swapaxes(joined[which], 1, 2) for which in (REDUCE, SQUEEZE))
    joined = [value.reshape(kernel.shape) for value, kernel in zip(joined, kernels)]
    both = jnp.stack([unfit_vectors(backa, back), unfit_vectors(backa2, back2)])
    return (
        out.array,
        da.array,
        *joined,
        both[:, 1],
        both[:, 0],
    )


def solution(mesh):
    split = P(AXES, None, None, None, None)
    sizes = tuple(mesh.shape[axis] for axis in AXES)
    return jax.shard_map(
        functools.partial(shards, sizes),
        mesh=mesh,
        in_specs=(split, split, P(AXES)) + (P(),) * 9,
        out_specs=(split, split) + (P(),) * 8,
        check_vma=False,
    )
```

```python
import functools

import jax
import jax.numpy as jnp
from jax import lax
from jax.experimental import pallas as pl
from jax.experimental.pallas import tpu as pltpu
from jax.sharding import PartitionSpec as P

AXES = ("dp", "rep")
F32 = jnp.float32
LOW = jnp.bfloat16
EDGE = 32
TAPS = [(dh, dw) for dh in (-1, 0, 1) for dw in (-1, 0, 1)]
UNIT_TILES = [("b", 0), ("b", 1), ("c", 0), ("c", 1), ("c", 2), ("c", 3), ("b", 2)]
VMEM = pl.BlockSpec(memory_space=pltpu.VMEM)
SMEM = pl.BlockSpec(memory_space=pltpu.SMEM)
MIB = 1024 * 1024


def struct(shape, kind):
    return jax.ShapeDtypeStruct(shape, kind)


def scoped(scratch, room):
    total = 0
    for item in scratch:
        if isinstance(item, jax.core.ShapedArray) or hasattr(item, "shape"):
            shape = item.shape
            if len(shape) >= 2:
                size = -(-shape[-1] // 128) * 128 * -(-shape[-2] // 8) * 8 * jnp.dtype(item.dtype).itemsize
                for n in shape[:-2]:
                    size *= n
                total += size
    return total + room * MIB


def with_fetch(body, scalars, fetch, late, many_ins, many_outs, *refs):
    ins, outs = list(refs[0:many_ins]), refs[many_ins : many_ins + many_outs]
    scratch = list(refs[many_ins + many_outs :])
    sems = scratch.pop()
    moved = fetch + late
    parts = scratch[len(scratch) - len(moved) :]
    scratch = scratch[0 : len(scratch) - len(moved)]
    copies = [pltpu.make_async_copy(ins[i], part, sems.at[k]) for k, (i, part) in enumerate(zip(moved, parts))]
    for copy in copies:
        copy.start()
    for copy in copies[0 : len(fetch)]:
        copy.wait()
    for i, part in zip(moved, parts):
        ins[i] = part

    def ready():
        for copy in copies[len(fetch) :]:
            copy.wait()

    body(*ins, *outs, *scratch, **({"ready": ready} if late else {}))


def call(body, ins, outs, scratch=(), scalars=2, room=3, name=None, fetch=(), late=()):
    fetch, late, scratch = list(fetch), list(late), list(scratch)
    specs = [SMEM] * scalars + [VMEM] * (len(ins) - scalars)
    if fetch or late:
        body = functools.partial(with_fetch, body, scalars, fetch, late, len(ins), len(outs))
        for i in fetch + late:
            specs[i] = pl.BlockSpec(memory_space=pl.ANY)
            scratch.append(pltpu.VMEM(ins[i].shape, ins[i].dtype))
    limit = scoped(scratch, room)
    if fetch or late:
        scratch.append(pltpu.SemaphoreType.DMA((len(fetch) + len(late),)))
    return pl.pallas_call(
        body,
        out_shape=tuple(outs),
        in_specs=specs,
        out_specs=tuple([VMEM] * len(outs)),
        scratch_shapes=scratch,
        compiler_params=pltpu.CompilerParams(vmem_limit_bytes=limit),
        cost_estimate=pl.CostEstimate(flops=1, bytes_accessed=1, transcendentals=0),
        name=name,
    )(*ins)


def tile(index, width=1):
    return slice(index * 128, (index + width) * 128)


def lanes():
    return lax.broadcasted_iota(jnp.int32, (1, 128), 1)


def silu(half):
    return half * (jnp.tanh(half) + 1.0)


def double_slope(half):
    bent = jnp.tanh(half)
    return (1.0 + bent) * (1.0 + half * (1.0 - bent))


def places(frame, side):
    at = lax.broadcasted_iota(jnp.int32, (frame, 1), 0).astype(F32)
    row = jnp.floor((at + 0.5) * (1.0 / side))
    return row, at - row * side


def crop_mask(frame, side, crop):
    row, column = places(frame, side)
    return jnp.where((row < crop) & (column < crop), 1.0, 0.0).astype(F32)


def column_mask(frame, side, step):
    row, column = places(frame, side)
    inside = (column + step > -0.5) & (column + step < side - 0.5)
    return jnp.where(inside, 1.0, 0.0).astype(F32)


def crop_of(group_ref, sides_ref, halved):
    crop = sides_ref[group_ref[0]]
    if halved:
        crop = lax.shift_right_logical(crop, 1)
    return crop.astype(F32)


def moments(sums, count):
    mean = sums[0:1] / count
    square = sums[1:2] / count
    return mean, lax.rsqrt(square - mean * mean + 1e-05)


def back_terms(sums, count, gamma, mean, inverse):
    scale = gamma * inverse
    slope = scale * inverse * (sums[1:2] / count)
    return scale, scale * (sums[0:1] / count) - mean * slope, slope


def add_sums(ref, at, first, second):
    ref[0:1, at] += jnp.sum(first, axis=0, keepdims=True)
    ref[1:2, at] += jnp.sum(second, axis=0, keepdims=True)


def neighbour_sum(values, around, frame, side, put):
    frames = len(values)
    left = column_mask(frame, side, -1)
    right = column_mask(frame, side, 1)
    for t in range(frames):
        total = values[t]
        if t > 0:
            total = total + values[t - 1]
        if t < frames - 1:
            total = total + values[t + 1]
        around[0, EDGE : EDGE + frame, :] = total
        total = (
            total
            + around[0, EDGE - side : EDGE - side + frame, :]
            + around[0, EDGE + side : EDGE + side + frame, :]
        )
        around[0, EDGE : EDGE + frame, :] = total
        total = (
            total
            + around[0, EDGE - 1 : EDGE - 1 + frame, :] * left
            + around[0, EDGE + 1 : EDGE + 1 + frame, :] * right
        )
        put(t, total * (1.0 / 27.0))


def clear_edges(around, frame):
    tiles = around.shape[0]
    around[:, 0:EDGE, :] = jnp.zeros((tiles, EDGE, 128), F32)
    around[:, EDGE + frame : 2 * EDGE + frame, :] = jnp.zeros((tiles, EDGE, 128), F32)


def dot(a, b):
    return lax.dot_general(a, b, (((1,), (0,)), ((), ())), preferred_element_type=F32)


def dot_nt(a, b):
    return lax.dot_general(a, b, (((1,), (1,)), ((), ())), preferred_element_type=F32)


def dot_tn(a, b):
    return lax.dot_general(a, b, (((0,), (0,)), ((), ())), preferred_element_type=F32)


class Layer:
    def __init__(self, frames, side, halved):
        self.frames = frames
        self.side = side
        self.halved = halved
        self.frame = -(-side * side // 16) * 16
        self.rows = frames * self.frame

    def at(self, t):
        return slice(t * self.frame, (t + 1) * self.frame)


def point_a(layer, mask, x_ref, w_ref, za_ref, sums_ref):
    sums_ref[...] = jnp.zeros(sums_ref.shape, F32)
    for t in range(layer.frames):
        z = dot_nt(x_ref[layer.at(t), :], w_ref[...])
        za_ref[layer.at(t), :] = z
        for j in range(3):
            part = z[:, tile(j)] * mask
            add_sums(sums_ref, tile(j), part, part * z[:, tile(j)])
    cells = jnp.sum(mask, axis=0, keepdims=True) * layer.frames
    sums_ref[2:3, :] = jnp.broadcast_to(cells, (1, 384))


def point_b(layer, mask, x_ref, kernels, zb_ref, sums_ref, around):
    sums_ref[...] = jnp.zeros(sums_ref.shape, F32)
    clear_edges(around, layer.frame)
    flat = []
    for t in range(layer.frames):
        source = x_ref[layer.at(t), :]
        z = dot(source, kernels[0])
        zb_ref[layer.at(t), 0:256] = z
        zb_ref[layer.at(t), tile(2)] = dot(source, kernels[1]) * mask
        for j in range(2):
            part = z[:, tile(j)] * mask
            add_sums(sums_ref, tile(j), part, part * z[:, tile(j)])
    flat = [zb_ref[layer.at(t), tile(2)] for t in range(layer.frames)]

    def put(t, value):
        zb_ref[layer.at(t), tile(2)] = value
        part = value * mask
        add_sums(sums_ref, tile(2), part, part * value)

    neighbour_sum(flat, around, layer.frame, layer.side, put)


def first_a(layer, group_ref, sides_ref, x_ref, reduce_ref, squeeze_ref, za_ref, sums_ref, wa_ref):
    mask = crop_mask(layer.frame, layer.side, crop_of(group_ref, sides_ref, layer.halved))
    side_by_side(reduce_ref[0], squeeze_ref[0], wa_ref)
    point_a(layer, mask, x_ref, wa_ref, za_ref, sums_ref)


def first_b(layer, group_ref, sides_ref, x_ref, single_ref, project_ref, zb_ref, sums_ref, around):
    mask = crop_mask(layer.frame, layer.side, crop_of(group_ref, sides_ref, layer.halved))
    point_b(layer, mask, x_ref, [single_ref[0], project_ref[0]], zb_ref, sums_ref, around)


def conv_forward(
    layer, group_ref, sides_ref, za_ref, suma_ref, para_ref, sumb_ref, w_ref, wn_ref,
    wide_ref, thin_ref, zc_ref, sums_ref, around, rem,
):
    frames, frame, side = layer.frames, layer.frame, layer.side
    mask = crop_mask(frame, side, crop_of(group_ref, sides_ref, layer.halved))
    count = suma_ref[2:3, :]
    mean, inverse = moments(suma_ref, count)
    gain = 0.5 * para_ref[0:1, :] * inverse
    offset = 0.5 * para_ref[1:2, :] - mean * gain
    column = [column_mask(frame, side, dw) for dw in (-1, 0, 1)]
    part_of = lanes() // 32
    clear_edges(around, frame)
    for t in range(frames):
        rows = layer.at(t)
        for j in range(3):
            half = za_ref[rows, tile(j)] * gain[:, tile(j)] + offset[:, tile(j)]
            around[j, EDGE : EDGE + frame, :] = silu(half) * mask
        mixed = {1: [None] * 3, 2: [None] * 3}
        for k, (dh, dw) in enumerate(TAPS):
            start = EDGE + dh * side + dw
            shifted = around[0, start : start + frame, :]
            if dw:
                shifted = shifted * column[dw + 1]
            wide_ref[rows, tile(k)] = shifted.astype(LOW)
            for j in (1, 2):
                shifted = around[j, start : start + frame, :]
                if dw:
                    shifted = shifted * column[dw + 1]
                shifted = jnp.where(part_of == k % 4, shifted, 0.0)
                held = mixed[j][k // 4]
                mixed[j][k // 4] = shifted if held is None else held + shifted
        for g in range(3):
            wide_ref[rows, tile(9 + g)] = mixed[1][g].astype(LOW)
            thin_ref[rows, tile(g)] = mixed[2][g].astype(LOW)
    sums_ref[:, 0:384] = sumb_ref[...]
    sums_ref[:, 384:896] = jnp.zeros((2, 512), F32)
    zc_ref[...] = jnp.zeros(zc_ref.shape, F32)
    for t in range(frames):
        source = wide_ref[layer.at(t), :]
        thin = thin_ref[layer.at(t), :]
        for k in range(3):
            to = t + 1 - k
            if 0 <= to < frames:
                rows = layer.at(to)
                zc_ref[rows, 0:256] += dot(source, w_ref[:, k * 256 : (k + 1) * 256])
                zc_ref[rows, tile(3)] += dot(thin, wn_ref[:, tile(k)])
        rem[layer.at(t), :] = dot(source, w_ref[:, 768:1024])
    for t in range(frames):
        rows = layer.at(t)
        total = pltpu.roll(rem[rows, 0:128], 64, 1)
        if t > 0:
            total = total + rem[layer.at(t - 1), 0:128]
        if t < frames - 1:
            total = total + rem[layer.at(t + 1), 128:256]
        zc_ref[rows, tile(2)] = jnp.where(lanes() < 64, total, 0.0)
        for j in range(4):
            z = zc_ref[rows, tile(j)]
            part = z * mask
            add_sums(sums_ref, tile(3 + j), part, part * z)


class Norms:
    def __init__(self, sums_ref, par_ref, count):
        mean, inverse = moments(sums_ref, count)
        self.mean, self.inverse = mean, inverse
        self.gamma, self.beta = par_ref[0:1, :], par_ref[1:2, :]

        self.half_gain = 0.5 * self.gamma * inverse
        self.half_offset = 0.5 * self.beta - mean * self.half_gain

    def lane(self, kind, j):
        return tile(j if kind == "b" else 3 + j)

    def half(self, z, at):
        return z * self.half_gain[:, at] + self.half_offset[:, at]

    def normed(self, z, at):
        return (z - self.mean[:, at]) * self.inverse[:, at]


def finish_lower(
    lower, upper, group_ref, sides_ref, zb_ref, zc_ref, suma_ref, sums_ref, par_ref, wa_ref, wb_ref,
    q_ref, za2_ref, zb2_ref, suma2_ref, sumb2_ref, around, y_ref,
):
    crop = crop_of(group_ref, sides_ref, False)
    mask = crop_mask(lower.frame, lower.side, crop)
    norms = Norms(sums_ref, par_ref, suma_ref[2:3, 0:1])
    pick = pair_matrix(upper, lower)
    for t in range(upper.frames):
        for index, (kind, j) in enumerate(UNIT_TILES):
            at = norms.lane(kind, j)
            z_ref = zb_ref if kind == "b" else zc_ref
            total = None
            for source in (2 * t, 2 * t + 1):
                out = silu(norms.half(z_ref[lower.at(source), tile(j)], at)) * mask
                total = out if total is None else total + out
            high = total.astype(LOW)
            y_ref[:, tile(index)] = high
            y_ref[:, tile(7 + index)] = (total - high.astype(F32)).astype(LOW)
        both = dot(pick, y_ref[...])
        q_ref[upper.at(t), :] = (both[:, 0:896] + both[:, 896:1792]).astype(LOW)
    small = crop_mask(upper.frame, upper.side, crop_of(group_ref, sides_ref, True))
    point_a(upper, small, q_ref, wa_ref, za2_ref, suma2_ref)
    point_b(upper, small, q_ref, [wb_ref[:, 0:256], wb_ref[:, 256:384]], zb2_ref, sumb2_ref, around)


def pair_matrix(upper, lower):
    at = lax.broadcasted_iota(jnp.int32, (upper.frame, lower.frame), 1).astype(F32)
    row = jnp.floor((at + 0.5) * (1.0 / lower.side))
    column = at - row * lower.side
    group = jnp.floor(row * 0.5 + 0.25) * upper.side + jnp.floor(column * 0.5 + 0.25)
    mine = lax.broadcasted_iota(jnp.int32, (upper.frame, lower.frame), 0).astype(F32)
    return jnp.where(jnp.abs(group - mine) < 0.5, 0.125, 0.0).astype(LOW)


def spread_matrix(upper, lower):
    at = lax.broadcasted_iota(jnp.int32, (lower.frame, upper.frame), 0).astype(F32)
    row = jnp.floor((at + 0.5) * (1.0 / lower.side))
    column = at - row * lower.side
    group = jnp.floor(row * 0.5 + 0.25) * upper.side + jnp.floor(column * 0.5 + 0.25)
    mine = lax.broadcasted_iota(jnp.int32, (lower.frame, upper.frame), 1).astype(F32)
    return jnp.where(jnp.abs(group - mine) < 0.5, 0.0625, 0.0).astype(LOW)


def finish_upper(
    layer, group_ref, sides_ref, zb_ref, zc_ref, suma_ref, sums_ref, par_ref, cot_ref,
    out_ref, gu_ref, back_ref,
):
    mask = crop_mask(layer.frame, layer.side, crop_of(group_ref, sides_ref, layer.halved))
    half_mask = 0.5 * mask
    norms = Norms(sums_ref, par_ref, suma_ref[2:3, 0:1])
    back_ref[...] = jnp.zeros(back_ref.shape, F32)
    for t in range(layer.frames):
        rows = layer.at(t)
        for index, (kind, j) in enumerate(UNIT_TILES):
            at = norms.lane(kind, j)
            z_ref = zb_ref if kind == "b" else zc_ref
            z = z_ref[rows, tile(j)]
            n, half = norms.normed(z, at), norms.half(z, at)
            out_ref[rows, tile(index)] = (silu(half) * mask).astype(LOW)
            gu = cot_ref[rows, tile(index)].astype(F32) * half_mask * double_slope(half)
            gu_ref[rows, tile(index)] = gu
            add_sums(back_ref, at, gu, gu * n)


def unit_backward(
    layer, group_ref, sides_ref, gu_ref, zb_ref, zc_ref, suma_ref, sums_ref, back_ref, par_ref,
    dzb_ref, three_ref, thin3_ref, around, flat,
):
    frames, frame, side = layer.frames, layer.frame, layer.side
    mask = crop_mask(frame, side, crop_of(group_ref, sides_ref, layer.halved))
    count = suma_ref[2:3, 0:1]
    norms = Norms(sums_ref, par_ref, count)
    c0, c1, c2 = back_terms(back_ref, count, norms.gamma, norms.mean, norms.inverse)
    low_half = lanes() < 64

    def dz_of(t, index):
        kind, j = UNIT_TILES[index]
        at = norms.lane(kind, j)
        z_ref = zb_ref if kind == "b" else zc_ref
        rows = layer.at(t)
        return (gu_ref[rows, tile(index)] * c0[:, at] - z_ref[rows, tile(j)] * c2[:, at] - c1[:, at]) * mask

    clear_edges(around, frame)
    for t in range(frames):
        for index in (0, 1):
            dzb_ref[layer.at(t), tile(index)] = dz_of(t, index).astype(LOW)
        flat[layer.at(t), :] = dz_of(t, 6)

    def put(t, value):
        dzb_ref[layer.at(t), tile(2)] = (value * mask).astype(LOW)

    neighbour_sum([flat[layer.at(t), :] for t in range(frames)], around, frame, side, put)
    for t in range(frames):
        flat[layer.at(t), :] = jnp.where(low_half, dz_of(t, 4), 0.0)
    empty = jnp.zeros((frame, 128), LOW)
    for t in range(frames):
        parts = [dz_of(t, index).astype(LOW) for index in (2, 3, 5)]
        for k in range(3):
            to = t - 1 + k
            if 0 <= to < frames:
                rows = layer.at(to)
                three_ref[rows, tile(2 * k)] = parts[0]
                three_ref[rows, tile(2 * k + 1)] = parts[1]
                thin3_ref[rows, tile(k)] = parts[2]
        rest = pltpu.roll(flat[layer.at(t), :], 64, 1)
        if t < frames - 1:
            rest = rest + flat[layer.at(t + 1), :]
        three_ref[layer.at(t), tile(6)] = rest.astype(LOW)
        three_ref[layer.at(t), tile(7)] = flat[layer.at(t - 1), :].astype(LOW) if t else empty
    for rows, k in ((layer.at(0), 2), (layer.at(frames - 1), 0)):
        three_ref[rows, tile(2 * k)] = empty
        three_ref[rows, tile(2 * k + 1)] = empty
        thin3_ref[rows, tile(k)] = empty


def unit_and_weights(
    layer, parts, columns, group_ref, sides_ref, me_ref, gu_ref, zb_ref, zc_ref, suma_ref, sums_ref, back_ref, par_ref,
    wide_ref, dza_ref, q_ref, thin_ref, x_ref, dzb_ref, three_ref, thin3_ref, keep_ref, send_ref, other_keep_ref,
    other_send_ref, around, flat, wide_grad, last_grad, other_wide_grad, thin_grad, point_grad,
):
    unit_backward(
        layer, group_ref, sides_ref, gu_ref, zb_ref, zc_ref, suma_ref, sums_ref, back_ref, par_ref,
        dzb_ref, three_ref, thin3_ref, around, flat,
    )
    weights(
        parts[0], columns[0], "wl", me_ref, wide_ref, three_ref, dza_ref, q_ref, keep_ref, send_ref, wide_grad, last_grad
    )
    weights(
        parts[1], columns[1], "wo", me_ref, wide_ref, three_ref, thin_ref, thin3_ref, x_ref, dzb_ref, other_keep_ref,
        other_send_ref, other_wide_grad, thin_grad, point_grad,
    )


def conv_backward(
    layer, group_ref, sides_ref, three_ref, thin3_ref, za_ref, suma_ref, para_ref, wt_ref, wnt_ref,
    gua_ref, backa_ref, around, shifts, thins, rem, main, ready=lambda: None,
):
    frames, frame, side = layer.frames, layer.frame, layer.side
    mask = crop_mask(frame, side, crop_of(group_ref, sides_ref, layer.halved))
    column = [column_mask(frame, side, dw) for dw in (-1, 0, 1)]
    low_half = lanes() < 64
    first_part = lanes() < 32
    clear_edges(around, frame)
    main[...] = jnp.zeros(main.shape, F32)
    rem[...] = jnp.zeros(rem.shape, F32)
    for t in range(frames):
        rows = layer.at(t)
        rest = jnp.where(low_half, 0.0, three_ref[rows, tile(6)].astype(F32))
        parts = [
            three_ref[rows, tile(2)].astype(F32),
            three_ref[rows, tile(3)].astype(F32),
            rest + pltpu.roll(rest, 64, 1),
            thin3_ref[rows, tile(1)].astype(F32),
        ]
        for j in range(4):
            around[j, EDGE : EDGE + frame, :] = parts[j]
        mixed = [None] * 5
        for k, (dh, dw) in enumerate(TAPS):
            start = EDGE - dh * side - dw
            for j in range(4):
                shifted = around[j, start : start + frame, :]
                if dw:
                    shifted = shifted * column[1 - dw]
                if j < 2:
                    shifts[:, tile(2 * k + j)] = shifted.astype(LOW)
                elif j == 3:
                    thins[:, tile(k)] = shifted.astype(LOW)
                else:
                    shifted = jnp.where(low_half if k % 2 == 0 else ~low_half, shifted, 0.0)
                    held = mixed[k // 2]
                    mixed[k // 2] = shifted if held is None else held + shifted
        for g in range(5):
            shifts[:, tile(18 + g)] = mixed[g].astype(LOW)
        if t == 0:
            ready()
        product = dot_nt(shifts[...], wt_ref[...])
        thin = dot_nt(thins[...], wnt_ref[...])
        for k in range(3):
            to = t - 1 + k
            if 0 <= to < frames:
                rows = layer.at(to)
                main[rows, :] += product[:, tile(k)]
                turn = (128 - 32 * k) % 128
                last = product[:, tile(3)]
                rem[rows, 0:128] += last if turn == 0 else pltpu.roll(last, turn, 1)
                rem[rows, 128:256] += thin if turn == 0 else pltpu.roll(thin, turn, 1)
    mean, inverse = moments(suma_ref, suma_ref[2:3, :])
    half_mask, half_gamma, half_beta = 0.5 * mask, 0.5 * para_ref[0:1, :], 0.5 * para_ref[1:2, :]
    backa_ref[...] = jnp.zeros(backa_ref.shape, F32)
    for t in range(frames):
        rows = layer.at(t)
        for j in range(3):
            grad = main[rows, :] if j == 0 else rem[rows, tile(j - 1)]
            n = (za_ref[rows, tile(j)] - mean[:, tile(j)]) * inverse[:, tile(j)]
            gu = grad * half_mask * double_slope(half_gamma[:, tile(j)] * n + half_beta[:, tile(j)])
            if j:
                gu = jnp.where(first_part, gu, 0.0)
            gua_ref[rows, tile(j)] = gu
            add_sums(backa_ref, tile(j), gu, gu * n)


def point_back(layer, mask, gua_ref, za_ref, suma_ref, backa_ref, para_ref, dza_ref):
    count = suma_ref[2:3, :]
    mean, inverse = moments(suma_ref, count)
    c0, c1, c2 = back_terms(backa_ref, count, para_ref[0:1, :], mean, inverse)
    for t in range(layer.frames):
        rows = layer.at(t)
        for j in range(3):
            at = tile(j)
            dz = (gua_ref[rows, at] * c0[:, at] - za_ref[rows, at] * c2[:, at] - c1[:, at]) * mask
            if j:
                dz = jnp.where(lanes() < 32, dz, 0.0)
            dza_ref[rows, at] = dz.astype(LOW)


def join_blocks(
    upper, lower, group_ref, sides_ref, gua_ref, za_ref, suma_ref, backa_ref, para_ref, dzb_ref, wa_ref, wb_ref,
    zb_ref, zc_ref, suma1_ref, sums1_ref, par1_ref, dza_ref, gu_ref, back_ref, wide,
):
    small = crop_mask(upper.frame, upper.side, crop_of(group_ref, sides_ref, True))
    point_back(upper, small, gua_ref, za_ref, suma_ref, backa_ref, para_ref, dza_ref)
    mask = crop_mask(lower.frame, lower.side, crop_of(group_ref, sides_ref, False))
    norms = Norms(sums1_ref, par1_ref, suma1_ref[2:3, 0:1])
    back_ref[...] = jnp.zeros(back_ref.shape, F32)
    pick = spread_matrix(upper, lower)
    for t in range(upper.frames):
        rows = upper.at(t)
        dq = dot_nt(dzb_ref[rows, :], wb_ref[...]) + dot(dza_ref[rows, :], wa_ref[...])
        high = dq.astype(LOW)
        rest = (dq - high.astype(F32)).astype(LOW)
        wide[...] = dot(pick, high) + dot(pick, rest)
        for source in (2 * t, 2 * t + 1):
            at_rows = lower.at(source)
            for index, (kind, j) in enumerate(UNIT_TILES):
                at = norms.lane(kind, j)
                z_ref = zb_ref if kind == "b" else zc_ref
                z = z_ref[at_rows, tile(j)]
                n = norms.normed(z, at)
                gu = wide[:, tile(index)] * mask * double_slope(norms.half(z, at))
                gu_ref[at_rows, tile(index)] = gu
                add_sums(back_ref, at, gu, gu * n)


def last_back(
    layer, group_ref, sides_ref, gua_ref, za_ref, suma_ref, backa_ref, para_ref, dzb_ref, wa_ref, single_ref, project_ref, dza_ref, grad_ref,
):
    mask = crop_mask(layer.frame, layer.side, crop_of(group_ref, sides_ref, layer.halved))
    point_back(layer, mask, gua_ref, za_ref, suma_ref, backa_ref, para_ref, dza_ref)
    for t in range(layer.frames):
        rows = layer.at(t)
        total = dot_nt(dzb_ref[rows, 0:256], single_ref[0]) + dot_nt(dzb_ref[rows, 256:384], project_ref[0])
        total = total + dot(dza_ref[rows, :], wa_ref[...])
        grad_ref[rows, :] = (total * mask).astype(LOW)


def place(me, pair, core):
    bits = lax.shift_right_logical(me, 1) ^ pair
    x, y = bits & 1, lax.shift_right_logical(bits, 1) & 1
    near, far = lax.shift_right_logical(bits, 2) & 1, lax.shift_right_logical(bits, 3) & 1
    first = x + core * (y - x)
    second = y + core * (x - y)
    return first * 8 + second * 4 + near * 2 + far


def put_pair(me, keep_ref, send_ref, pair, rows, even, odd):
    core = me & 1
    mine = core == 0
    keep_ref[place(me, pair, core), rows, :] = jnp.where(mine, even, odd)
    send_ref[place(me, pair, 1 - core), rows, :] = jnp.where(mine, odd, even)


def get_pair(me, own_ref, other_ref, pair, rows):
    core = me & 1
    mine = core == 0
    own = own_ref[place(me, pair, core), rows, :]
    other = other_ref[place(me, pair, 1 - core), rows, :]
    return jnp.where(mine, own, other), jnp.where(mine, other, own)


def segments(blocks):
    rows = -(-sum(length for _, length in blocks) // 256) * 8
    pieces, piece, room = [], [], rows
    for name, length in blocks:
        at = 0
        while at < length:
            take = min(room, length - at)
            piece.append((name, at, at + take, rows - room))
            at += take
            room -= take
            if not room:
                pieces.append(piece)
                piece, room = [], rows
    if piece:
        pieces.append(piece)
    return rows, pieces + [[]] * (32 - len(pieces))


def wide(layer, *tiles):
    return [(("wide", j, layer), 720 if j == 7 else 1440) for j in tiles]


def point_and_thin(layer):
    return [(("point", j, layer), 832) for j in range(3)] + [(("thin", j, layer), 288) for j in range(3)]


def last(layer):
    return [(("last", j, layer), 96 if j == 6 else 192) for j in range(7)]


PARTS = [
    segments(wide(1, *range(8)) + point_and_thin(1)),
    segments(wide(0, 0, 1, 2, 3, 6) + last(1)),
    segments(wide(0, 4, 5, 7) + point_and_thin(0)),
    segments(last(0)),
]


def piece_value(piece, rows, read):
    parts = [read(name, first, end) for name, first, end, _ in piece]
    filled = sum(end - first for _, first, end, _ in piece)
    if filled < rows:
        parts.append(jnp.zeros((rows - filled, 128), F32))
    return parts[0] if len(parts) == 1 else jnp.concatenate(parts, axis=0)


def put_pieces(me, keep_ref, send_ref, part, read):
    rows, pieces = part
    for pair in range(16):
        even, odd = (piece_value(pieces[2 * pair + i], rows, read) for i in (0, 1))
        put_pair(me, keep_ref, send_ref, pair, slice(0, rows), even, odd)


def fold(ref, at, rows):
    value = jnp.where(lanes() < 64, ref[0 : 2 * rows, at], 0.0)
    ref[0:rows, at] = value[0:rows] + pltpu.roll(value[rows : 2 * rows], 64, 1)


def without_gap(ref, grad):
    if grad.shape[0] == 896:
        ref[0:576, :] = grad[0:576]
        ref[576:832, :] = grad[640:896]
    else:
        ref[...] = grad


def weights(part, columns, kinds, me_ref, *refs):
    refs = list(refs)
    read_from = {}
    operands = [refs.pop(0) for _ in range({"w": 2, "o": 4, "l": 2}[kinds[0]] + (0 if len(kinds) == 1 else {"o": 4, "l": 2}[kinds[1]]))]
    keep_ref, send_ref = refs.pop(0), refs.pop(0)
    for kind in kinds:
        if kind == "w":
            wide_ref, three_ref = operands.pop(0), operands.pop(0)
            grad = refs.pop(0)
            at = 0
            for first, count in columns:
                grad[:, tile(at, count)] = dot_tn(wide_ref[:, 0:1440], three_ref[:, tile(first, count)])
                for j in range(count):
                    read_from["wide", first + j] = (grad, at + j)
                    if first + j == 7:
                        fold(grad, tile(at + j), 720)
                at += count
        elif kind == "o":
            thin_ref, thin3_ref, x_ref, dzb_ref = (operands.pop(0) for _ in range(4))
            thin_grad, point_grad = refs.pop(0), refs.pop(0)
            thin_grad[...] = dot_tn(thin_ref[...], thin3_ref[...])
            without_gap(point_grad, dot_tn(x_ref[...], dzb_ref[...]))
            for j in range(3):
                read_from["point", j] = (point_grad, j)
                read_from["thin", j] = (thin_grad, j)
        else:
            dza_ref, x_ref = operands.pop(0), operands.pop(0)
            last_grad = refs.pop(0)
            grad = dot_tn(dza_ref[...], x_ref[...])
            if grad.shape[1] == 896:
                grad = close_gap(grad)
            width = grad.shape[1]
            last_grad[0:160, 0:width] = grad[0:160]
            last_grad[160:192, 0:width] = grad[256:288]
            if width < 896:
                last_grad[:, width:896] = jnp.zeros((192, 896 - width), F32)
            fold(last_grad, tile(6), 96)
            for j in range(7):
                read_from["last", j] = (last_grad, j)

    def read(name, first, end):
        ref, j = read_from[name[0:2]]
        return ref[first:end, tile(j)]

    put_pieces(me_ref[0], keep_ref, send_ref, part, read)


OUT_SHAPES = [(832, 256), (160, 832), (27, 160, 320), (32, 832), (27, 32, 128), (832, 128)]
SINGLE, REDUCE, SPATIAL, SQUEEZE, NARROW, PROJECT = range(6)


def assemble(sources, targets, aliased, me_ref, *refs):
    me = me_ref[0]
    many = sum(2 if relative else 1 for _, relative in sources)
    arrived, refs = list(refs[0:many]), refs[many + (6 if aliased else 0) :]
    outs, stages, sems = refs[0:6], refs[6 : 6 + len(targets)], refs[6 + len(targets)]
    stage = {(which, block): (ref, first) for (which, block, first, _), ref in zip(targets, stages)}

    def put_wide(block, k, lanes_at, first, value):
        ref, offset = stage[SPATIAL, block]
        done = 0
        while done < value.shape[0]:
            row = first + done
            if row < 1152:
                tap, channel = row // 128, row % 128
                take = min(128 - channel, value.shape[0] - done)
            else:
                tap, channel = (row - 1152) // 32, 128 + (row - 1152) % 32
                take = min(160 - channel, value.shape[0] - done)
            ref[k * 9 + tap - offset, channel : channel + take, lanes_at] = value[done : done + take]
            done += take

    def put_last(block, lanes_at, first, value):
        for which, low, high in ((REDUCE, 0, 160), (SQUEEZE, 160, 192)):
            begin, stop = max(first, low), min(first + value.shape[0], high)
            if begin < stop:
                stage[which, block][0][begin - low : stop - low, lanes_at] = value[begin - first : stop - first]

    def put(name, first, end, value):
        kind, j, block = name
        if kind == "wide":
            if j < 6:
                put_wide(block, j // 2, tile(j % 2), first, value)
            elif j == 6:
                put_wide(block, 0, slice(256, 320), first, value[:, 0:64])
                put_wide(block, 1, slice(256, 320), first, pltpu.roll(value, 64, 1)[:, 0:64])
            else:
                put_wide(block, 2, slice(256, 320), first, value[:, 0:64])
                put_wide(block, 2, slice(256, 320), first + 720, pltpu.roll(value, 64, 1)[:, 0:64])
        elif kind == "point":
            if j < 2:
                stage[SINGLE, block][0][first:end, tile(j)] = value
            else:
                stage[PROJECT, block][0][first:end, :] = value
        elif kind == "thin":
            done = 0
            while done < end - first:
                tap, channel = (first + done) // 32, (first + done) % 32
                take = min(32 - channel, end - first - done)
                stage[NARROW, block][0][j * 9 + tap, channel : channel + take, :] = value[done : done + take]
                done += take
        elif j < 6:
            put_last(block, tile(j), first, value)
        else:
            put_last(block, slice(768, 832), first, value[:, 0:64])
            put_last(block, slice(768, 832), first + 96, pltpu.roll(value, 64, 1)[:, 0:64])

    for (rows, pieces), relative in sources:
        held = [arrived.pop(0) for _ in range(2 if relative else 1)]
        for pair in range(16):
            if relative:
                both = get_pair(me, *held, pair, slice(0, rows))
            else:
                both = [held[0][2 * pair + i] for i in (0, 1)]
            for i in (0, 1):
                for name, first, end, row in pieces[2 * pair + i]:
                    put(name, first, end, both[i][row : row + end - first])
    copies = []
    for i, ((which, block, first, count), ref) in enumerate(zip(targets, stages)):
        to = outs[which].at[block]
        if count < OUT_SHAPES[which][0]:
            to = to.at[pl.ds(first, count)]
        copies.append(pltpu.make_async_copy(ref, to, sems.at[i]))
        copies[-1].start()
    for copy in copies:
        copy.wait()


def assemble_call(me, sources, targets, outs):
    anywhere = pl.BlockSpec(memory_space=pl.ANY)
    arrays = sum((list(found) for _, found in sources), [])
    targets = [(which, block, first, count or OUT_SHAPES[which][0]) for which, block, first, count in targets]
    scratch = [pltpu.VMEM((count,) + OUT_SHAPES[which][1:], F32) for which, _, _, count in targets]
    return pl.pallas_call(
        functools.partial(assemble, [(part, len(found) == 2) for part, found in sources], targets, outs is not None),
        out_shape=tuple(struct((2,) + shape, F32) for shape in OUT_SHAPES),
        in_specs=[SMEM] + [VMEM] * len(arrays) + [anywhere] * (0 if outs is None else 6),
        out_specs=tuple([anywhere] * 6),
        scratch_shapes=scratch + [pltpu.SemaphoreType.DMA((len(targets),))],
        input_output_aliases={} if outs is None else {1 + len(arrays) + i: i for i in range(6)},
        compiler_params=pltpu.CompilerParams(vmem_limit_bytes=scoped(scratch, 3)),
        cost_estimate=pl.CostEstimate(flops=1, bytes_accessed=1, transcendentals=0),
        name="assemble",
    )(me, *arrays, *([] if outs is None else outs))


def unfit_vectors(sums_a, sums):
    return jnp.concatenate(
        [sums[:, 0:256], sums_a[:, 0:160], sums[:, 384:704], sums_a[:, 256:288], sums[:, 768:896], sums[:, 256:384]], axis=1
    )


def open_gap(value):
    value = value.astype(F32)
    tiles = [value[:, tile(j)] for j in range(6)]
    tiles.append(jnp.concatenate([value[:, 768:832], jnp.zeros((value.shape[0], 64), F32)], axis=1))
    low_half = lanes() < 64
    turned = [pltpu.roll(part, 64, 1) for part in tiles[4:7]]
    tiles[4] = jnp.where(low_half, tiles[4], 0.0)
    tiles[5] = jnp.where(low_half, turned[0], turned[1])
    tiles[6] = jnp.where(low_half, turned[1], turned[2])
    return jnp.concatenate(tiles, axis=1).astype(LOW)


def close_gap(value):
    low_half = lanes() < 64
    tiles = [value[:, tile(j)] for j in range(7)]
    turned = [pltpu.roll(part, 64, 1) for part in tiles[5:7]]
    tiles[4] = jnp.where(low_half, tiles[4], turned[0])
    tiles[5] = jnp.where(low_half, turned[0], turned[1])
    tiles[6] = turned[1]
    return jnp.concatenate(tiles, axis=1)


def side_by_side(reduce, squeeze, wa_ref):
    wa_ref[0:128, :] = reduce[0:128]
    for i in range(4):
        wa_ref[128 + 32 * i : 160 + 32 * i, :] = reduce[128:160]
        wa_ref[256 + 32 * i : 288 + 32 * i, :] = squeeze


def fit_points(single_ref, project_ref, reduce_ref, squeeze_ref, wa_ref, wb_ref):
    gap = wa_ref.shape[1] == 896
    if gap:
        spans = [(slice(0, 576), slice(0, 576)), (slice(640, 896), slice(576, 832))]
        wb_ref[576:640, :] = jnp.zeros((64, 384), LOW)
    else:
        spans = [(slice(0, 832), slice(0, 832))]
    for to, source in spans:
        wb_ref[to, 0:256] = single_ref[0, source, :]
        wb_ref[to, 256:384] = project_ref[0, source, :]
    reduce, squeeze = reduce_ref[0], squeeze_ref[0]
    if gap:
        reduce, squeeze = open_gap(reduce), open_gap(squeeze)
    side_by_side(reduce, squeeze, wa_ref)


def pair_lanes(left, right):
    parts = [jnp.zeros((max(p.shape[0] for p in (left, right) if p is not None), 64), F32) if p is None else p.astype(F32) for p in (left, right)]
    return jnp.concatenate(parts, axis=1).astype(LOW)


def fit_forward(index, scale_ref, shift_ref, spatial_ref, narrow_ref, w_ref, wn_ref, para_ref, par_ref):
    spans = [(0, 128, 128 * tap, tap) for tap in range(9)] + [(128, 160, 1152 + 32 * tap, tap) for tap in range(9)]
    w_ref[1440:1536, :] = jnp.zeros((96, 1024), LOW)
    for first, end, row, tap in spans:
        rows = slice(row, row + end - first)
        rest = [spatial_ref[0, 9 * k + tap, first:end, 256:320] for k in range(3)]
        for k in range(3):
            w_ref[rows, k * 256 : (k + 1) * 256] = spatial_ref[0, 9 * k + tap, first:end, 0:256]
        w_ref[rows, 768:896] = pair_lanes(rest[0], rest[1])
        w_ref[rows, 896:1024] = pair_lanes(rest[2], None)
    wn_ref[288:384, :] = jnp.zeros((96, 384), LOW)
    for k in range(3):
        for tap in range(9):
            wn_ref[32 * tap : 32 * tap + 32, tile(k)] = narrow_ref[0, 9 * k + tap]
    for row, ref in ((0, scale_ref), (1, shift_ref)):
        vector = ref[index : index + 1, :]
        rest = vector[:, 384:416]
        squeeze = vector[:, 736:768]
        para_ref[row : row + 1, 0:128] = vector[:, 256:384]
        para_ref[row : row + 1, 128:256] = jnp.concatenate([rest] * 4, axis=1)
        para_ref[row : row + 1, 256:384] = jnp.concatenate([squeeze] * 4, axis=1)
        par_ref[row : row + 1, 0:256] = vector[:, 0:256]
        par_ref[row : row + 1, 256:384] = vector[:, 896:1024]
        par_ref[row : row + 1, 384:768] = jnp.concatenate([vector[:, 416:736], jnp.zeros((1, 64), F32)], axis=1)
        par_ref[row : row + 1, 768:896] = vector[:, 768:896]


def fit_backward(spatial_ref, narrow_ref, wt_ref, wnt_ref):
    wt_ref[480:512, :] = jnp.zeros((32, 2944), LOW)
    for k in range(3):
        for first, end, row in ((0, 128, 128 * k), (128, 160, 384 + 32 * k)):
            rows = slice(row, row + end - first)
            for tap in range(9):
                wt_ref[rows, tap * 256 : (tap + 1) * 256] = spatial_ref[0, 9 * k + tap, first:end, 0:256]
            for g in range(5):
                left = spatial_ref[0, 9 * k + 2 * g, first:end, 256:320]
                right = spatial_ref[0, 9 * k + 2 * g + 1, first:end, 256:320] if g < 4 else None
                wt_ref[rows, tile(18 + g)] = pair_lanes(left, right)
    wnt_ref[96:128, :] = jnp.zeros((32, 1152), LOW)
    for k in range(3):
        for tap in range(9):
            wnt_ref[32 * k : 32 * k + 32, tile(tap)] = narrow_ref[0, 9 * k + tap]


def fetch_block(body, index, held, made, *refs):
    whole, refs = refs[0 : len(refs) - 2 * held - made - 1], refs[len(refs) - 2 * held - made - 1 :]
    split, outs, parts, sems = refs[0:held], refs[held : held + made], refs[held + made : -1], refs[-1]
    copies = [pltpu.make_async_copy(ref.at[pl.ds(index, 1)], part, sems.at[i]) for i, (ref, part) in enumerate(zip(split, parts))]
    for copy in copies:
        copy.start()
    for copy in copies:
        copy.wait()
    body(*whole, *parts, *outs)


def layer_call(body, index, split, whole, outs, name=None, room=4):
    scratch = [pltpu.VMEM((1,) + x.shape[1:], x.dtype) for x in split]
    return pl.pallas_call(
        functools.partial(fetch_block, body, index, len(split), len(outs)),
        out_shape=tuple(outs),
        in_specs=[VMEM] * len(whole) + [pl.BlockSpec(memory_space=pl.ANY)] * len(split),
        out_specs=tuple([VMEM] * len(outs)),
        scratch_shapes=scratch + [pltpu.SemaphoreType.DMA((len(split),))],
        compiler_params=pltpu.CompilerParams(vmem_limit_bytes=scoped(scratch, room)),
        cost_estimate=pl.CostEstimate(flops=1, bytes_accessed=1, transcendentals=0),
        name=name,
    )(*whole, *split)


def exchange(value, sizes, bits):
    total = sizes[0] * sizes[1]

    def swap(mask):
        return lax.ppermute(value, AXES, [(i, i ^ mask) for i in range(total)])

    if len(bits) == 1:
        return value + swap(1 << bits[0])
    one, two = 1 << bits[0], 1 << bits[1]
    return (value + swap(one)) + (swap(two) + swap(one | two))


class Sum:
    def __init__(self, value, sizes):
        self.value, self.sizes, self.at = value, sizes, 0
        total = sizes[0] * sizes[1]
        bits = list(range(total.bit_length() - 1))
        self.stages = [bits[:1]] + [bits[at : at + 2] for at in range(1, len(bits), 2)]
        self.able = not (total & (total - 1))
        if not self.able:
            self.stages = []
            self.value = lax.psum(value, AXES)

    def step(self):
        if self.at < len(self.stages):
            self.value = exchange(self.value, self.sizes, self.stages[self.at])
            self.at += 1
        return self.value

    def result(self):
        while self.at < len(self.stages):
            self.step()
        return self.value


def sum_all(value, sizes):
    return Sum(value, sizes).result()


def meet(*holders):
    names = [[n for n in ("value", "keep", "send", "ready", "array") if getattr(holder, n, None) is not None] for holder in holders]
    values = lax.optimization_barrier([[getattr(h, n) for n in ns] for h, ns in zip(holders, names)])
    for holder, ns, got in zip(holders, names, values):
        for n, value in zip(ns, got):
            setattr(holder, n, value)


class Held:
    def __init__(self, array):
        self.array = array


class Sharing:
    def __init__(self, sizes):
        dp, rep = sizes
        self.sizes = sizes
        self.total = dp * rep
        self.able = not (self.total & (self.total - 1)) and dp >= 8 and rep >= 4
        low = rep.bit_length() - 1
        self.bits = [0, 1, low, low + 1, low + 2]
        self.other = [bit for bit in range(self.total.bit_length() - 1) if bit not in self.bits]

    def me(self):
        if not self.able:
            return jnp.zeros((1,), jnp.int32)
        flat = lax.axis_index("dp") * self.sizes[1] + lax.axis_index("rep")
        index = sum(((flat >> bit) & 1) << i for i, bit in enumerate(self.bits))
        return index.reshape(1).astype(jnp.int32)

    def swap(self, value, even, odd=None):
        masks = [sum(1 << self.bits[i] for i in bits) for bits in (even, even if odd is None else odd)]
        return lax.ppermute(value, AXES, [(i, i ^ masks[i & 1]) for i in range(self.total)])

    def chain(self, keep, send):
        return Chain(self, keep, send)


CORE, FIRST, SECOND, BOTH = ((0,), (0,)), ((1,), (2,)), ((2,), (1,)), ((1, 2), (1, 2))
FAR, NEAR, ENDS = ((4,), (4,)), ((3,), (3,)), ((3, 4), (3, 4))


class Chain:
    early = False

    def __init__(self, sharing, keep, send, short=False):
        self.sharing, self.keep, self.send, self.short = sharing, keep, send, short
        self.ready = None
        names = ["core", "both" if short else "first", None if short else "second", "depth"]
        self.stages = [n for n in names + ["up_depth"] + ["up_" + n for n in reversed(names[0:3]) if n] if n]
        if not sharing.able:
            self.keep, self.send, self.stages = lax.psum(keep, AXES), lax.psum(send, AXES), []

    def offers(self):
        stage, send, keep = self.stages[0], self.send, self.keep
        if stage == "up_first" and self.early:
            return [(FIRST, send), (CORE, send)]
        if stage in ("core", "up_core"):
            return [(CORE, send)]
        if stage in ("first", "up_first"):
            return [(FIRST, send)]
        if stage in ("second", "up_second"):
            return [(SECOND, send)]
        if stage == "both":
            return [(FIRST, send[0:4]), (SECOND, keep[4:8]), (BOTH, send[4:8])]
        if stage == "up_both":
            return [(SECOND, send), (FIRST, send), (BOTH, send)]
        if stage == "depth":
            return [(FAR, send[0]), (NEAR, send[1]), (ENDS, send[2])]
        return [(FAR, send), (NEAR, send), (ENDS, send)]

    def accept(self, got):
        stage, send, keep = self.stages.pop(0), self.send, self.keep
        if stage in ("core", "first"):
            half = keep.shape[0] // 2
            self.keep, self.send = keep[0:half] + got[0][0:half], keep[half:] + got[0][half:]
        elif stage == "second":
            self.split([keep[i] + got[0][i] for i in range(4)])
        elif stage == "both":
            self.split([(keep[i] + got[0][i]) + (got[1][i] + got[2][i]) for i in range(4)])
        elif stage == "depth":
            whole = (keep + got[0]) + (got[1] + got[2])
            for bit in self.sharing.other:
                whole = exchange(whole, self.sharing.sizes, [bit])
            self.keep, self.send = None, whole
        elif stage == "up_depth":
            self.send = jnp.stack([send, *got])
        elif stage == "up_first" and self.early:
            self.keep, self.send = [send, got[1]], got[0]
        elif stage == "up_core" and self.early:
            self.keep, self.send = jnp.concatenate([keep[0], send]), jnp.concatenate([keep[1], got[0]])
        elif stage == "up_core":
            self.keep, self.send = send, got[0]
        else:
            self.send = jnp.concatenate([send, *got])

    def rest(self):
        if not self.stages:
            return
        first, second = self.sharing.swap(self.send, *FIRST), self.sharing.swap(self.ready, *SECOND)
        self.split([(self.keep[i] + first[i]) + second[i] for i in range(4)])
        self.ready = None
        self.stages = self.stages[2:]

    def split(self, parts):
        self.keep, self.send = parts[0], parts[1:]

    def half(self):
        if not self.stages:
            return
        if self.ready is None:
            self.ready = self.keep[4:8] + self.sharing.swap(self.send[4:8], *FIRST)
            self.keep, self.send = self.keep[0:4], self.send[0:4]
        else:
            self.keep = self.keep + self.sharing.swap(self.send, *FIRST)
            self.send, self.ready = self.ready, None
            self.stages.pop(0)

    def result(self):
        return [self.keep, self.send]


def advance(*chains):
    chains = [chain for chain in chains if chain.stages]
    offered = [chain.offers() for chain in chains]
    got = [[None] * len(offers) for offers in offered]
    partners = {}
    for i, offers in enumerate(offered):
        for j, (partner, _) in enumerate(offers):
            partners.setdefault((partner, i if partner == CORE else 0), []).append((i, j))
    for (partner, _), places in partners.items():
        values = [offered[i][j][1] for i, j in places]
        flat = [value.reshape(-1, 128) for value in values]
        arrived = chains[0].sharing.swap(flat[0] if len(flat) == 1 else jnp.concatenate(flat), *partner)
        at = 0
        for (i, j), value, rows in zip(places, values, flat):
            got[i][j] = arrived[at : at + rows.shape[0]].reshape(value.shape)
            at += rows.shape[0]
    for chain, received in zip(chains, got):
        chain.accept(received)


def shards(sizes, *arguments):
    clip_input, cotangent, clip_group, crop_sides = arguments[:4]
    kernels, bn_scale, bn_shift = arguments[4:10], arguments[10], arguments[11]
    w_single, w_reduce, w_spatial, w_squeeze, w_narrow, w_project = kernels
    _, frames, side, _, width = clip_input.shape
    lower, upper = Layer(frames, side, False), Layer(frames // 2, side // 2, True)
    where = [clip_group, crop_sides]
    merged = [w_spatial.reshape(2, 27, 160, 320), w_narrow.reshape(2, 27, 32, 128)]
    turned = [jnp.swapaxes(w_reduce, 1, 2), jnp.swapaxes(w_squeeze, 1, 2)]
    points = layer_call(
        fit_points, 1, [w_single, w_project] + turned, [],
        [struct((384, 896), LOW), struct((896, 384), LOW)], name="fit_points",
    )
    fitted = [
        layer_call(
            functools.partial(fit_forward, i),
            i,
            merged,
            [bn_scale, bn_shift],
            [struct((1536, 1024), LOW), struct((384, 384), LOW), struct((2, 384), F32), struct((2, 896), F32)],
            name="fit_forward",
        )
        for i in (0, 1)
    ]
    pars = [item[2:4] for item in fitted]

    def turned_weights(index, kernels):
        return layer_call(
            fit_backward, index, kernels, [], [struct((512, 2944), LOW), struct((128, 1152), LOW)], name="fit_backward"
        )

    def frames_first(value, layer):
        value = jnp.transpose(value, (0, 2, 3, 1, 4)).reshape(layer.side * layer.side, layer.frames, width)
        return jnp.transpose(value, (1, 0, 2))

    def frames_back(value, layer):
        value = jnp.transpose(value, (1, 0, 2)).reshape(1, layer.side, layer.side, layer.frames, width)
        return jnp.transpose(value, (0, 3, 1, 2, 4))

    x = frames_first(clip_input, lower).reshape(lower.rows, width)
    cot = frames_first(cotangent, upper)
    cot = jnp.concatenate(
        [cot[..., 0:576], jnp.zeros(cot.shape[:2] + (64,), LOW), cot[..., 576:832]], axis=2
    )
    cot = jnp.pad(cot, ((0, 0), (0, upper.frame - upper.side * upper.side), (0, 0))).reshape(upper.rows, 896)

    def around(layer, tiles):
        return pltpu.VMEM((tiles, layer.frame + 2 * EDGE, 128), F32)

    def forward(layer, za, suma, sumb, index):
        r = layer.rows
        return call(
            functools.partial(conv_forward, layer),
            where + [za, suma, pars[index][0], sumb, *fitted[index][0:2]],
            [struct((r, 1536), LOW), struct((r, 384), LOW), struct((r, 512), F32), struct((2, 896), F32)],
            [around(layer, 3), pltpu.VMEM((r, 256), F32)],
            name="conv_forward",
        )

    def unit_back(layer, gu, zb, zc, suma, sums, back, index):
        r = layer.rows
        return call(
            functools.partial(unit_backward, layer),
            where + [gu, zb, zc, suma, sums, back, pars[index][1]],
            [struct((r, 384), LOW), struct((r, 1024), LOW), struct((r, 384), LOW)],
            [around(layer, 1), pltpu.VMEM((r, 128), F32)],
            fetch=[2, 3, 4] if layer.halved else [],
            name="unit_backward",
        )

    def conv_back(layer, three, thin3, za, suma, index, turned):
        r = layer.rows
        return call(
            functools.partial(conv_backward, layer),
            where + [three, thin3, za, suma, pars[index][0], *turned],
            [struct((r, 384), F32), struct((2, 384), F32)],
            [
                around(layer, 4),
                pltpu.VMEM((layer.frame, 2944), LOW),
                pltpu.VMEM((layer.frame, 1152), LOW),
                pltpu.VMEM((r, 256), F32),
                pltpu.VMEM((r, 128), F32),
            ],
            late=[7, 8] if layer.halved else [],
            name="conv_backward",
        )

    sharing = Sharing(sizes)
    me = sharing.me()

    def make_weights(index, columns, kinds, *operands, short=False, fetch=False):
        part = PARTS[index]
        scratch = []
        for kind in kinds:
            if kind == "w":
                scratch.append((1440, 128 * sum(count for _, count in columns)))
            elif kind == "o":
                scratch += [(384, 384), (832, 384)]
            else:
                scratch.append((192, 896))
        made = call(
            functools.partial(weights, part, columns, kinds),
            [me, *operands],
            [struct((16, part[0], 128), F32)] * 2,
            [pltpu.VMEM(shape, F32) for shape in scratch],
            scalars=1,
            fetch=range(1, 1 + len(operands)) if fetch else [],
            name="weights",
        )
        return Chain(sharing, *made, short=short)

    def unit_and_first(layer, gu, zb, zc, suma, sums, back, index, wide, dza, upper_source, thin, source):
        r = layer.rows
        parts, columns = PARTS[1:3], ([(0, 2), (2, 2), (6, 1)], [(4, 2), (7, 1)])
        pieces = [struct((16, part[0], 128), F32) for part in parts for _ in (0, 1)]
        grads = [(1440, 640), (192, 896), (1440, 384), (384, 384), (832, 384)]
        *made, keep, send, other_keep, other_send = call(
            functools.partial(unit_and_weights, layer, parts, columns),
            where + [me, gu, zb, zc, suma, sums, back, pars[index][1], wide, dza, upper_source, thin, source],
            [struct((r, 384), LOW), struct((r, 1024), LOW), struct((r, 384), LOW)] + pieces,
            [around(layer, 1), pltpu.VMEM((r, 128), F32)] + [pltpu.VMEM(shape, F32) for shape in grads],
            scalars=3,
            name="unit_and_weights",
        )
        return made, Chain(sharing, keep, send), Chain(sharing, other_keep, other_send)

    r0, r1 = lower.rows, upper.rows
    za, suma, wa = call(
        functools.partial(first_a, lower),
        where + [x, *turned],
        [struct((r0, 384), F32), struct((3, 384), F32), struct((384, 832), LOW)],
        fetch=[3, 4],
        name="first_a",
    )
    small, held = Sum(suma, sizes), Held(list(fitted[0]))
    small.step()
    small.step()
    meet(small, held)
    fitted[0] = held.array
    pars[0] = fitted[0][2:4]
    suma = small.result()
    zb, sumb = call(
        functools.partial(first_b, lower),
        where + [x, w_single, w_project],
        [struct((r0, 384), F32), struct((2, 384), F32)],
        [around(lower, 1)],
        name="first_b",
    )
    wide, thin, zc, sums = forward(lower, za, suma, sumb, 0)
    sums = sum_all(sums, sizes)
    q, za2, zb2, suma2, sumb2 = call(
        functools.partial(finish_lower, lower, upper),
        where + [zb, zc, suma, sums, pars[0][1], *points],
        [struct((r1, 896), LOW), struct((r1, 384), F32), struct((r1, 384), F32), struct((3, 384), F32), struct((2, 384), F32)],
        [around(upper, 1), pltpu.VMEM((lower.frame, 1792), LOW)],
        name="finish_lower",
    )
    suma2 = sum_all(suma2, sizes)
    wide2, thin2, zc2, sums2 = forward(upper, za2, suma2, sumb2, 1)
    sums2 = sum_all(sums2, sizes)
    out, gu2, back2 = call(
        functools.partial(finish_upper, upper),
        where + [zb2, zc2, suma2, sums2, pars[1][1], cot],
        [struct((r1, 896), LOW), struct((r1, 896), F32), struct((2, 896), F32)],
        name="finish_upper",
    )
    small, held = Sum(back2, sizes), Held(list(merged))
    small.step()
    meet(small, held)
    merged = held.array
    held = Held(list(turned_weights(1, merged)))
    small.step()
    meet(small, held)
    turned2 = held.array
    back2 = small.result()
    dzb2, three2, thin32 = unit_back(upper, gu2, zb2, zc2, suma2, sums2, back2, 1)
    gua2, backa2 = conv_back(upper, three2, thin32, za2, suma2, 1, turned2)
    small = Sum(backa2, sizes)
    small.step()
    one = make_weights(0, [(0, 2), (2, 2), (4, 2), (6, 2)], "wo", wide2, three2, thin2, thin32, q, dzb2)
    meet(small, one)
    small.step()
    advance(one)
    meet(small, one)
    backa2 = small.result()
    one.half()
    dza2, gu, back = call(
        functools.partial(join_blocks, upper, lower),
        where + [gua2, za2, suma2, backa2, pars[1][0], dzb2, *points, zb, zc, suma, sums, pars[0][1]],
        [struct((r1, 384), LOW), struct((r0, 896), F32), struct((2, 896), F32)],
        [pltpu.VMEM((lower.frame, 896), F32)],
        name="join_blocks",
    )
    small, held = Sum(back, sizes), Held(list(merged))
    small.step()
    meet(small, held)
    held = Held(list(turned_weights(0, held.array)))
    small.step()
    meet(small, held)
    turned = held.array
    meet(small, one)
    one.rest()
    back = small.result()
    (dzb, three, thin3), two, more = unit_and_first(
        lower, gu, zb, zc, suma, sums, back, 0, wide, dza2, q, thin, x
    )
    held = Held(three)
    meet(one, two, more, held)
    advance(one)
    advance(two)
    meet(two, more)
    advance(two)
    advance(more)
    more.early = True
    gua, backa = conv_back(lower, held.array, thin3, za, suma, 0, turned)
    small = Sum(backa, sizes)
    meet(two, more, small)
    more.half()
    small.step()
    small.step()
    meet(one, more, small)
    advance(one)
    more.rest()
    advance(two)
    backa = small.result()
    dza, da = call(
        functools.partial(last_back, lower),
        where + [gua, za, suma, backa, pars[0][0], dzb, wa, w_single, w_project],
        [struct((r0, 384), LOW), struct((r0, 832), LOW)],
        name="last_back",
    )
    held = Held(dza)
    meet(one, two, more, held)
    final = make_weights(3, [], "l", held.array, x, short=True)
    advance(one, two)
    advance(final)
    meet(one, two, more, final)
    advance(one, two, more, final)
    meet(one, two, more, final)
    advance(one, more, final)
    advance(two)
    advance(two)
    meet(one, two, more, final)
    joined = Held(assemble_call(me, [(PARTS[0], one.result())], [(which, 1, 0, 0) for which in (SINGLE, SPATIAL, NARROW, PROJECT)], None))
    advance(two, more, final)
    meet(two, more, final, joined)
    joined.array = assemble_call(
        me, [(PARTS[1], two.result())], [(SPATIAL, 0, 0, 18), (REDUCE, 1, 0, 0), (SQUEEZE, 1, 0, 0)], list(joined.array)
    )
    da = Held(frames_back(da.reshape(lower.frames, lower.frame, width), lower))
    out = jnp.concatenate([out[:, 0:576], out[:, 640:896]], axis=1)
    out = out.reshape(upper.frames, upper.frame, width)[:, 0 : upper.side * upper.side]
    out = Held(frames_back(out, upper))
    advance(more, final)
    meet(more, final, joined, da, out)
    advance(more, final)
    joined = list(joined.array)
    joined = list(assemble_call(
        me,
        [(PARTS[2], more.result()), (PARTS[3], final.result())],
        [(SPATIAL, 0, 18, 9)] + [(which, 0, 0, 0) for which in (SINGLE, REDUCE, SQUEEZE, NARROW, PROJECT)],
        joined,
    ))
    joined[REDUCE], joined[SQUEEZE] = (jnp.swapaxes(joined[which], 1, 2) for which in (REDUCE, SQUEEZE))
    joined = [value.reshape(kernel.shape) for value, kernel in zip(joined, kernels)]
    both = jnp.stack([unfit_vectors(backa, back), unfit_vectors(backa2, back2)])
    return (
        out.array,
        da.array,
        *joined,
        both[:, 1],
        both[:, 0],
    )


def solution(mesh):
    split = P(AXES, None, None, None, None)
    sizes = tuple(mesh.shape[axis] for axis in AXES)
    return jax.shard_map(
        functools.partial(shards, sizes),
        mesh=mesh,
        in_specs=(split, split, P(AXES)) + (P(),) * 9,
        out_specs=(split, split) + (P(),) * 8,
        check_vma=False,
    )
```
